32 devices in a mesh: pts: 8 (over y, x, core), fn: 4 (over z).
Axes of the slice: x: 2, y: 2, z: 4, core: 2. Of those that a mesh axis runs over, the one named last changes fastest.
Arguments:
- query_feats: float32 [32768, 128], P(('pts', 'fn')), may hold values from -6 to 6
- query_coords: float32 [3, 32768], P(None, ('pts', 'fn')), may hold values from 0 to 1
- func_feats: float32 [3, 2048, 128], P(None, 'fn'), may hold values from -6 to 6
- func_counts: int32 [3], replicated, may hold values from 1 to 2048, as said below
- func_present: int32 [3], replicated, may hold values from 0 to 1, as said below
- attn_proj: float32 [2, 2, 3, 128, 128], replicated, may hold values from -1 to 1
- attn_out: float32 [2, 2, 128, 128], replicated, may hold values from -1 to 1
- norm_gain: float32 [2, 5, 128], replicated, may hold values from 0.5 to 1.5
- norm_bias: float32 [2, 5, 128], replicated, may hold values from -3 to 3
- exp_w_in: float32 [2, 2, 4, 128, 256], replicated, may hold values from -0.5 to 0.5
- exp_b_in: float32 [2, 2, 4, 256], replicated, may hold values from -1.5 to 1.5
- exp_w_out: float32 [2, 2, 4, 256, 128], replicated, may hold values from -0.75 to 0.75
- exp_b_out: float32 [2, 2, 4, 128], replicated, may hold values from -1.5 to 1.5
- gate_w_in: float32 [2, 2, 3, 128], replicated, may hold values from -6 to 6
- gate_b_in: float32 [2, 2, 128], replicated, may hold values from -6 to 6
- gate_w_out: float32 [2, 2, 4, 128], replicated, may hold values from -1 to 1
- out_cot: float32 [32768, 128], P(('pts', 'fn')), may hold values from -6 to 6
Outputs:
- query_out: float32 [32768, 128], P(('pts', 'fn'))
- query_grad: float32 [32768, 128], P(('pts', 'fn'))
- func_grad: float32 [3, 2048, 128], P(None, 'fn')
- grad_attn_proj: float32 [2, 2, 3, 128, 128], replicated
- grad_attn_out: float32 [2, 2, 128, 128], replicated
- grad_norm_gain: float32 [2, 5, 128], replicated
- grad_norm_bias: float32 [2, 5, 128], replicated
- grad_exp_w_in: float32 [2, 2, 4, 128, 256], replicated
- grad_exp_b_in: float32 [2, 2, 4, 256], replicated
- grad_exp_w_out: float32 [2, 2, 4, 256, 128], replicated
- grad_exp_b_out: float32 [2, 2, 4, 128], replicated
- grad_gate_w_in: float32 [2, 2, 3, 128], replicated
- grad_gate_b_in: float32 [2, 2, 128], replicated
- grad_gate_w_out: float32 [2, 2, 4, 128], replicated
The draws below stay inside these ranges and needn't reach their ends.
Inputs may be any that keep to these rules, and one draw needn't show every extreme that they name: `func_counts`: one function, drawn from the seed, has exactly 2048 valid points; a function's valid points are its first ones. `func_present`: the function with 2048 valid points is always present.
All inputs are finite; a program needn't handle non-finite values.
Results may differ from the reference program's by a relative error of at most 0.0003.
Values sent between devices are 32-bit elements; how exact they have to be, the bound alone decides.
A program may use at most 192 MiB of HBM per device.

```python
import jax
import jax.numpy as jnp
from jax import lax

D = 128
HEADS = 8
HEAD_SIZE = 16
FH = 256
GH = 128
EXPERTS = 4
NF = 3
LAYERS = 2
QTOK = 32768
MF = 2048


def full_function(key):
    return jax.random.randint(key, (), 0, NF)


def draw_func_counts(key, part):
    chosen = full_function(key)
    key = jax.random.fold_in(key, 5)
    counts = jax.random.randint(key, (NF,), 1, MF + 1)
    return jnp.where(jnp.arange(NF) == chosen, MF, counts).astype(jnp.int32)


def draw_func_present(key, part):
    chosen = full_function(key)
    key = jax.random.fold_in(key, 7)
    flags = jax.random.randint(key, (NF,), 0, 2)
    return jnp.where(jnp.arange(NF) == chosen, 1, flags).astype(jnp.int32)


def level_of(stream_key, shape, split, low, largest):
    factor_of, own = 1.0, jax.random.fold_in(stream_key, 6)
    for dim, parts in split:
        steps = jnp.exp(jax.random.uniform(jax.random.fold_in(own, dim), (parts,), jnp.float32, low / len(split), largest / len(split)))
        factor_of = factor_of * jnp.repeat(steps, shape[dim] // parts).reshape([-1 if axis == dim else 1 for axis in range(len(shape))])
    return factor_of


def noise(rng, extent, spread, reach, cuts=(), held_as=jnp.bfloat16):
    drawn = jax.random.normal(rng, extent, jnp.float32) * spread
    if len(cuts) > 0:
        drawn = level_of(rng, extent, cuts, -0.22, 0.18) * drawn
    return jnp.clip(drawn, min=-reach, max=reach).astype(held_as)


def setup_inputs(seed: int = 0) -> dict:
    keys = jax.random.split(jax.random.key(seed), 18)
    query_feats = noise(keys[0], (QTOK, D), 1.0, 6.0, ((0, 32),), jnp.float32)
    query_coords = jnp.clip(1.0 * jax.random.uniform(keys[1], (3, QTOK), jnp.float32) ** level_of(keys[1], (3, QTOK), ((1, 32),), -0.2, 0.2), 0.0, 1.0)
    func_feats = noise(keys[2], (NF, MF, D), 1.0, 6.0, ((1, 4),), jnp.float32)
    func_counts = draw_func_counts(jax.random.fold_in(keys[17], 71), 0)
    func_present = draw_func_present(jax.random.fold_in(keys[17], 71), 0)
    attn_proj = noise(keys[5], (LAYERS, 2, 3, D, D), (D // 4) ** -0.5, 1.0, (), jnp.float32)
    attn_out = noise(keys[6], (LAYERS, 2, D, D), (D // 4) ** -0.5, 1.0, (), jnp.float32)
    norm_gain = jnp.clip(1.0 + 0.1 * jax.random.normal(keys[7], (LAYERS, 5, D), jnp.float32), 0.5, 1.5)
    norm_bias = noise(keys[8], (LAYERS, 5, D), 0.2, 3.0, (), jnp.float32)
    exp_w_in = noise(keys[9], (LAYERS, 2, EXPERTS, D, FH), D ** -0.5, 0.5, (), jnp.float32)
    exp_b_in = noise(keys[10], (LAYERS, 2, EXPERTS, FH), 0.1, 1.5, (), jnp.float32)
    exp_w_out = noise(keys[11], (LAYERS, 2, EXPERTS, FH, D), (FH // 4) ** -0.5, 0.75, (), jnp.float32)
    exp_b_out = noise(keys[12], (LAYERS, 2, EXPERTS, D), 0.1, 1.5, (), jnp.float32)
    gate_w_in = noise(keys[13], (LAYERS, 2, 3, GH), 1 ** -0.5, 6.0, (), jnp.float32)
    gate_b_in = noise(keys[14], (LAYERS, 2, GH), 0.5, 6.0, (), jnp.float32)
    gate_w_out = noise(keys[15], (LAYERS, 2, EXPERTS, GH), (GH // 4) ** -0.5, 1.0, (), jnp.float32)
    out_cot = noise(keys[16], (QTOK, D), 1.0, 6.0, ((0, 32),), jnp.float32)
    return dict(query_feats=query_feats, query_coords=query_coords, func_feats=func_feats, func_counts=func_counts, func_present=func_present, attn_proj=attn_proj, attn_out=attn_out, norm_gain=norm_gain, norm_bias=norm_bias, exp_w_in=exp_w_in, exp_b_in=exp_b_in, exp_w_out=exp_w_out, exp_b_out=exp_b_out, gate_w_in=gate_w_in, gate_b_in=gate_b_in, gate_w_out=gate_w_out, out_cot=out_cot)


precise = lax.Precision.HIGHEST

@jax.custom_vjp
def low(v):
    return lax.optimization_barrier(v.astype(jnp.bfloat16)).astype(jnp.float32)

@jax.custom_vjp
def low_back(v):
    return v

def low_keep(v):
    return (low(v), None)

def low_pass(kept, grad):
    return (grad,)

def back_keep(v):
    return (v, None)

def back_low(kept, grad):
    return (low(grad),)
low.defvjp(low_keep, low_pass)
low_back.defvjp(back_keep, back_low)

def layer_norm(stream, gain_vec, bias_vec):
    average = lax.optimization_barrier(jnp.mean(stream, axis=-1, keepdims=True))
    centred = stream - average
    variance = lax.optimization_barrier(jnp.mean(centred * centred, axis=-1, keepdims=True))
    return centred * lax.rsqrt(variance + 1e-05) * gain_vec + bias_vec

def head_softmax(values):
    shaped = values.reshape(values.shape[:-1] + (HEADS, HEAD_SIZE))
    return jax.nn.softmax(shaped, axis=-1)

def function_summary(func_rows, row_mask, key_weight, value_weight, gain_vec, bias_vec):
    normed = layer_norm(func_rows, gain_vec, bias_vec)
    key_soft = head_softmax(jnp.einsum('frd,de->fre', normed, key_weight, precision=precise))
    values = jnp.einsum('frd,de->fre', normed, value_weight, precision=precise).reshape(key_soft.shape)
    weighted = key_soft * row_mask[:, :, None, None]
    summary = jnp.einsum('frha,frhb->fhab', weighted, values, precision=precise)
    return (summary, lax.optimization_barrier(jnp.sum(weighted, axis=1)))

def cross_block(stream, query_weight, out_weight, gain_vec, bias_vec, summary, totals, func_share):
    normed = layer_norm(stream, gain_vec, bias_vec)
    queries = head_softmax(jnp.dot(normed, query_weight, precision=precise))
    numerator = jnp.einsum('rha,fhab->frhb', queries, summary, precision=precise)
    denominator = jnp.einsum('rha,fha->frh', queries, totals, precision=precise)
    blended = jnp.einsum('frhb,f->rhb', numerator / denominator[..., None], func_share, precision=precise)
    return stream + jnp.dot(blended.reshape(stream.shape), out_weight, precision=precise)

def expert_block(stream, coords, gain_vec, bias_vec, w_in, b_in, w_out, b_out, gate_in, gate_bias, gate_out):
    normed = layer_norm(stream, gain_vec, bias_vec)
    gate_hidden = jax.nn.gelu(jnp.dot(gate_in.T, coords, precision=precise) + gate_bias[:, None])
    gate_share = jax.nn.softmax(jnp.dot(gate_out, gate_hidden, precision=precise), axis=0)
    hidden = jax.nn.gelu(jnp.einsum('rd,edh->erh', normed, w_in, precision=precise) + b_in[:, None, :])
    outputs = jnp.einsum('erh,ehd->erd', hidden, w_out, precision=precise) + b_out[:, None, :]
    return stream + jnp.einsum('er,erd->rd', gate_share, outputs, precision=precise)

def self_summary(normed, key_weight, value_weight):
    key_soft = head_softmax(jnp.dot(normed, key_weight, precision=precise))
    values = jnp.dot(normed, value_weight, precision=precise).reshape(key_soft.shape)
    return (jnp.einsum('rha,rhb->hab', key_soft, values, precision=precise), lax.optimization_barrier(jnp.sum(key_soft, axis=0)))

def self_output(stream, normed, query_weight, out_weight, summary, totals):
    queries = head_softmax(jnp.dot(normed, query_weight, precision=precise))
    numerator = jnp.einsum('rha,hab->rhb', queries, summary, precision=precise)
    denominator = jnp.einsum('rha,ha->rh', queries, totals, precision=precise)
    attended = (numerator / denominator[..., None]).reshape(stream.shape)
    return stream + jnp.dot(attended, out_weight, precision=precise)

def forward(query_feats, func_feats, attn_proj, attn_out, norm_gain, norm_bias, exp_w_in, exp_b_in, exp_w_out, exp_b_out, gate_w_in, gate_b_in, gate_w_out, query_coords, row_mask, func_share):
    stream = query_feats
    run_experts = jax.checkpoint(expert_block)
    for layer_index in range(LAYERS):
        summary, totals = function_summary(func_feats, row_mask, attn_proj[layer_index, 0, 1], attn_proj[layer_index, 0, 2], norm_gain[layer_index, 1], norm_bias[layer_index, 1])
        stream = cross_block(stream, attn_proj[layer_index, 0, 0], attn_out[layer_index, 0], norm_gain[layer_index, 0], norm_bias[layer_index, 0], summary, totals, func_share)
        for expert_set in (0, 1):
            if expert_set == 1:
                normed = layer_norm(stream, norm_gain[layer_index, 3], norm_bias[layer_index, 3])
                summary, totals = self_summary(normed, attn_proj[layer_index, 1, 1], attn_proj[layer_index, 1, 2])
                stream = self_output(stream, normed, attn_proj[layer_index, 1, 0], attn_out[layer_index, 1], summary, totals)
            slot = 2 + 2 * expert_set
            stream = run_experts(stream, query_coords, norm_gain[layer_index, slot], norm_bias[layer_index, slot], exp_w_in[layer_index, expert_set], exp_b_in[layer_index, expert_set], exp_w_out[layer_index, expert_set], exp_b_out[layer_index, expert_set], gate_w_in[layer_index, expert_set], gate_b_in[layer_index, expert_set], gate_w_out[layer_index, expert_set])
    return stream

def reference(query_feats, query_coords, func_feats, func_counts, func_present, attn_proj, attn_out, norm_gain, norm_bias, exp_w_in, exp_b_in, exp_w_out, exp_b_out, gate_w_in, gate_b_in, gate_w_out, out_cot):
    positions = jnp.arange(MF, dtype=jnp.int32)
    row_mask = (positions[None, :] < func_counts[:, None]).astype(jnp.float32)
    present = func_present.astype(jnp.float32)
    func_share = present / jnp.sum(present)

    def wrapped(query_in, func_in, proj_in, out_in, gain_in, bias_in, w_first, b_first, w_second, b_second, gate_first, gate_bias, gate_second):
        return forward(query_in, func_in, proj_in, out_in, gain_in, bias_in, w_first, b_first, w_second, b_second, gate_first, gate_bias, gate_second, query_coords, row_mask, func_share)
    result, pullback = jax.vjp(wrapped, query_feats, func_feats, attn_proj, attn_out, norm_gain, norm_bias, exp_w_in, exp_b_in, exp_w_out, exp_b_out, gate_w_in, gate_b_in, gate_w_out)
    grads = pullback(out_cot)
    return (result, grads[0], grads[1], grads[2], grads[3], grads[4], grads[5], grads[6], grads[7], grads[8], grads[9], grads[10], grads[11], grads[12])
```

```python
import math
from types import SimpleNamespace

import jax
import jax.numpy as jnp
from jax import lax
from jax.experimental import pallas as pl
from jax.experimental.pallas import tpu as pltpu
from jax.sharding import PartitionSpec as P

D = 128
HEADS = 8
HEAD_SIZE = 16
FH = 256
EXPERTS = 4
HID = EXPERTS * FH
NF = 3
LAYERS = 2
GROUP = 8

f32, bf16 = jnp.float32, jnp.bfloat16
CHUNK = 128
MESH = pl.DeviceIdType.MESH


def split(v):
    hi = v.astype(bf16)
    return hi, (v - hi.astype(f32)).astype(bf16)


def join(hi, lo):
    return hi.astype(f32) + lo.astype(f32)


def dot(a, b, ca, cb):
    return lax.dot_general(a, b, (((ca,), (cb,)), ((), ())), preferred_element_type=f32)


def nn(a, b):
    return dot(a, b, 1, 0)


def tn(a, b):
    return dot(a, b, 0, 0)


def nt(a, b):
    return dot(a, b, 1, 1)


def k3(hi, lo):
    return jnp.concatenate([hi, hi, lo], axis=0)


def nn_rows(w_ref, at, hi, lo):
    both = nn(w_ref[at + (slice(0, 256),)], hi)
    return both[:128] + both[128:] + nn(w_ref[at + (slice(0, 128),)], lo)


def nt_pair(a_hi, a_lo, b_both, b_hi):
    wide = nt(a_hi, b_both)
    n = b_hi.shape[0]
    return wide[:, :n] + wide[:, n:] + nt(a_lo, b_hi)


def normalise(v):
    average = jnp.mean(v, axis=0, keepdims=True)
    centred = v - average
    variance = jnp.mean(centred * centred, axis=0, keepdims=True)
    scale = lax.rsqrt(variance + 1e-05)
    return centred * scale, scale


def norm_back(d_normed, gain_col, unit, scale):
    d_unit = d_normed * gain_col
    first = jnp.mean(d_unit, axis=0, keepdims=True)
    second = jnp.mean(d_unit * unit, axis=0, keepdims=True)
    return scale * (d_unit - first - unit * second)


def by_head(v):
    return v.reshape(HEADS, HEAD_SIZE, v.shape[1])


def head_softmax(v):
    shaped = by_head(v)
    top = jnp.max(shaped, axis=1, keepdims=True)
    power = jnp.exp(shaped - top)
    total = jnp.sum(power, axis=1, keepdims=True)
    return (power * (1.0 / total)).reshape(v.shape)


def head_softmax_back(soft, d_soft):
    total = jnp.sum(by_head(soft * d_soft), axis=1, keepdims=True)
    return (by_head(soft) * (by_head(d_soft) - total)).reshape(soft.shape)


def head_rows(v):
    total = jnp.sum(by_head(v), axis=1, keepdims=True)
    return jnp.concatenate([total[h] for h in range(HEADS)], axis=0)


def head_spread(rows):
    return jnp.concatenate(
        [jnp.broadcast_to(rows[h : h + 1], (HEAD_SIZE, rows.shape[1])) for h in range(HEADS)], axis=0
    )


C1 = 0.7978845608028654
C2 = C1 * 0.044715


def gelu_both(v):
    square = v * v
    gate = 0.5 + 0.5 * jnp.tanh(v * (C1 + C2 * square))
    value = v * gate
    slope = gate + value * (1.0 - gate) * (2.0 * C1 + 6.0 * C2 * square)
    return value, slope


def fold_lanes(v):
    total = v[:, :128]
    for start in range(128, v.shape[1], 128):
        total = total + v[:, start : start + 128]
    return total


def row_sum(folded):
    return jnp.sum(folded.T, axis=0, keepdims=True)


def head_masks():
    rows = lax.broadcasted_iota(jnp.int32, (D, D), 0) // HEAD_SIZE
    cols = lax.broadcasted_iota(jnp.int32, (D, D), 1) // HEAD_SIZE
    square = jnp.where(rows == cols, 1.0, 0.0).astype(f32)
    heads = lax.broadcasted_iota(jnp.int32, (HEADS, D), 0)
    cols8 = lax.broadcasted_iota(jnp.int32, (HEADS, D), 1) // HEAD_SIZE
    return square, jnp.where(heads == cols8, 1.0, 0.0).astype(f32)


def pack_summary(square_part, total_row, square):
    compact = jnp.sum((square_part * square).reshape(HEADS, HEAD_SIZE, D), axis=0)
    return jnp.concatenate([compact, total_row, jnp.zeros((7, D), f32)], axis=0)


def unpack_summary(block, square):
    spread = jnp.concatenate([block[:HEAD_SIZE]] * HEADS, axis=0) * square
    return spread, block[HEAD_SIZE : HEAD_SIZE + 1]


class Exchange:
    def __init__(self, stages, slots, sends, receives):
        self.stages, self.slots, self.sends, self.receives = stages, slots, sends, receives

    @staticmethod
    def place(stage):
        axis, stride, size = stage
        index = lax.axis_index(axis)
        digit = lax.rem(lax.div(index, stride), size)
        return axis, index - digit * stride, digit

    @staticmethod
    def member(stage, offset):
        axis, stride, size = stage
        axis, base, digit = Exchange.place(stage)
        other = lax.rem(digit + offset, size)
        return other, {axis: base + other * stride}

    def copy(self, n, offset, arriving=False):
        stage = self.stages[n]
        _, _, digit = self.place(stage)
        other, device = self.member(stage, offset)
        place = other if arriving else digit
        return pltpu.make_async_remote_copy(
            src_ref=self.slots[n].at[place],
            dst_ref=self.slots[n].at[place],
            send_sem=self.sends[n].at[offset],
            recv_sem=self.receives[n].at[place],
            device_id=device,
            device_id_type=MESH,
        )

    def start(self, n, value):
        _, _, digit = self.place(self.stages[n])
        self.slots[n][digit] = value
        for offset in range(1, self.stages[n][2]):
            self.copy(n, offset).start()

    def finish(self, n):
        size = self.stages[n][2]
        for offset in range(1, size):
            self.copy(n, offset, True).wait_recv()
        total = self.slots[n][0]
        for place in range(1, size):
            total = total + self.slots[n][place]
        for offset in range(1, size):
            self.copy(n, offset).wait_send()
        return total

    def finish_all(self, n=0):
        while True:
            total = self.finish(n)
            n += 1
            if n == len(self.stages):
                return total
            self.start(n, total)


class Reduction:
    def __init__(self, buffers, total, rows, first, n_pts, n_fn):
        self.r = SimpleNamespace(**buffers)
        self.total, self.first = total, first
        self.plane, self.n_fn = n_pts // 2, n_fn
        self.half = rows // 2
        self.part = self.half // self.plane
        self.deep = self.part % (8 * n_fn) == 0
        self.last = self.part // n_fn if self.deep else self.part
        index, self.z = lax.axis_index("pts"), lax.axis_index("fn")
        self.core, self.q = lax.rem(index, 2), lax.div(index, 2)
        self.steps = [self.add_pair, self.add_plane, self.add_fn, self.spread_plane, self.spread_pair, self.end]
        pair, plane, fn = 1.5 + rows / 700, 3.5 + rows / 160, 4.5 + rows / 320
        self.waits = [pair, plane, fn, fn if self.deep else 0.5, plane + 0.5, pair + 0.5]

    @staticmethod
    def scratch(rows, n_pts, n_fn):
        plane = n_pts // 2
        part = max(rows // (2 * plane), 1)
        last = part // n_fn if part % (8 * n_fn) == 0 else part
        dma = pltpu.SemaphoreType.DMA
        return dict(
            stage=pltpu.VMEM((rows, 256), f32),
            pair=pltpu.VMEM((rows // 2, 256), f32),
            planes=pltpu.VMEM((plane, part, 256), f32),
            fns=pltpu.VMEM((n_fn, last, 256), f32),
            pair_sems=dma((2,)),
            plane_sends=dma((plane,)),
            plane_receives=dma((plane,)),
            fn_sends=dma((n_fn,)),
            fn_receives=dma((n_fn,)),
            out_pair_sems=dma((2,)),
            out_plane_sends=dma((plane,)),
            out_plane_receives=dma((plane,)),
            out_fn_sends=dma((n_fn,)),
            out_fn_receives=dma((n_fn,)),
            local_sem=dma((1,)),
        )

    @staticmethod
    def remote(src, dst, send, receive, device):
        return pltpu.make_async_remote_copy(
            src_ref=src, dst_ref=dst, send_sem=send, recv_sem=receive, device_id=device, device_id_type=MESH
        )

    def rows(self, start, count):
        return pl.ds(pl.multiple_of(start, 8), count)

    def own_part(self):
        return self.core * self.half + self.q * self.part

    def own_last(self):
        return self.own_part() + (self.z * self.last if self.deep else 0)

    def in_total(self, start, count):
        return self.total.at[self.rows(self.first + start, count)]

    def pair_copy(self):
        away = self.r.stage.at[self.rows((1 - self.core) * self.half, self.half)]
        sems = self.r.pair_sems
        device = {"pts": 2 * self.q + 1 - self.core}
        return self.remote(away, self.r.pair.at[pl.ds(0, self.half)], sems.at[0], sems.at[1], device)

    def plane_copy(self, offset, arriving=False):
        other = lax.rem(self.q + offset, self.plane)
        src = self.r.stage.at[self.rows(self.core * self.half + other * self.part, self.part)]
        slot = other if arriving else self.q
        return self.remote(
            src,
            self.r.planes.at[slot, pl.ds(0, self.part)],
            self.r.plane_sends.at[offset],
            self.r.plane_receives.at[slot],
            {"pts": 2 * other + self.core},
        )

    def fn_copy(self, offset, arriving=False):
        other = lax.rem(self.z + offset, self.n_fn)
        start = self.own_part() + (other * self.last if self.deep else 0)
        slot = other if arriving else self.z
        return self.remote(
            self.r.stage.at[self.rows(start, self.last)],
            self.r.fns.at[slot, pl.ds(0, self.last)],
            self.r.fn_sends.at[offset],
            self.r.fn_receives.at[slot],
            {"fn": other},
        )

    def local_copy(self):
        src = self.r.stage.at[self.rows(self.own_last(), self.last)]
        return pltpu.make_async_copy(src, self.in_total(self.own_last(), self.last), self.r.local_sem.at[0])

    def out_fn_copy(self, offset, arriving=False):
        other = lax.rem(self.z + offset, self.n_fn)
        place = other if arriving else self.z
        src = self.r.stage.at[self.rows(self.own_last(), self.last)]
        return self.remote(
            src,
            self.in_total(self.own_part() + place * self.last, self.last),
            self.r.out_fn_sends.at[offset],
            self.r.out_fn_receives.at[place],
            {"fn": other},
        )

    def out_plane_copy(self, offset, arriving=False):
        other = lax.rem(self.q + offset, self.plane)
        place = other if arriving else self.q
        region = self.in_total(self.core * self.half + place * self.part, self.part)
        return self.remote(
            region,
            region,
            self.r.out_plane_sends.at[offset],
            self.r.out_plane_receives.at[place],
            {"pts": 2 * other + self.core},
        )

    def out_pair_copy(self, arriving=False):
        place = 1 - self.core if arriving else self.core
        region = self.in_total(place * self.half, self.half)
        sems = self.r.out_pair_sems
        return self.remote(region, region, sems.at[0], sems.at[1], {"pts": 2 * self.q + 1 - self.core})

    def begin(self):
        self.pair_copy().start()

    def step(self):
        self.steps.pop(0)()

    def add_pair(self):
        self.pair_copy().wait()
        mine = self.rows(self.core * self.half, self.half)
        self.r.stage[mine, :] += self.r.pair[0 : self.half, :]
        for offset in range(1, self.plane):
            self.plane_copy(offset).start()

    def add_plane(self):
        mine = self.rows(self.own_part(), self.part)
        sums = self.r.stage[mine, :]
        for offset in range(1, self.plane):
            self.plane_copy(offset, True).wait_recv()
            sums = sums + self.r.planes[lax.rem(self.q + offset, self.plane), 0 : self.part, :]
        self.r.stage[mine, :] = sums
        for offset in range(1, self.plane):
            self.plane_copy(offset).wait_send()
        for offset in range(1, self.n_fn):
            self.fn_copy(offset).start()

    def add_fn(self):
        mine = self.rows(self.own_last(), self.last)
        self.r.fns[self.z, 0 : self.last, :] = self.r.stage[mine, :]
        for offset in range(1, self.n_fn):
            self.fn_copy(offset, True).wait_recv()
        for offset in range(1, self.n_fn):
            self.fn_copy(offset).wait_send()
        sums = self.r.fns[0, 0 : self.last, :]
        for place in range(1, self.n_fn):
            sums = sums + self.r.fns[place, 0 : self.last, :]
        self.r.stage[mine, :] = sums
        self.local_copy().start()
        if self.deep:
            for offset in range(1, self.n_fn):
                self.out_fn_copy(offset).start()

    def spread_plane(self):
        self.local_copy().wait()
        if self.deep:
            for offset in range(1, self.n_fn):
                self.out_fn_copy(offset, True).wait_recv()
            for offset in range(1, self.n_fn):
                self.out_fn_copy(offset).wait_send()
        for offset in range(1, self.plane):
            self.out_plane_copy(offset).start()

    def spread_pair(self):
        for offset in range(1, self.plane):
            self.out_plane_copy(offset, True).wait_recv()
        for offset in range(1, self.plane):
            self.out_plane_copy(offset).wait_send()
        self.out_pair_copy().start()

    def end(self):
        self.out_pair_copy().wait_send()
        self.out_pair_copy(True).wait_recv()


class SharedReduction:
    def __init__(self, buffers, total, n_pts, n_fn):
        self.r = SimpleNamespace(**buffers)
        self.total, self.n_pts, self.n_fn = total, n_pts, n_fn
        self.part = self.r.stage.shape[0] // n_pts
        self.p, self.z = lax.axis_index("pts"), lax.axis_index("fn")
        self.steps = [self.add, self.end]
        self.waits = [5.0, 5.0]

    @staticmethod
    def scratch(rows, n_pts, n_fn):
        dma = pltpu.SemaphoreType.DMA
        return dict(
            stage=pltpu.VMEM((rows, D), f32),
            slots=pltpu.VMEM((n_fn, rows // n_pts, D), f32),
            fn_sends=dma((n_fn,)),
            fn_receives=dma((n_fn,)),
            sends=dma((n_pts,)),
            receives=dma((n_pts,)),
            local_sem=dma((1,)),
        )

    def mine(self, place):
        return pl.ds(pl.multiple_of(place * self.part, 8), self.part)

    def fn_copy(self, offset, arriving=False):
        other = lax.rem(self.z + offset, self.n_fn)
        slot = other if arriving else self.z
        src, dst = self.r.stage.at[self.mine(self.p)], self.r.slots.at[slot]
        return Reduction.remote(
            src, dst, self.r.fn_sends.at[offset], self.r.fn_receives.at[slot], {"fn": other}
        )

    def out_copy(self, offset, arriving=False):
        other = lax.rem(self.p + offset, self.n_pts)
        place = other if arriving else self.p
        src, dst = self.r.stage.at[self.mine(self.p)], self.total.at[self.mine(place)]
        return Reduction.remote(
            src, dst, self.r.sends.at[offset], self.r.receives.at[place], {"pts": other}
        )

    def local_copy(self):
        src, dst = self.r.stage.at[self.mine(self.p)], self.total.at[self.mine(self.p)]
        return pltpu.make_async_copy(src, dst, self.r.local_sem.at[0])

    def begin(self):
        for offset in range(1, self.n_fn):
            self.fn_copy(offset).start()
        self.r.slots[self.z] = self.r.stage[self.mine(self.p), :]

    def step(self):
        self.steps.pop(0)()

    def add(self):
        for offset in range(1, self.n_fn):
            self.fn_copy(offset, True).wait_recv()
        for offset in range(1, self.n_fn):
            self.fn_copy(offset).wait_send()
        sums = self.r.slots[0]
        for place in range(1, self.n_fn):
            sums = sums + self.r.slots[place]
        self.r.stage[self.mine(self.p), :] = sums
        self.local_copy().start()
        for offset in range(1, self.n_pts):
            self.out_copy(offset).start()

    def end(self):
        self.local_copy().wait()
        for offset in range(1, self.n_pts):
            self.out_copy(offset, True).wait_recv()
        for offset in range(1, self.n_pts):
            self.out_copy(offset).wait_send()


HALF = EXPERTS * D
PIECES = {
    ("out", 1, 1): ("out0", 512),
    ("in", 1, 1): ("in0", 512),
    ("out", 1, 0): ("out1", 768),
    ("in", 1, 0): ("in1", 512),
    ("out", 0, 1): ("out2", 512),
    ("in", 0, 1): ("in0", 768),
    ("out", 0, 0): ("out1", 768),
    ("in", 0, 0): ("in1", 512),
    "points": ("points", 256),
}
FIRST_ROW = {name: sum(rows for _, rows in list(PIECES.values())[:n]) for n, name in enumerate(PIECES)}
TOTAL_ROWS = sum(rows for _, rows in PIECES.values())


def function_rows(n_pts):
    return -(-(2 * D + 8) // (8 * n_pts)) * 8 * n_pts


WEIGHTS = ["ap", "ao", "ng", "nb", "ewi", "ebi", "ewo", "ebo", "gwi", "gbi", "gwo"]
IN_NAMES = ["x", "co", "ff", "counts", "present"] + WEIGHTS + ["cot"]
OUT_NAMES = ["q_out", "q_grad", "f_grad", "total", "f_total"]
KEPT_NAMES = ["kept_hi", "kept_lo", "kept_slope"]


def make_kernel(n_pts, n_fn, points, f_rows):
    tile = next(width for width in (256, 128) if points % width == 0)
    wide_tile = next(width for width in (512, 256, 128) if points % width == 0)
    f_tile = next(width for width in (512, 256, 128) if f_rows % width == 0)
    f_tiles = f_rows // f_tile
    inner = min(n_pts, GROUP)
    pts_stages = [("pts", 1, inner)]
    if n_pts > inner:
        pts_stages.append(("pts", inner, n_pts // inner))
    fn_stages = [("fn", 1, n_fn)]
    every = pts_stages + fn_stages
    syncs = {
        "P0": (fn_stages, 72),
        "P1": (fn_stages, 72),
        "S0": (every, 24),
        "S1": (every, 24),
        "dS1": (every, 24),
        "dC1": (every, 72),
        "dS0": (every, 24),
        "dC0": (every, 72),
    }
    scratch = dict(
        XS=pltpu.VMEM((6, D, points), f32),
        CUR=pltpu.VMEM((D, points), f32),
        COL=pltpu.VMEM((D, D), f32),
        TMP=pltpu.VMEM((32, D), f32),
        TMPK=pltpu.VMEM((16, 3 * D), f32),
        WC=pltpu.VMEM((LAYERS, 3 * D, D), bf16),
        WS=pltpu.VMEM((LAYERS, 3 * D, 3 * D), bf16),
        WF=pltpu.VMEM((LAYERS, 3 * D, 2 * D), bf16),
        WAO=pltpu.VMEM((LAYERS, 2, 3 * D, D), bf16),
        WI=pltpu.VMEM((4, 3 * D + 16, HID), bf16),
        WO=pltpu.VMEM((4, HID, 2 * D), bf16),
        BO=pltpu.VMEM((4, 32, D), bf16),
        BK=pltpu.VMEM((4, 16, 3 * D), bf16),
        GW=pltpu.VMEM((4, 32, D), bf16),
        GWK=pltpu.VMEM((4, 16, 3 * D), bf16),
        GWR=pltpu.VMEM((4, 32, D), bf16),
        CA=pltpu.VMEM((32, points), bf16),
        G=pltpu.VMEM((4, 8, points), f32),
        GB=pltpu.VMEM((4, 32, points), bf16),
        DL=pltpu.VMEM((4, 8, points), f32),
        GHH=pltpu.VMEM((3, HID, points), bf16),
        GHL=pltpu.VMEM((3, HID, points), bf16),
        GD=pltpu.VMEM((2, HID, points), f32),
        QCH=pltpu.VMEM((LAYERS, D, points), bf16),
        QCL=pltpu.VMEM((LAYERS, D, points), bf16),
        QSH=pltpu.VMEM((LAYERS, 3 * D, points), bf16),
        QSL=pltpu.VMEM((LAYERS, 3 * D, points), bf16),
        CR=pltpu.VMEM((LAYERS, 416, 3 * D), bf16),
        SE=pltpu.VMEM((LAYERS, 144, 3 * D), bf16),
        DK=pltpu.VMEM((432, D), bf16),
        PK=pltpu.VMEM((72, D), f32),
        ACC=pltpu.VMEM((416, D), f32),
        A4=pltpu.VMEM((4, 2 * D + 16, points), bf16),
        CC=pltpu.VMEM((4, 2 * D, points), bf16),
        OH=pltpu.VMEM((2, D, points), bf16),
        OL=pltpu.VMEM((2, D, points), bf16),
        DZH=pltpu.VMEM((4 * D, points), bf16),
        DZL=pltpu.VMEM((4 * D, points), bf16),
        LG=pltpu.VMEM((8, D, D), f32),
        GGA=pltpu.VMEM((4, 8, D), f32),
        GGB=pltpu.VMEM((4, 8, D), f32),
        dma_in=pltpu.SemaphoreType.DMA((10,)),
        dma_keep=pltpu.SemaphoreType.DMA((2, 2, 3)),
    )
    dma = pltpu.SemaphoreType.DMA
    for name, (stages, rows) in syncs.items():
        scratch[name] = [
            [pltpu.VMEM((stage[2], rows, D), f32), dma((stage[2],)), dma((stage[2],))] for stage in stages
        ]
    for buffers in dict.fromkeys(buffers for buffers, _ in PIECES.values()):
        rows = max(count for name, count in PIECES.values() if name == buffers)
        scratch[buffers] = Reduction.scratch(rows, n_pts, n_fn)
    scratch["functions"] = SharedReduction.scratch(function_rows(n_pts), n_pts, n_fn)
    shapes, tree = jax.tree.flatten(scratch)
    names = IN_NAMES + OUT_NAMES + KEPT_NAMES

    def kernel(*refs):
        r = SimpleNamespace(
            **dict(zip(names, refs)), **jax.tree.unflatten(tree, refs[len(names) :])
        )
        ex = {name: Exchange(stages, *zip(*vars(r)[name])) for name, (stages, _) in syncs.items()}
        piece = {
            name: Reduction(vars(r)[buffers], r.total, rows, FIRST_ROW[name], n_pts, n_fn)
            for name, (buffers, rows) in PIECES.items()
        }

        piece["functions"] = SharedReduction(r.functions, r.f_total, n_pts, n_fn)

        def staging(name):
            return piece[name].r.stage

        def small(layer):
            return staging("points").at[pl.ds(D + 32 * layer, 32)]

        barrier = pltpu.get_barrier_semaphore()
        greeted = 0
        for stage in every:
            for offset in range(1, stage[2]):
                _, device = Exchange.member(stage, offset)
                pl.semaphore_signal(barrier, inc=1, device_id=device, device_id_type=MESH)
                greeted += 1

        def weight_in(layer):
            into = r.GD.at[layer]
            every_copy = []
            for s in range(2):
                n = 4 * layer + 2 * s
                every_copy.append(
                    pltpu.make_async_copy(
                        r.ewi.at[layer, s],
                        into.at[pl.ds(s * EXPERTS * D, EXPERTS * D), pl.ds(0, FH)],
                        r.dma_in.at[n],
                    )
                )
                every_copy.append(
                    pltpu.make_async_copy(
                        r.ewo.at[layer, s],
                        into.at[:, pl.ds(FH + D * s, D)],
                        r.dma_in.at[n + 1],
                    )
                )
            return every_copy

        def points_in():
            return (
                pltpu.make_async_copy(r.x, r.q_grad, r.dma_in.at[8]),
                pltpu.make_async_copy(r.cot, r.q_out, r.dma_in.at[9]),
            )

        def kept(n, back):
            pairs = ((r.GHH, r.kept_hi), (r.GHL, r.kept_lo), (r.GD, r.kept_slope))
            copies = []
            for k, (near, far) in enumerate(pairs):
                ends = (near.at[n], far.at[n])
                src, dst = reversed(ends) if back else ends
                copies.append(pltpu.make_async_copy(src, dst, r.dma_keep.at[n, int(back), k]))
            return copies

        def start(copies):
            for copy in copies:
                copy.start()

        def wait(copies):
            for copy in copies:
                copy.wait()

        for copy in weight_in(0) + list(points_in()) + weight_in(1):
            copy.start()

        square, mask8 = head_masks()
        square = lambda: head_masks()[0]
        mask8 = lambda: head_masks()[1]

        def over_tiles(body, width=tile):
            def step(j, carry):
                body(pl.ds(pl.multiple_of(j * width, width), width))
                return carry

            lax.fori_loop(0, points // width, step, 0)

        def over(count, body):
            def step(j, carry):
                body(j)
                return carry

            lax.fori_loop(0, count, step, 0)

        def rows_of(e, width):
            return pl.ds(pl.multiple_of(e * width, width), width)

        def col(layer, j):
            return r.COL[:, layer * 5 + j : layer * 5 + j + 1]

        def bias_col(layer, j):
            return r.COL[:, 16 + layer * 5 + j : 17 + layer * 5 + j]

        norm_slot = {4: 0, 3: 0, 2: 1, 0: 2, 1: 3}

        def add_norm_grads(j, d_normed, unit):
            n = 2 * norm_slot[j]
            r.LG[n] += fold_lanes(d_normed * unit)
            r.LG[n + 1] += fold_lanes(d_normed)

        def clear_norm_grads(*which):
            for j in which:
                n = 2 * norm_slot[j]
                r.LG[n : n + 2] = jnp.zeros((2, D, D), f32)

        def put_norm_grads(layer, *which):
            for j in which:
                n = 2 * norm_slot[j]
                gain, bias = row_sum(r.LG[n]), row_sum(r.LG[n + 1])
                if j == 1 and layer == 0:
                    staging("functions")[2 * D : 2 * D + 1, :] = gain
                    staging("functions")[2 * D + 1 : 2 * D + 2, :] = bias
                    continue
                share = 1.0 / n_pts if j == 1 else 1.0
                small(layer)[j : j + 1, 0:D] = gain * share
                small(layer)[j : j + 1, D:] = bias * share

        def row_stack(ref, at, w):
            hi, lo = split(w)
            ref[at + (slice(0, D),)] = hi
            ref[at + (slice(D, 2 * D),)] = lo
            ref[at + (slice(2 * D, 3 * D),)] = hi

        def prepare_norms():
            r.COL[...] = jnp.zeros((D, D), f32)
            for layer in range(LAYERS):
                for j in range(5):
                    n = layer * 5 + j
                    r.COL[n : n + 1, :] = r.ng[j, layer : layer + 1]
                    r.COL[16 + n : 17 + n, :] = r.nb[j, layer : layer + 1]
            r.COL[...] = r.COL[...].T

        def prepare_func(layer):
            both = jnp.concatenate([r.ap[layer, 0, 1], r.ap[layer, 0, 2]], axis=1)
            row_stack(r.WF, (layer,), both)

        def prepare_attention(layer):
            row_stack(r.WC, (layer,), r.ap[layer, 0, 0])
            three = jnp.concatenate([r.ap[layer, 1, n] for n in range(3)], axis=1)
            row_stack(r.WS, (layer,), three)
            for c in range(2):
                row_stack(r.WAO, (layer, c), r.ao[layer, c])

        def small_rows(ref, n, hi, lo, count):
            tmp = r.TMP
            tmp[...] = jnp.zeros(tmp.shape, f32)
            tmp[0:count] = hi
            tmp[8 : 8 + count] = lo
            tmp[16 : 16 + count] = hi
            ref[n] = tmp[...].astype(bf16)

        def small_cols(ref, n, w):
            hi, lo = split(w)
            tmp = r.TMPK
            tmp[...] = jnp.zeros(tmp.shape, f32)
            tmp[0:4] = jnp.concatenate([hi.astype(f32), lo.astype(f32), hi.astype(f32)], axis=1)
            ref[n] = tmp[...].astype(bf16)

        def pair(v):
            hi, lo = split(v)
            return hi.astype(f32), lo.astype(f32)

        def prepare_experts(layer, s):
            n = 2 * layer + s
            staged = r.GD

            def body(e):
                w = staged[layer, rows_of(s * EXPERTS + e, D), 0:FH]
                hi, lo = split(w)
                cols = rows_of(e, FH)
                r.WI[n, 0:D, cols] = hi
                r.WI[n, D : 2 * D, cols] = lo
                r.WI[n, 2 * D : 3 * D, cols] = hi
                b_hi, b_lo = pair(r.ebi[layer, s, pl.ds(e, 1), :])
                r.WI[n, 3 * D : 3 * D + 16, cols] = jnp.concatenate(
                    [b_hi, b_lo, jnp.zeros((14, FH), f32)], axis=0
                ).astype(bf16)
                w = staged[layer, cols, FH + D * s : FH + D * (s + 1)]
                hi, lo = split(w)
                r.WO[n, cols, :] = jnp.concatenate([hi, lo], axis=1)

            over(EXPERTS, body)
            b_hi, b_lo = pair(r.ebo[layer, s])
            small_rows(r.BO, n, b_hi, b_lo, EXPERTS)
            small_cols(r.BK, n, r.ebo[layer, s])

        def prepare_gates(layer, s):
            n = 2 * layer + s
            for k in range(3):
                r.TMP[k : k + 1] = r.gwi[layer, k, s : s + 1]
            r.TMP[3:4] = r.gbi[layer, s : s + 1]
            hi, lo = pair(r.TMP[0:4])
            small_rows(r.GW, n, hi, lo, 4)
            hi, lo = pair(r.gwo[layer, s])
            small_rows(r.GWR, n, hi, lo, EXPERTS)
            small_cols(r.GWK, n, r.gwo[layer, s])

        def prepare_coords():
            hi, lo = pair(r.co[...])
            tmp = r.G
            tmp[...] = jnp.zeros(tmp.shape, f32)
            one = jnp.ones((1, points), f32)
            tmp[0, 0:3], tmp[0, 3:4] = hi, one
            tmp[1, 0:3], tmp[1, 3:4] = hi, one
            tmp[2, 0:3] = lo
            r.CA[...] = jnp.concatenate([tmp[n] for n in range(4)], axis=0).astype(bf16)

        def gates(n):
            def body(s):
                hidden, _ = gelu_both(tn(r.GW[n], r.CA[:, s]))
                logits = nn(r.GWK[n], k3(*split(hidden)))[0:8]
                real = lax.broadcasted_iota(jnp.int32, logits.shape, 0) < EXPERTS
                logits = jnp.where(real, logits, -1e30)
                power = jnp.exp(logits - jnp.max(logits, axis=0, keepdims=True))
                power = jnp.where(real, power, 0.0)
                share = power / jnp.sum(power, axis=0, keepdims=True)
                r.G[n, :, s] = share
                hi, lo = pair(share)
                r.GB[n, :, s] = jnp.concatenate([hi, hi, lo, jnp.zeros_like(hi)], axis=0).astype(bf16)

            over_tiles(body)

        def gates_back(n):
            r.GGA[n] = jnp.zeros((8, D), f32)
            r.GGB[n] = jnp.zeros((8, D), f32)

            def body(s):
                hidden, slope = gelu_both(tn(r.GW[n], r.CA[:, s]))
                hi, lo = pair(r.DL[n, :, s])
                stacked = jnp.concatenate([hi, hi, lo, jnp.zeros_like(hi)], axis=0).astype(bf16)
                h_hi, h_lo = split(hidden)
                first = nt(stacked, h_hi)
                r.GGA[n] += first[0:8] + first[16:24] + nt(stacked, h_lo)[0:8]
                d_hi, d_lo = split(tn(r.GWR[n], stacked) * slope)
                coords = r.CA[:, s]
                first = nt(coords, d_hi)
                r.GGB[n] += first[0:8] + first[16:24] + nt(coords, d_lo)[0:8]

            over_tiles(body)

        def func_parts(layer, f, s):
            unit, scale = normalise(r.ff[f, s, :].T)
            hi, lo = split(unit * col(layer, 1) + bias_col(layer, 1))
            kv = tn(r.WF[layer], k3(hi, lo))
            position = (
                lax.axis_index("fn") * f_rows
                + s.start
                + lax.broadcasted_iota(jnp.int32, (1, s.size), 1)
            )
            mask = jnp.where(position < r.counts[f], 1.0, 0.0).astype(f32)
            return unit, scale, hi, lo, head_softmax(kv[:D]) * mask, kv[D:]

        ones = lambda width: jnp.ones((16, width), bf16)

        def summary_part(k_hi, k_lo, v_hi, v_lo):
            width = k_hi.shape[1]
            v_ones = jnp.concatenate([v_hi, ones(width)], axis=0)
            wide = nt(v_ones, jnp.concatenate([k_hi, k_lo], axis=0))
            part = wide[:, :D] + wide[:, D:]
            return jnp.concatenate([part[:D] + nt(v_lo, k_hi), part[D:]], axis=0)

        def func_forward(layer):
            def per_function(f):
                r.ACC[0:144] = jnp.zeros((144, D), f32)

                def body(j):
                    _, _, _, _, keys, values = func_parts(layer, f, rows_of(j, f_tile))
                    r.ACC[0:144] += summary_part(*split(keys), *split(values))

                over(f_tiles, body)
                packed = pack_summary(r.ACC[0:D], r.ACC[D : D + 1], square())
                r.PK[rows_of(f, 24), :] = packed

            over(NF, per_function)
            return r.PK[...]

        def use_cross(layer, block):
            spread, rows = [], []
            for f in range(NF):
                wide, total = unpack_summary(block[24 * f : 24 * f + 24], square())
                spread.append(wide)
                rows.append(total * mask8())
            full = jnp.concatenate(spread + rows + [jnp.zeros((8, D), f32)], axis=0)
            hi, lo = split(full)
            r.CR[layer] = jnp.concatenate([hi, lo, hi], axis=1)

        def use_self(layer, block):
            wide, total = unpack_summary(block, square())
            full = jnp.concatenate([wide, total * mask8(), jnp.zeros((8, D), f32)], axis=0)
            hi, lo = split(full)
            r.SE[layer] = jnp.concatenate([hi, lo, hi], axis=1)

        def use_back(block):
            wide, total = unpack_summary(block, square())
            hi, lo = split(jnp.concatenate([wide, total, jnp.zeros((15, D), f32)], axis=0))
            r.DK[...] = jnp.concatenate([hi, lo, hi], axis=0)

        def keys_values_back(k_hi, k_lo, v_hi, v_lo):
            one = ones(k_hi.shape[1])
            zero = jnp.zeros_like(one)
            d_keys = tn(r.DK[...], jnp.concatenate([v_hi, one, v_hi, one, v_lo, zero], axis=0))
            both = nn(r.DK[0:272], k_hi)
            d_values = both[0:D] + both[144:272] + nn(r.DK[0:D], k_lo)
            return d_keys, d_values

        def func_backward(layer, into_keys, into_values, share):
            clear_norm_grads(1)
            into_keys[...] = jnp.zeros((D, D), f32)
            into_values[...] = jnp.zeros((D, D), f32)

            def per_function(f):
                use_back(r.PK[rows_of(f, 24), :])

                def body(j):
                    s = rows_of(j, f_tile)
                    unit, scale, a_hi, a_lo, keys, values = func_parts(layer, f, s)
                    d_keys, d_values = keys_values_back(*split(keys), *split(values))
                    d_z = jnp.concatenate([head_softmax_back(keys, d_keys), d_values], axis=0)
                    z_hi, z_lo = split(d_z)
                    wide = nt(jnp.concatenate([a_hi, a_lo], axis=0), z_hi)
                    full = wide[:D] + wide[D:] + nt(a_hi, z_lo)
                    into_keys[...] += full[:, :D] * share
                    into_values[...] += full[:, D:] * share
                    d_normed = nn_rows(r.WF, (layer,), z_hi, z_lo)
                    add_norm_grads(1, d_normed, unit)
                    d_rows = norm_back(d_normed, col(layer, 1), unit, scale).T
                    if layer == LAYERS - 1:
                        r.f_grad[f, s, :] = d_rows
                    else:
                        r.f_grad[f, s, :] += d_rows

                over(f_tiles, body)

            over(NF, per_function)
            put_norm_grads(layer, 1)

        def present_shares(width):
            total = r.present[0] + r.present[1] + r.present[2]
            total = jnp.full((1, width), total, jnp.int32).astype(f32)
            return [
                jnp.full((1, width), r.present[f], jnp.int32).astype(f32) / total for f in range(NF)
            ]

        def cross_apply(layer, q_hi, q_lo):
            applied = nn(r.CR[layer], k3(q_hi, q_lo))
            outs, inverse = [], []
            for f in range(NF):
                spread = head_spread(1.0 / applied[3 * D + 8 * f : 3 * D + 8 * f + 8])
                inverse.append(spread)
                outs.append(applied[D * f : D * (f + 1)] * spread)
            shares = present_shares(q_hi.shape[1])
            mixed = outs[0] * shares[0] + outs[1] * shares[1] + outs[2] * shares[2]
            return outs, inverse, shares, mixed

        def self_apply(layer, q_hi, q_lo):
            applied = nn(r.SE[layer], k3(q_hi, q_lo))
            spread = head_spread(1.0 / applied[D : D + 8])
            return applied[:D] * spread, spread

        def cross_forward(layer, x, s):
            unit, _ = normalise(x)
            normed = unit * col(layer, 0) + bias_col(layer, 0)
            q_hi, q_lo = split(head_softmax(tn(r.WC[layer], k3(*split(normed)))))
            r.QCH[layer, :, s] = q_hi
            r.QCL[layer, :, s] = q_lo
            _, _, _, mixed = cross_apply(layer, q_hi, q_lo)
            return x + tn(r.WAO[layer, 0], k3(*split(mixed)))

        def experts_forward(layer, which, x, s):
            n = 2 * layer + which
            j = 2 + 2 * which
            unit, _ = normalise(x)
            hi, lo = split(unit * col(layer, j) + bias_col(layer, j))
            stacked = jnp.concatenate([hi, hi, lo, ones(hi.shape[1])], axis=0)
            share = r.G[n, :, s]
            for c in range(HID // CHUNK):
                rows = slice(c * CHUNK, (c + 1) * CHUNK)
                e = c * CHUNK // FH
                value, slope = gelu_both(tn(r.WI[n, :, rows], stacked))
                h_hi, h_lo = split(value * share[e : e + 1])
                r.GHH[which, rows, s] = h_hi
                r.GHL[which, rows, s] = h_lo
                r.GD[which, rows, s] = slope * share[e : e + 1]
            both = tn(r.WO[n], r.GHH[which, :, s])
            more = tn(r.WO[n, :, 0:D], r.GHL[which, :, s])
            return x + tn(r.BO[n], r.GB[n, :, s]) + (both[:D] + both[D:] + more)

        def stream(layer, n):
            return 4 * layer + n - 1

        def first_stream(layer, s):
            return r.XS[stream(layer, 0), :, s] if layer else r.q_grad[s, :].T

        def phase_a(layer):
            r.ACC[0:144] = jnp.zeros((144, D), f32)

            xs = r.XS

            def cross(s):
                xs[stream(layer, 1), :, s] = cross_forward(layer, first_stream(layer, s), s)

            over_tiles(cross)

            def experts(s):
                x1 = xs[stream(layer, 1), :, s]
                xs[stream(layer, 2), :, s] = experts_forward(layer, 0, x1, s)

            over_tiles(experts, wide_tile)
            if layer == 0:
                start(kept(0, False))

            def sums(s):
                x2 = xs[stream(layer, 2), :, s]
                unit, _ = normalise(x2)
                normed = unit * col(layer, 3) + bias_col(layer, 3)
                qkv = tn(r.WS[layer], k3(*split(normed)))
                q_hi, q_lo = split(head_softmax(qkv[:D]))
                k_hi, k_lo = split(head_softmax(qkv[D : 2 * D]))
                v_hi, v_lo = split(qkv[2 * D :])
                r.QSH[layer, :, s] = jnp.concatenate([q_hi, k_hi, v_hi], axis=0)
                r.QSL[layer, :, s] = jnp.concatenate([q_lo, k_lo, v_lo], axis=0)
                r.ACC[0:144] += summary_part(k_hi, k_lo, v_hi, v_lo)

            over_tiles(sums)
            return pack_summary(r.ACC[0:D], r.ACC[D : D + 1], square())

        def self_forward(layer, s):
            mixed, _ = self_apply(layer, r.QSH[layer, 0:D, s], r.QSL[layer, 0:D, s])
            x2 = r.XS[stream(layer, 2), :, s]
            return x2 + tn(r.WAO[layer, 1], k3(*split(mixed)))

        def keep_cot(m, cot, s):
            c_hi, c_lo = split(cot)
            r.CC[m, 0:D, s] = c_hi
            r.CC[m, D : 2 * D, s] = c_lo

        def experts_backward(layer, which, x, cot, s):
            n = 2 * layer + which
            j = 2 + 2 * which
            c_hi, c_lo = r.CC[2 * which + 1, 0:D, s], r.CC[2 * which + 1, D : 2 * D, s]
            stacked = jnp.concatenate([c_hi, c_hi], axis=0)
            share = r.G[n, :, s]
            scores = share * nn(r.BK[n], k3(c_hi, c_lo))[0:8]
            place = lax.broadcasted_iota(jnp.int32, scores.shape, 0)

            part = None
            for c in range(HID // CHUNK):
                rows = slice(c * CHUNK, (c + 1) * CHUNK)
                back = nn(r.WO[n, rows, :], stacked) + nn(r.WO[n, rows, 0:D], c_lo)
                hidden = join(r.GHH[which, rows, s], r.GHL[which, rows, s])
                terms = (back * hidden).reshape(CHUNK // 8, 8, back.shape[1])
                terms = jnp.sum(terms, axis=0)
                part = terms if part is None else part + terms
                if (c + 1) * CHUNK % FH == 0:
                    total = jnp.sum(part, axis=0, keepdims=True)
                    scores = scores + jnp.where(place == c * CHUNK // FH, total, 0.0)
                    part = None
                z_hi, z_lo = split(back * r.GD[which, rows, s])
                r.GHH[2, rows, s] = z_hi
                r.GHL[2, rows, s] = z_lo
            both = nn(r.WI[n, 0 : 2 * D, :], r.GHH[2, :, s])
            d_normed = both[:D] + both[D:] + nn(r.WI[n, 0:D, :], r.GHL[2, :, s])
            r.DL[n, :, s] = scores - share * jnp.sum(scores, axis=0, keepdims=True)
            unit, scale = normalise(x)
            keep_normed(layer, j, unit, s, which * 2 + 1)
            add_norm_grads(j, d_normed, unit)
            return cot + norm_back(d_normed, col(layer, j), unit, scale)

        def keep_normed(layer, j, unit, s, n):
            hi, lo = split(unit * col(layer, j) + bias_col(layer, j))
            r.A4[n, 0:D, s] = lo
            r.A4[n, D : 2 * D, s] = hi

        def self_back_first(layer, d_x3, s):
            q_hi, q_lo = r.QSH[layer, 0:D, s], r.QSL[layer, 0:D, s]
            mixed, inverse = self_apply(layer, q_hi, q_lo)
            r.OH[1, :, s], r.OL[1, :, s] = split(mixed)
            c_hi, c_lo = split(d_x3)
            r.CC[2, 0:D, s] = c_hi
            r.CC[2, D : 2 * D, s] = c_lo
            d_num = nn_rows(r.WAO, (layer, 1), c_hi, c_lo) * inverse
            d_den = -head_rows(d_num * mixed)
            n_hi, n_lo = split(jnp.concatenate([d_num, d_den, jnp.zeros_like(d_den)], axis=0))
            r.ACC[0:144] += nt_pair(n_hi, n_lo, jnp.concatenate([q_hi, q_lo], axis=0), q_hi)
            both = tn(r.SE[layer, :, 0 : 2 * D], n_hi)
            d_q = both[:D] + both[D:] + tn(r.SE[layer, :, 0:D], n_lo)
            z_hi, z_lo = split(head_softmax_back(join(q_hi, q_lo), d_q))
            r.DZH[0:D, s] = z_hi
            r.DZL[0:D, s] = z_lo

        def phase_c(layer, tile_body):
            r.ACC[0:144] = jnp.zeros((144, D), f32)
            clear_norm_grads(4)

            def experts(s):
                r.CUR[:, s] = tile_body(s)

            over_tiles(experts, wide_tile)
            over_tiles(lambda s: self_back_first(layer, r.CUR[:, s], s))
            acc = r.ACC
            total = jnp.sum(acc[D : D + 8] * mask8(), axis=0, keepdims=True)
            return pack_summary(acc[0:D], total, square())

        def phase_d(layer, put, after_self, after_experts):
            r.ACC[...] = jnp.zeros(r.ACC.shape, f32)
            clear_norm_grads(3, 2, 0)
            n = 2 * layer

            def self_side(s):
                k_hi, k_lo = r.QSH[layer, D : 2 * D, s], r.QSL[layer, D : 2 * D, s]
                v_hi, v_lo = r.QSH[layer, 2 * D :, s], r.QSL[layer, 2 * D :, s]
                d_keys, d_values = keys_values_back(k_hi, k_lo, v_hi, v_lo)
                d_z = jnp.concatenate([head_softmax_back(join(k_hi, k_lo), d_keys), d_values], axis=0)
                z_hi, z_lo = split(d_z)
                r.DZH[D : 3 * D, s] = z_hi
                r.DZL[D : 3 * D, s] = z_lo
                d_normed = nn_rows(r.WS, (layer,), r.DZH[0 : 3 * D, s], r.DZL[0 : 3 * D, s])
                unit, scale = normalise(r.XS[stream(layer, 2), :, s])
                keep_normed(layer, 3, unit, s, 2)
                add_norm_grads(3, d_normed, unit)
                d_x2 = r.CUR[:, s] + norm_back(d_normed, col(layer, 3), unit, scale)
                r.CUR[:, s] = d_x2
                keep_cot(1, d_x2, s)

            over_tiles(self_side)
            spend(2.5)
            after_self()

            def experts(s):
                x1 = r.XS[stream(layer, 1), :, s]
                r.CUR[:, s] = experts_backward(layer, 0, x1, r.CUR[:, s], s)

            over_tiles(experts, wide_tile)
            spend(4)
            after_experts()

            def cross(s):
                d_x1 = r.CUR[:, s]
                q_hi, q_lo = r.QCH[layer, :, s], r.QCL[layer, :, s]
                outs, inverse, shares, mixed = cross_apply(layer, q_hi, q_lo)
                r.OH[0, :, s], r.OL[0, :, s] = split(mixed)
                c_hi, c_lo = split(d_x1)
                r.CC[0, 0:D, s] = c_hi
                r.CC[0, D : 2 * D, s] = c_lo
                d_o = nn_rows(r.WAO, (layer, 0), c_hi, c_lo)
                d_nums = [d_o * shares[f] * inverse[f] for f in range(NF)]
                d_dens = [-head_rows(d_nums[f] * outs[f]) for f in range(NF)]
                n_hi, n_lo = split(
                    jnp.concatenate(d_nums + d_dens + [jnp.zeros_like(d_dens[0])], axis=0)
                )
                r.ACC[...] += nt_pair(n_hi, n_lo, jnp.concatenate([q_hi, q_lo], axis=0), q_hi)
                both = tn(r.CR[layer, :, 0 : 2 * D], n_hi)
                d_q = both[:D] + both[D:] + tn(r.CR[layer, :, 0:D], n_lo)
                z_hi, z_lo = split(head_softmax_back(join(q_hi, q_lo), d_q))
                r.DZH[3 * D :, s] = z_hi
                r.DZL[3 * D :, s] = z_lo
                d_normed = nn_rows(r.WC, (layer,), z_hi, z_lo)
                unit, scale = normalise(first_stream(layer, s))
                keep_normed(layer, 0, unit, s, 0)
                add_norm_grads(0, d_normed, unit)
                put(s, d_x1 + norm_back(d_normed, col(layer, 0), unit, scale))

            over_tiles(cross)
            acc, blocks = r.ACC, []
            for f in range(NF):
                rows = acc[3 * D + 8 * f : 3 * D + 8 * f + 8] * mask8()
                total = jnp.sum(rows, axis=0, keepdims=True)
                blocks.append(pack_summary(acc[f * D : (f + 1) * D], total, square()))
            return jnp.concatenate(blocks, axis=0)

        def grad_in(layer, which):
            into = staging(("in", layer, which))
            m = 2 * which + 1

            def body(e):
                rows = rows_of(e, FH)
                wide = nt(r.A4[m], r.GHH[2, rows, :])
                more = nt(r.A4[m, D:, :], r.GHL[2, rows, :])
                into[rows_of(e, D), :] = wide[0:D] + wide[D : 2 * D] + more[0:D]
                bias = wide[2 * D : 2 * D + 1] + more[D : D + 1]
                small(layer)[pl.ds(8 + EXPERTS * which + e, 1), :] = bias

            over(EXPERTS, body)
            spend(2)

        def grad_out(layer, which):
            into = staging(("out", layer, which))
            m = 2 * which + 1

            def body(e):
                rows = rows_of(e, FH)
                h_hi, h_lo = r.GHH[which, rows, :], r.GHL[which, rows, :]
                down = pl.ds(pl.multiple_of(lax.rem(e, 2) * FH, FH), FH)
                across = pl.ds(pl.multiple_of(lax.div(e, 2) * D, D), D)
                into[down, across] = nt_pair(h_hi, h_lo, r.CC[m], r.CC[m, 0:D])

            over(EXPERTS, body)
            spend(1.6)

        def grad_gates(layer, which):
            n = 2 * layer + which
            wide = nt(r.GB[n], r.CC[2 * which + 1])
            bias = wide[0:4, :D] + wide[0:4, D:] + wide[16:20, :D]
            at = 16 + EXPERTS * which
            small(layer)[at : at + 4, 0:D] = bias
            gates_back(n)
            spend(1.6)
            small(layer)[at : at + 4, D:] = r.GGA[n, 0:4]
            at = 24 + 3 * which
            small(layer)[at : at + 3, 0:D] = r.GGB[n, 0:3]
            small(layer)[24 + which : 25 + which, D:] = r.GGB[n, 3:4]

        def grad_out_proj(c):
            m = 2 * c
            return nt_pair(r.OH[c], r.OL[c], r.CC[m], r.CC[m, 0:D])

        def grad_proj(c):
            rows = slice(0, 3 * D) if c else slice(3 * D, 4 * D)
            wide = nt(r.A4[2 * c, 0 : 2 * D, :], r.DZH[rows, :])
            return wide[:D] + wide[D:] + nt(r.A4[2 * c, D : 2 * D, :], r.DZL[rows, :])

        def grad_self(into, at):
            full = grad_proj(1)
            into[at : at + D, :] = full[:, 0 : 2 * D]
            into[at + D : at + 2 * D, 0:D] = full[:, 2 * D :]
            into[at + D : at + 2 * D, D:] = grad_out_proj(1)

        def grad_cross(into, at):
            into[at : at + D, 0:D] = grad_proj(0)
            into[at : at + D, D:] = grad_out_proj(0)

        running, clock = [], [0.0]

        def spend(us):
            clock[0] += us
            tick()

        def begin(name):
            piece[name].begin()
            running.append([piece[name], clock[0] + piece[name].waits[0]])

        def advance(entry):
            one = entry[0]
            one.step()
            if one.steps:
                entry[1] = clock[0] + one.waits[len(one.waits) - len(one.steps)]
            else:
                running.remove(entry)

        def tick():
            for entry in list(running):
                if entry[1] <= clock[0]:
                    advance(entry)

        def drain(name=None):
            while True:
                left = [entry for entry in running if name is None or entry[0] is piece[name]]
                if not left:
                    return
                entry = min(left, key=lambda each: each[1])
                clock[0] = max(clock[0], entry[1])
                advance(entry)

        prepare_norms()
        prepare_func(0)
        block = func_forward(0)
        pl.semaphore_wait(barrier, greeted)
        ex["P0"].start(0, block)
        prepare_func(1)
        for layer in range(LAYERS):
            prepare_attention(layer)
        prepare_coords()
        for m in (1, 3):
            r.A4[m, 2 * D :, :] = jnp.ones((16, points), bf16)
        for layer in range(LAYERS):
            for s in range(2):
                prepare_gates(layer, s)
        for copy in weight_in(0) + list(points_in()):
            copy.wait()
        for s in range(2):
            prepare_experts(0, s)
        gates(0)
        gates(1)
        ex["P1"].start(0, func_forward(1))
        use_cross(0, ex["P0"].finish(0))

        block = phase_a(0)
        ex["S0"].start(0, block)
        for copy in weight_in(1):
            copy.wait()
        for s in range(2):
            prepare_experts(1, s)
        gates(2)
        gates(3)
        use_cross(1, ex["P1"].finish(0))
        use_self(0, ex["S0"].finish_all())

        def first_self(s):
            r.XS[stream(0, 3), :, s] = self_forward(0, s)

        over_tiles(first_self)

        def first_out(s):
            x3 = r.XS[stream(0, 3), :, s]
            r.XS[stream(1, 0), :, s] = experts_forward(0, 1, x3, s)

        over_tiles(first_out, wide_tile)
        start(kept(1, False))
        wait(kept(0, False))
        block = phase_a(1)
        ex["S1"].start(0, block)
        use_self(1, ex["S1"].finish_all())

        wait(kept(1, False))

        def last_self(s):
            r.CUR[:, s] = self_forward(1, s)

        over_tiles(last_self)

        def turn(s):
            x3 = r.CUR[:, s]
            x4 = experts_forward(1, 1, x3, s)
            cot = r.q_out[s, :].T
            r.q_out[s, :] = x4.T
            keep_cot(3, cot, s)
            return experts_backward(1, 1, x3, cot, s)

        def put_current(s, v):
            r.CUR[:, s] = v
            keep_cot(3, v, s)

        def put_result(s, v):
            r.q_grad[s, :] = v.T

        for name in ("points", "functions"):
            staging(name)[...] = jnp.zeros(staging(name).shape, f32)
        block = phase_c(1, turn)
        ex["dS1"].start(0, block)
        put_norm_grads(1, 4)
        grad_out(1, 1)
        begin(("out", 1, 1))
        grad_in(1, 1)
        begin(("in", 1, 1))
        start(kept(1, True))
        ex["dS1"].start(1, ex["dS1"].finish(0))
        spend(1)
        grad_gates(1, 1)
        use_back(ex["dS1"].finish_all(1))
        spend(2)

        def after_self(layer):
            name = ("out", layer, 0)
            if not layer:
                drain(("out", 1, 0))
            grad_out(layer, 0)
            grad_self(staging(name), HALF)
            spend(0.8)
            begin(name)

        def after_experts(layer):
            if layer:
                start(kept(0, True))
            else:
                drain(("in", 1, 0))
            grad_in(layer, 0)
            begin(("in", layer, 0))

        block = phase_d(1, put_current, lambda: after_self(1), lambda: after_experts(1))
        ex["dC1"].start(0, block)
        spend(5)
        put_norm_grads(1, 3, 2, 0)
        wait(kept(1, True))
        grad_out(0, 1)
        begin(("out", 0, 1))
        grad_gates(1, 0)

        def second_experts(s):
            return experts_backward(0, 1, r.XS[stream(0, 3), :, s], r.CUR[:, s], s)

        ex["dC1"].start(1, ex["dC1"].finish(0))
        block = phase_c(0, second_experts)
        ex["dS0"].start(0, block)
        spend(6)
        put_norm_grads(0, 4)
        drain(("in", 1, 1))
        into = staging(("in", 0, 1))
        grad_cross(into, HALF)
        grad_in(0, 1)
        r.PK[...] = ex["dC1"].finish_all(1)
        ex["dS0"].start(1, ex["dS0"].finish(0))
        spend(1)
        keys, values = [into.at[pl.ds(HALF + D, D), pl.ds(n * D, D)] for n in range(2)]
        func_backward(1, keys, values, 1.0 / n_pts)
        begin(("in", 0, 1))
        spend(6)
        grad_gates(0, 1)
        use_back(ex["dS0"].finish_all(1))
        wait(kept(0, True))
        block = phase_d(0, put_result, lambda: after_self(0), lambda: after_experts(0))
        ex["dC0"].start(0, block)
        spend(5)
        put_norm_grads(0, 3, 2, 0)
        grad_cross(staging("points"), 0)
        grad_gates(0, 0)
        begin("points")
        ex["dC0"].start(1, ex["dC0"].finish(0))
        spend(2)
        r.PK[...] = ex["dC0"].finish_all(1)
        spend(3)
        keys, values = [staging("functions").at[pl.ds(n * D, D)] for n in range(2)]
        func_backward(0, keys, values, 1.0)
        begin("functions")
        spend(6)
        drain()

    return kernel, shapes


RESULTS = ["q_out", "q_grad", "f_grad"] + WEIGHTS
SMALL = ["ng", "nb", "ebi", "ebo", "gwi", "gbi", "gwo"]


def hand_out(*refs):
    sources = SimpleNamespace(**dict(zip(OUT_NAMES, refs)))
    refs = refs[len(OUT_NAMES) :]
    results = SimpleNamespace(**dict(zip(RESULTS, refs)))
    total, f_total, q_out, q_grad, f_grad, sems = refs[len(RESULTS) :]
    staged = [
        pltpu.make_async_copy(src, dst, sems.at[n])
        for n, (src, dst) in enumerate(
            [
                (sources.f_total, f_total),
                (sources.q_out, q_out),
                (sources.q_grad, q_grad),
                (sources.f_grad, f_grad),
            ]
            + [
                (sources.total.at[pl.ds(FIRST_ROW[name], count)], total.at[pl.ds(FIRST_ROW[name], count)])
                for name, (_, count) in PIECES.items()
            ]
        )
    ]
    for copy in staged:
        copy.start()

    def rows(name, start, count, lanes=slice(None)):
        lanes = pl.ds(lanes * D, D) if isinstance(lanes, int) else lanes
        return total.at[pl.ds(FIRST_ROW[name] + start, count), lanes]

    pairs = [(q_out, results.q_out), (q_grad, results.q_grad), (f_grad, results.f_grad)]
    for layer in range(LAYERS):
        for which in range(2):
            pairs.append((rows(("in", layer, which), 0, HALF), results.ewi.at[layer, which]))
            for n in range(2):
                into = results.ewo.at[layer, which, pl.ds(n * HALF, HALF)]
                pairs.append((rows(("out", layer, which), 0, HALF, n), into))
        self_rows, cross_rows = ("out", layer, 0), ("in", 0, 1)
        for n in range(3):
            pairs.append((rows(self_rows, HALF + n // 2 * D, D, n % 2), results.ap.at[layer, 1, n]))
        pairs.append((rows(self_rows, HALF + D, D, 1), results.ao.at[layer, 1]))
        if layer:
            for n, place in enumerate((0, 2, 3)):
                src = rows(cross_rows, HALF + place // 2 * D, D, place % 2)
                pairs.append((src, results.ap.at[layer, 0, n]))
            pairs.append((rows(cross_rows, HALF, D, 1), results.ao.at[layer, 0]))
        else:
            pairs.append((rows("points", 0, D, 0), results.ap.at[layer, 0, 0]))
            for n in range(2):
                pairs.append((f_total.at[pl.ds(n * D, D)], results.ap.at[layer, 0, 1 + n]))
            pairs.append((rows("points", 0, D, 1), results.ao.at[layer, 0]))
    for copy in staged:
        copy.wait()
    copies = [
        pltpu.make_async_copy(src, dst, sems.at[len(staged) + n]) for n, (src, dst) in enumerate(pairs)
    ]
    for copy in copies:
        copy.start()
    for layer in range(LAYERS):
        mine = rows("points", D + 32 * layer, 32)
        at = pl.ds(layer, 1)
        for j in range(5):
            if j == 1 and layer == 0:
                results.ng[j, at] = f_total[2 * D : 2 * D + 1]
                results.nb[j, at] = f_total[2 * D + 1 : 2 * D + 2]
            else:
                results.ng[j, at] = mine[j : j + 1, 0:D]
                results.nb[j, at] = mine[j : j + 1, D:]
        for which in range(2):
            at = EXPERTS * which
            results.ebi[layer, which] = mine[8 + at : 8 + at + EXPERTS, :]
            results.ebo[layer, which] = mine[16 + at : 16 + at + EXPERTS, 0:D]
            results.gwo[layer, which] = mine[16 + at : 16 + at + EXPERTS, D:]
            for k in range(3):
                row = 24 + 3 * which + k
                results.gwi[layer, k, which : which + 1] = mine[row : row + 1, 0:D]
            results.gbi[layer, which : which + 1] = mine[24 + which : 25 + which, D:]
    for copy in copies:
        copy.wait()


def solution(mesh):
    n_pts, n_fn = mesh.shape["pts"], mesh.shape["fn"]

    def per_device(*args):
        named = dict(zip(IN_NAMES, args))
        points, f_rows = named["x"].shape[0], named["ff"].shape[1]
        kernel, scratch = make_kernel(n_pts, n_fn, points, f_rows)
        named["ewi"] = named["ewi"].reshape(LAYERS, 2, EXPERTS * D, FH)
        named["ewo"] = named["ewo"].reshape(LAYERS, 2, HID, D)
        named["ng"], named["nb"] = [named[n].transpose(1, 0, 2) for n in ("ng", "nb")]
        named["gwi"] = named["gwi"].transpose(0, 2, 1, 3)
        vmem = pl.BlockSpec(memory_space=pltpu.VMEM)
        smem = pl.BlockSpec(memory_space=pltpu.SMEM)
        anywhere = pl.BlockSpec(memory_space=pl.ANY)
        places = {"counts": smem, "present": smem}
        for name in ["x", "cot", "ewi", "ewo", "total", "f_total"] + KEPT_NAMES:
            places[name] = anywhere
        like = lambda name: jax.ShapeDtypeStruct(named[name].shape, f32)
        out_shape = [like(n) for n in ("x", "x", "ff")]
        out_shape.append(jax.ShapeDtypeStruct((TOTAL_ROWS, 256), f32))
        out_shape.append(jax.ShapeDtypeStruct((function_rows(n_pts), D), f32))
        kept = (2, HID, points)
        out_shape += [jax.ShapeDtypeStruct(kept, kind) for kind in (bf16, bf16, f32)]
        outs = pl.pallas_call(
            kernel,
            out_shape=out_shape,
            in_specs=[places.get(n, vmem) for n in IN_NAMES],
            out_specs=[places.get(n, vmem) for n in OUT_NAMES + KEPT_NAMES],
            scratch_shapes=scratch,
            compiler_params=pltpu.CompilerParams(
                collective_id=0, has_side_effects=True, vmem_limit_bytes=int(63.5 * 2**20)
            ),
        )(*[named[n] for n in IN_NAMES])
        results = pl.pallas_call(
            hand_out,
            out_shape=out_shape[:3] + [like(n) for n in WEIGHTS],
            in_specs=[anywhere] * len(OUT_NAMES),
            out_specs=[vmem if n in SMALL else anywhere for n in RESULTS],
            scratch_shapes=[
                pltpu.VMEM(out_shape[n].shape, f32) for n in (3, 4, 0, 1, 2)
            ]
            + [pltpu.SemaphoreType.DMA((64,))],
            compiler_params=pltpu.CompilerParams(vmem_limit_bytes=60 * 2**20),
        )(*outs[: len(OUT_NAMES)])
        results = list(results)
        results[5], results[6] = results[5].transpose(1, 0, 2), results[6].transpose(1, 0, 2)
        results[11] = results[11].transpose(0, 2, 1, 3)
        results[7] = results[7].reshape(LAYERS, 2, EXPERTS, D, FH)
        results[9] = results[9].reshape(LAYERS, 2, EXPERTS, FH, D)
        return tuple(results)

    points = P(("pts", "fn"), None)
    return jax.shard_map(
        per_device,
        mesh=mesh,
        in_specs=(points, P(None, ("pts", "fn")), P(None, "fn", None)) + (P(),) * 13 + (points,),
        out_specs=(points, points, P(None, "fn", None)) + (P(),) * 11,
        check_vma=False,
    )
```

```python
import math
from types import SimpleNamespace

import jax
import jax.numpy as jnp
from jax import lax
from jax.experimental import pallas as pl
from jax.experimental.pallas import tpu as pltpu
from jax.sharding import PartitionSpec as P

D = 128
HEADS = 8
HEAD_SIZE = 16
FH = 256
EXPERTS = 4
HID = EXPERTS * FH
NF = 3
LAYERS = 2
GROUP = 8

f32, bf16 = jnp.float32, jnp.bfloat16
CHUNK = 128
MESH = pl.DeviceIdType.MESH


def split(v):
    hi = v.astype(bf16)
    return hi, (v - hi.astype(f32)).astype(bf16)


def join(hi, lo):
    return hi.astype(f32) + lo.astype(f32)


def dot(a, b, ca, cb):
    return lax.dot_general(a, b, (((ca,), (cb,)), ((), ())), preferred_element_type=f32)


def nn(a, b):
    return dot(a, b, 1, 0)


def tn(a, b):
    return dot(a, b, 0, 0)


def nt(a, b):
    return dot(a, b, 1, 1)


def k3(hi, lo):
    return jnp.concatenate([hi, hi, lo], axis=0)


def nn_rows(w_ref, at, hi, lo):
    both = nn(w_ref[at + (slice(0, 256),)], hi)
    return both[:128] + both[128:] + nn(w_ref[at + (slice(0, 128),)], lo)


def nt_pair(a_hi, a_lo, b_both, b_hi):
    wide = nt(a_hi, b_both)
    n = b_hi.shape[0]
    return wide[:, :n] + wide[:, n:] + nt(a_lo, b_hi)


def normalise(v):
    average = jnp.mean(v, axis=0, keepdims=True)
    centred = v - average
    variance = jnp.mean(centred * centred, axis=0, keepdims=True)
    scale = lax.rsqrt(variance + 1e-05)
    return centred * scale, scale


def norm_back(d_normed, gain_col, unit, scale):
    d_unit = d_normed * gain_col
    first = jnp.mean(d_unit, axis=0, keepdims=True)
    second = jnp.mean(d_unit * unit, axis=0, keepdims=True)
    return scale * (d_unit - first - unit * second)


def by_head(v):
    return v.reshape(HEADS, HEAD_SIZE, v.shape[1])


def head_softmax(v):
    shaped = by_head(v)
    top = jnp.max(shaped, axis=1, keepdims=True)
    power = jnp.exp(shaped - top)
    total = jnp.sum(power, axis=1, keepdims=True)
    return (power * (1.0 / total)).reshape(v.shape)


def head_softmax_back(soft, d_soft):
    total = jnp.sum(by_head(soft * d_soft), axis=1, keepdims=True)
    return (by_head(soft) * (by_head(d_soft) - total)).reshape(soft.shape)


def head_rows(v):
    total = jnp.sum(by_head(v), axis=1, keepdims=True)
    return jnp.concatenate([total[h] for h in range(HEADS)], axis=0)


def head_spread(rows):
    return jnp.concatenate(
        [jnp.broadcast_to(rows[h : h + 1], (HEAD_SIZE, rows.shape[1])) for h in range(HEADS)], axis=0
    )


C1 = 0.7978845608028654
C2 = C1 * 0.044715


def gelu_both(v):
    square = v * v
    gate = 0.5 + 0.5 * jnp.tanh(v * (C1 + C2 * square))
    value = v * gate
    slope = gate + value * (1.0 - gate) * (2.0 * C1 + 6.0 * C2 * square)
    return value, slope


def fold_lanes(v):
    total = v[:, :128]
    for start in range(128, v.shape[1], 128):
        total = total + v[:, start : start + 128]
    return total


def row_sum(folded):
    return jnp.sum(folded.T, axis=0, keepdims=True)


def head_masks():
    rows = lax.broadcasted_iota(jnp.int32, (D, D), 0) // HEAD_SIZE
    cols = lax.broadcasted_iota(jnp.int32, (D, D), 1) // HEAD_SIZE
    square = jnp.where(rows == cols, 1.0, 0.0).astype(f32)
    heads = lax.broadcasted_iota(jnp.int32, (HEADS, D), 0)
    cols8 = lax.broadcasted_iota(jnp.int32, (HEADS, D), 1) // HEAD_SIZE
    return square, jnp.where(heads == cols8, 1.0, 0.0).astype(f32)


def pack_summary(square_part, total_row, square):
    compact = jnp.sum((square_part * square).reshape(HEADS, HEAD_SIZE, D), axis=0)
    return jnp.concatenate([compact, total_row, jnp.zeros((7, D), f32)], axis=0)


def unpack_summary(block, square):
    spread = jnp.concatenate([block[:HEAD_SIZE]] * HEADS, axis=0) * square
    return spread, block[HEAD_SIZE : HEAD_SIZE + 1]


class Exchange:
    def __init__(self, stages, slots, sends, receives):
        self.stages, self.slots, self.sends, self.receives = stages, slots, sends, receives

    @staticmethod
    def place(stage):
        axis, stride, size = stage
        index = lax.axis_index(axis)
        digit = lax.rem(lax.div(index, stride), size)
        return axis, index - digit * stride, digit

    @staticmethod
    def member(stage, offset):
        axis, stride, size = stage
        axis, base, digit = Exchange.place(stage)
        other = lax.rem(digit + offset, size)
        return other, {axis: base + other * stride}

    def copy(self, n, offset, arriving=False):
        stage = self.stages[n]
        _, _, digit = self.place(stage)
        other, device = self.member(stage, offset)
        place = other if arriving else digit
        return pltpu.make_async_remote_copy(
            src_ref=self.slots[n].at[place],
            dst_ref=self.slots[n].at[place],
            send_sem=self.sends[n].at[offset],
            recv_sem=self.receives[n].at[place],
            device_id=device,
            device_id_type=MESH,
        )

    def start(self, n, value):
        _, _, digit = self.place(self.stages[n])
        self.slots[n][digit] = value
        for offset in range(1, self.stages[n][2]):
            self.copy(n, offset).start()

    def finish(self, n):
        size = self.stages[n][2]
        for offset in range(1, size):
            self.copy(n, offset, True).wait_recv()
        total = self.slots[n][0]
        for place in range(1, size):
            total = total + self.slots[n][place]
        for offset in range(1, size):
            self.copy(n, offset).wait_send()
        return total

    def finish_all(self, n=0):
        while True:
            total = self.finish(n)
            n += 1
            if n == len(self.stages):
                return total
            self.start(n, total)


class Reduction:
    def __init__(self, buffers, total, rows, first, n_pts, n_fn):
        self.r = SimpleNamespace(**buffers)
        self.total, self.first = total, first
        self.plane, self.n_fn = n_pts // 2, n_fn
        self.half = rows // 2
        self.part = self.half // self.plane
        self.deep = self.part % (8 * n_fn) == 0
        self.last = self.part // n_fn if self.deep else self.part
        index, self.z = lax.axis_index("pts"), lax.axis_index("fn")
        self.core, self.q = lax.rem(index, 2), lax.div(index, 2)
        self.steps = [self.add_pair, self.add_plane, self.add_fn, self.spread_plane, self.spread_pair, self.end]
        pair, plane, fn = 1.1 + rows / 1000, 2.5 + rows / 230, 3.2 + rows / 460
        self.waits = [pair, plane, fn, fn if self.deep else 0.3, plane + 0.3, pair + 0.3]

    @staticmethod
    def scratch(rows, n_pts, n_fn):
        plane = n_pts // 2
        part = max(rows // (2 * plane), 1)
        last = part // n_fn if part % (8 * n_fn) == 0 else part
        dma = pltpu.SemaphoreType.DMA
        return dict(
            stage=pltpu.VMEM((rows, 256), f32),
            pair=pltpu.VMEM((rows // 2, 256), f32),
            planes=pltpu.VMEM((plane, part, 256), f32),
            fns=pltpu.VMEM((n_fn, last, 256), f32),
            pair_sems=dma((2,)),
            plane_sends=dma((plane,)),
            plane_receives=dma((plane,)),
            fn_sends=dma((n_fn,)),
            fn_receives=dma((n_fn,)),
            out_pair_sems=dma((2,)),
            out_plane_sends=dma((plane,)),
            out_plane_receives=dma((plane,)),
            out_fn_sends=dma((n_fn,)),
            out_fn_receives=dma((n_fn,)),
            local_sem=dma((1,)),
        )

    @staticmethod
    def remote(src, dst, send, receive, device):
        return pltpu.make_async_remote_copy(
            src_ref=src, dst_ref=dst, send_sem=send, recv_sem=receive, device_id=device, device_id_type=MESH
        )

    def rows(self, start, count):
        return pl.ds(pl.multiple_of(start, 8), count)

    def own_part(self):
        return self.core * self.half + self.q * self.part

    def own_last(self):
        return self.own_part() + (self.z * self.last if self.deep else 0)

    def in_total(self, start, count):
        return self.total.at[self.rows(self.first + start, count)]

    def pair_copy(self):
        away = self.r.stage.at[self.rows((1 - self.core) * self.half, self.half)]
        sems = self.r.pair_sems
        device = {"pts": 2 * self.q + 1 - self.core}
        return self.remote(away, self.r.pair.at[pl.ds(0, self.half)], sems.at[0], sems.at[1], device)

    def plane_copy(self, offset, arriving=False):
        other = lax.rem(self.q + offset, self.plane)
        src = self.r.stage.at[self.rows(self.core * self.half + other * self.part, self.part)]
        slot = other if arriving else self.q
        return self.remote(
            src,
            self.r.planes.at[slot, pl.ds(0, self.part)],
            self.r.plane_sends.at[offset],
            self.r.plane_receives.at[slot],
            {"pts": 2 * other + self.core},
        )

    def fn_copy(self, offset, arriving=False):
        other = lax.rem(self.z + offset, self.n_fn)
        start = self.own_part() + (other * self.last if self.deep else 0)
        slot = other if arriving else self.z
        return self.remote(
            self.r.stage.at[self.rows(start, self.last)],
            self.r.fns.at[slot, pl.ds(0, self.last)],
            self.r.fn_sends.at[offset],
            self.r.fn_receives.at[slot],
            {"fn": other},
        )

    def local_copy(self):
        src = self.r.stage.at[self.rows(self.own_last(), self.last)]
        return pltpu.make_async_copy(src, self.in_total(self.own_last(), self.last), self.r.local_sem.at[0])

    def out_fn_copy(self, offset, arriving=False):
        other = lax.rem(self.z + offset, self.n_fn)
        place = other if arriving else self.z
        src = self.r.stage.at[self.rows(self.own_last(), self.last)]
        return self.remote(
            src,
            self.in_total(self.own_part() + place * self.last, self.last),
            self.r.out_fn_sends.at[offset],
            self.r.out_fn_receives.at[place],
            {"fn": other},
        )

    def out_plane_copy(self, offset, arriving=False):
        other = lax.rem(self.q + offset, self.plane)
        place = other if arriving else self.q
        region = self.in_total(self.core * self.half + place * self.part, self.part)
        return self.remote(
            region,
            region,
            self.r.out_plane_sends.at[offset],
            self.r.out_plane_receives.at[place],
            {"pts": 2 * other + self.core},
        )

    def out_pair_copy(self, arriving=False):
        place = 1 - self.core if arriving else self.core
        region = self.in_total(place * self.half, self.half)
        sems = self.r.out_pair_sems
        return self.remote(region, region, sems.at[0], sems.at[1], {"pts": 2 * self.q + 1 - self.core})

    def begin(self):
        self.pair_copy().start()

    def step(self):
        self.steps.pop(0)()

    def add_pair(self):
        self.pair_copy().wait()
        mine = self.rows(self.core * self.half, self.half)
        self.r.stage[mine, :] += self.r.pair[0 : self.half, :]
        for offset in range(1, self.plane):
            self.plane_copy(offset).start()

    def add_plane(self):
        mine = self.rows(self.own_part(), self.part)
        sums = self.r.stage[mine, :]
        for offset in range(1, self.plane):
            self.plane_copy(offset, True).wait_recv()
            sums = sums + self.r.planes[lax.rem(self.q + offset, self.plane), 0 : self.part, :]
        self.r.stage[mine, :] = sums
        for offset in range(1, self.plane):
            self.plane_copy(offset).wait_send()
        for offset in range(1, self.n_fn):
            self.fn_copy(offset).start()

    def add_fn(self):
        mine = self.rows(self.own_last(), self.last)
        self.r.fns[self.z, 0 : self.last, :] = self.r.stage[mine, :]
        for offset in range(1, self.n_fn):
            self.fn_copy(offset, True).wait_recv()
        for offset in range(1, self.n_fn):
            self.fn_copy(offset).wait_send()
        sums = self.r.fns[0, 0 : self.last, :]
        for place in range(1, self.n_fn):
            sums = sums + self.r.fns[place, 0 : self.last, :]
        self.r.stage[mine, :] = sums
        self.local_copy().start()
        if self.deep:
            for offset in range(1, self.n_fn):
                self.out_fn_copy(offset).start()

    def spread_plane(self):
        self.local_copy().wait()
        if self.deep:
            for offset in range(1, self.n_fn):
                self.out_fn_copy(offset, True).wait_recv()
            for offset in range(1, self.n_fn):
                self.out_fn_copy(offset).wait_send()
        for offset in range(1, self.plane):
            self.out_plane_copy(offset).start()

    def spread_pair(self):
        for offset in range(1, self.plane):
            self.out_plane_copy(offset, True).wait_recv()
        for offset in range(1, self.plane):
            self.out_plane_copy(offset).wait_send()
        self.out_pair_copy().start()

    def end(self):
        self.out_pair_copy().wait_send()
        self.out_pair_copy(True).wait_recv()


class SharedReduction:
    def __init__(self, buffers, total, n_pts, n_fn):
        self.r = SimpleNamespace(**buffers)
        self.total, self.n_pts, self.n_fn = total, n_pts, n_fn
        self.part = self.r.stage.shape[0] // n_pts
        self.p, self.z = lax.axis_index("pts"), lax.axis_index("fn")
        self.steps = [self.add, self.end]
        self.waits = [5.0, 5.0]

    @staticmethod
    def scratch(rows, n_pts, n_fn):
        dma = pltpu.SemaphoreType.DMA
        return dict(
            stage=pltpu.VMEM((rows, D), f32),
            slots=pltpu.VMEM((n_fn, rows // n_pts, D), f32),
            fn_sends=dma((n_fn,)),
            fn_receives=dma((n_fn,)),
            sends=dma((n_pts,)),
            receives=dma((n_pts,)),
            local_sem=dma((1,)),
        )

    def mine(self, place):
        return pl.ds(pl.multiple_of(place * self.part, 8), self.part)

    def fn_copy(self, offset, arriving=False):
        other = lax.rem(self.z + offset, self.n_fn)
        slot = other if arriving else self.z
        src, dst = self.r.stage.at[self.mine(self.p)], self.r.slots.at[slot]
        return Reduction.remote(
            src, dst, self.r.fn_sends.at[offset], self.r.fn_receives.at[slot], {"fn": other}
        )

    def out_copy(self, offset, arriving=False):
        other = lax.rem(self.p + offset, self.n_pts)
        place = other if arriving else self.p
        src, dst = self.r.stage.at[self.mine(self.p)], self.total.at[self.mine(place)]
        return Reduction.remote(
            src, dst, self.r.sends.at[offset], self.r.receives.at[place], {"pts": other}
        )

    def local_copy(self):
        src, dst = self.r.stage.at[self.mine(self.p)], self.total.at[self.mine(self.p)]
        return pltpu.make_async_copy(src, dst, self.r.local_sem.at[0])

    def begin(self):
        for offset in range(1, self.n_fn):
            self.fn_copy(offset).start()
        self.r.slots[self.z] = self.r.stage[self.mine(self.p), :]

    def step(self):
        self.steps.pop(0)()

    def add(self):
        for offset in range(1, self.n_fn):
            self.fn_copy(offset, True).wait_recv()
        for offset in range(1, self.n_fn):
            self.fn_copy(offset).wait_send()
        sums = self.r.slots[0]
        for place in range(1, self.n_fn):
            sums = sums + self.r.slots[place]
        self.r.stage[self.mine(self.p), :] = sums
        self.local_copy().start()
        for offset in range(1, self.n_pts):
            self.out_copy(offset).start()

    def end(self):
        self.local_copy().wait()
        for offset in range(1, self.n_pts):
            self.out_copy(offset, True).wait_recv()
        for offset in range(1, self.n_pts):
            self.out_copy(offset).wait_send()


HALF = EXPERTS * D
PIECES = {
    ("out", 1, 1): ("out0", 512),
    ("in", 1, 1): ("in0", 512),
    ("out", 1, 0): ("out1", 768),
    ("in", 1, 0): ("in1", 512),
    ("out", 0, 1): ("out2", 512),
    ("in", 0, 1): ("in0", 768),
    ("out", 0, 0): ("out1", 768),
    ("in", 0, 0): ("in1", 512),
    "points": ("points", 256),
}
FIRST_ROW = {name: sum(rows for _, rows in list(PIECES.values())[:n]) for n, name in enumerate(PIECES)}
TOTAL_ROWS = sum(rows for _, rows in PIECES.values())


def function_rows(n_pts):
    return -(-(2 * D + 8) // (8 * n_pts)) * 8 * n_pts


WEIGHTS = ["ap", "ao", "ng", "nb", "ewi", "ebi", "ewo", "ebo", "gwi", "gbi", "gwo"]
IN_NAMES = ["x", "co", "ff", "counts", "present"] + WEIGHTS + ["cot"]
OUT_NAMES = ["q_out", "q_grad", "f_grad", "total", "f_total"]
KEPT_NAMES = ["kept_hi", "kept_lo", "kept_slope"]


def make_kernel(n_pts, n_fn, points, f_rows):
    tile = next(width for width in (512, 256, 128) if points % width == 0)
    f_tile = next(width for width in (512, 256, 128) if f_rows % width == 0)
    f_tiles = f_rows // f_tile
    inner = min(n_pts, GROUP)
    pts_stages = [("pts", 1, inner)]
    if n_pts > inner:
        pts_stages.append(("pts", inner, n_pts // inner))
    fn_stages = [("fn", 1, n_fn)]
    every = pts_stages + fn_stages
    syncs = {
        "P0": (fn_stages, 72),
        "P1": (fn_stages, 72),
        "S0": (every, 24),
        "S1": (every, 24),
        "dS1": (every, 24),
        "dC1": (every, 72),
        "dS0": (every, 24),
        "dC0": (every, 72),
    }
    scratch = dict(
        XS=pltpu.VMEM((6, D, points), f32),
        CUR=pltpu.VMEM((D, points), f32),
        COL=pltpu.VMEM((D, D), f32),
        TMP=pltpu.VMEM((32, D), f32),
        TMPK=pltpu.VMEM((16, 3 * D), f32),
        WC=pltpu.VMEM((LAYERS, 3 * D, D), bf16),
        WS=pltpu.VMEM((LAYERS, 3 * D, 3 * D), bf16),
        WF=pltpu.VMEM((LAYERS, 3 * D, 2 * D), bf16),
        WAO=pltpu.VMEM((LAYERS, 2, 3 * D, D), bf16),
        WI=pltpu.VMEM((4, 3 * D + 16, HID), bf16),
        WO=pltpu.VMEM((4, HID, 2 * D), bf16),
        BO=pltpu.VMEM((4, 32, D), bf16),
        BK=pltpu.VMEM((4, 16, 3 * D), bf16),
        GW=pltpu.VMEM((4, 32, D), bf16),
        GWK=pltpu.VMEM((4, 16, 3 * D), bf16),
        GWR=pltpu.VMEM((4, 32, D), bf16),
        CA=pltpu.VMEM((32, points), bf16),
        G=pltpu.VMEM((4, 8, points), f32),
        GB=pltpu.VMEM((4, 32, points), bf16),
        DL=pltpu.VMEM((4, 8, points), f32),
        GHH=pltpu.VMEM((3, HID, points), bf16),
        GHL=pltpu.VMEM((3, HID, points), bf16),
        GD=pltpu.VMEM((2, HID, points), f32),
        QCH=pltpu.VMEM((LAYERS, D, points), bf16),
        QCL=pltpu.VMEM((LAYERS, D, points), bf16),
        QSH=pltpu.VMEM((LAYERS, 3 * D, points), bf16),
        QSL=pltpu.VMEM((LAYERS, 3 * D, points), bf16),
        CR=pltpu.VMEM((LAYERS, 416, 3 * D), bf16),
        SE=pltpu.VMEM((LAYERS, 144, 3 * D), bf16),
        DK=pltpu.VMEM((432, D), bf16),
        PK=pltpu.VMEM((72, D), f32),
        ACC=pltpu.VMEM((416, D), f32),
        A4=pltpu.VMEM((4, 2 * D + 16, points), bf16),
        CC=pltpu.VMEM((4, 2 * D, points), bf16),
        OH=pltpu.VMEM((2, D, points), bf16),
        OL=pltpu.VMEM((2, D, points), bf16),
        DZH=pltpu.VMEM((4 * D, points), bf16),
        DZL=pltpu.VMEM((4 * D, points), bf16),
        LG=pltpu.VMEM((8, D, D), f32),
        GGA=pltpu.VMEM((4, 8, D), f32),
        GGB=pltpu.VMEM((4, 8, D), f32),
        dma_in=pltpu.SemaphoreType.DMA((10,)),
        dma_keep=pltpu.SemaphoreType.DMA((2, 2, 3)),
    )
    dma = pltpu.SemaphoreType.DMA
    for name, (stages, rows) in syncs.items():
        scratch[name] = [
            [pltpu.VMEM((stage[2], rows, D), f32), dma((stage[2],)), dma((stage[2],))] for stage in stages
        ]
    for buffers in dict.fromkeys(buffers for buffers, _ in PIECES.values()):
        rows = max(count for name, count in PIECES.values() if name == buffers)
        scratch[buffers] = Reduction.scratch(rows, n_pts, n_fn)
    scratch["functions"] = SharedReduction.scratch(function_rows(n_pts), n_pts, n_fn)
    shapes, tree = jax.tree.flatten(scratch)
    names = IN_NAMES + OUT_NAMES + KEPT_NAMES

    def kernel(*refs):
        r = SimpleNamespace(
            **dict(zip(names, refs)), **jax.tree.unflatten(tree, refs[len(names) :])
        )
        ex = {name: Exchange(stages, *zip(*vars(r)[name])) for name, (stages, _) in syncs.items()}
        piece = {
            name: Reduction(vars(r)[buffers], r.total, rows, FIRST_ROW[name], n_pts, n_fn)
            for name, (buffers, rows) in PIECES.items()
        }

        piece["functions"] = SharedReduction(r.functions, r.f_total, n_pts, n_fn)

        def staging(name):
            return piece[name].r.stage

        def small(layer):
            return staging("points").at[pl.ds(D + 32 * layer, 32)]

        barrier = pltpu.get_barrier_semaphore()
        greeted = 0
        for stage in every:
            for offset in range(1, stage[2]):
                _, device = Exchange.member(stage, offset)
                pl.semaphore_signal(barrier, inc=1, device_id=device, device_id_type=MESH)
                greeted += 1

        def staged(n):
            into = r.GD.at[1]
            first = into.at[pl.ds(n % 2 * HALF, HALF), pl.ds(n // 2 * FH, FH)]
            return first, into.at[:, pl.ds(2 * FH + D * n, D)]

        def weight_in(n):
            first, second = staged(n)
            return [
                pltpu.make_async_copy(r.ewi.at[n // 2, n % 2], first, r.dma_in.at[2 * n]),
                pltpu.make_async_copy(r.ewo.at[n // 2, n % 2], second, r.dma_in.at[2 * n + 1]),
            ]

        def points_in():
            return (
                pltpu.make_async_copy(r.x, r.q_grad, r.dma_in.at[8]),
                pltpu.make_async_copy(r.cot, r.q_out, r.dma_in.at[9]),
            )

        def kept(n, back):
            pairs = ((r.GHH, r.kept_hi), (r.GHL, r.kept_lo), (r.GD, r.kept_slope))
            copies = []
            for k, (near, far) in enumerate(pairs):
                ends = (near.at[n], far.at[n])
                src, dst = reversed(ends) if back else ends
                copies.append(pltpu.make_async_copy(src, dst, r.dma_keep.at[n, int(back), k]))
            return copies

        def start(copies):
            for copy in copies:
                copy.start()

        def wait(copies):
            for copy in copies:
                copy.wait()

        start(weight_in(0) + list(points_in()) + weight_in(1) + weight_in(2) + weight_in(3))

        square, mask8 = head_masks()
        square = lambda: head_masks()[0]
        mask8 = lambda: head_masks()[1]

        def over_tiles(body, width=tile):
            def step(j, carry):
                body(pl.ds(pl.multiple_of(j * width, width), width))
                return carry

            lax.fori_loop(0, points // width, step, 0, unroll=True)

        def over(count, body):
            def step(j, carry):
                body(j)
                return carry

            lax.fori_loop(0, count, step, 0)

        def rows_of(e, width):
            return pl.ds(pl.multiple_of(e * width, width), width)

        def col(layer, j):
            return r.COL[:, layer * 5 + j : layer * 5 + j + 1]

        def bias_col(layer, j):
            return r.COL[:, 16 + layer * 5 + j : 17 + layer * 5 + j]

        norm_slot = {4: 0, 3: 0, 2: 1, 0: 2, 1: 3}

        def add_norm_grads(j, d_normed, unit):
            n = 2 * norm_slot[j]
            r.LG[n] += fold_lanes(d_normed * unit)
            r.LG[n + 1] += fold_lanes(d_normed)

        def clear_norm_grads(*which):
            for j in which:
                n = 2 * norm_slot[j]
                r.LG[n : n + 2] = jnp.zeros((2, D, D), f32)

        def put_norm_grads(layer, *which):
            for j in which:
                n = 2 * norm_slot[j]
                gain, bias = row_sum(r.LG[n]), row_sum(r.LG[n + 1])
                if j == 1 and layer == 0:
                    staging("functions")[2 * D : 2 * D + 1, :] = gain
                    staging("functions")[2 * D + 1 : 2 * D + 2, :] = bias
                    continue
                share = 1.0 / n_pts if j == 1 else 1.0
                small(layer)[j : j + 1, 0:D] = gain * share
                small(layer)[j : j + 1, D:] = bias * share

        def row_stack(ref, at, w):
            hi, lo = split(w)
            ref[at + (slice(0, D),)] = hi
            ref[at + (slice(D, 2 * D),)] = lo
            ref[at + (slice(2 * D, 3 * D),)] = hi

        def prepare_norms():
            r.COL[...] = jnp.zeros((D, D), f32)
            for layer in range(LAYERS):
                for j in range(5):
                    n = layer * 5 + j
                    r.COL[n : n + 1, :] = r.ng[j, layer : layer + 1]
                    r.COL[16 + n : 17 + n, :] = r.nb[j, layer : layer + 1]
            r.COL[...] = r.COL[...].T

        def prepare_func(layer):
            both = jnp.concatenate([r.ap[layer, 0, 1], r.ap[layer, 0, 2]], axis=1)
            row_stack(r.WF, (layer,), both)

        def prepare_attention(layer):
            row_stack(r.WC, (layer,), r.ap[layer, 0, 0])
            three = jnp.concatenate([r.ap[layer, 1, n] for n in range(3)], axis=1)
            row_stack(r.WS, (layer,), three)
            for c in range(2):
                row_stack(r.WAO, (layer, c), r.ao[layer, c])

        def small_rows(ref, n, hi, lo, count):
            tmp = r.TMP
            tmp[...] = jnp.zeros(tmp.shape, f32)
            tmp[0:count] = hi
            tmp[8 : 8 + count] = lo
            tmp[16 : 16 + count] = hi
            ref[n] = tmp[...].astype(bf16)

        def small_cols(ref, n, w):
            hi, lo = split(w)
            tmp = r.TMPK
            tmp[...] = jnp.zeros(tmp.shape, f32)
            tmp[0:4] = jnp.concatenate([hi.astype(f32), lo.astype(f32), hi.astype(f32)], axis=1)
            ref[n] = tmp[...].astype(bf16)

        def pair(v):
            hi, lo = split(v)
            return hi.astype(f32), lo.astype(f32)

        def prepare_experts(layer, s):
            n = 2 * layer + s
            wait(weight_in(n))
            first, second = staged(n)

            def body(e):
                w = first[rows_of(e, D), :]
                hi, lo = split(w)
                cols = rows_of(e, FH)
                r.WI[n, 0:D, cols] = hi
                r.WI[n, D : 2 * D, cols] = lo
                r.WI[n, 2 * D : 3 * D, cols] = hi
                b_hi, b_lo = pair(r.ebi[layer, s, pl.ds(e, 1), :])
                r.WI[n, 3 * D : 3 * D + 16, cols] = jnp.concatenate(
                    [b_hi, b_lo, jnp.zeros((14, FH), f32)], axis=0
                ).astype(bf16)
                w = second[cols, :]
                hi, lo = split(w)
                r.WO[n, cols, :] = jnp.concatenate([hi, lo], axis=1)

            over(EXPERTS, body)
            b_hi, b_lo = pair(r.ebo[layer, s])
            small_rows(r.BO, n, b_hi, b_lo, EXPERTS)
            small_cols(r.BK, n, r.ebo[layer, s])

        def prepare_gates(layer, s):
            n = 2 * layer + s
            for k in range(3):
                r.TMP[k : k + 1] = r.gwi[layer, k, s : s + 1]
            r.TMP[3:4] = r.gbi[layer, s : s + 1]
            hi, lo = pair(r.TMP[0:4])
            small_rows(r.GW, n, hi, lo, 4)
            hi, lo = pair(r.gwo[layer, s])
            small_rows(r.GWR, n, hi, lo, EXPERTS)
            small_cols(r.GWK, n, r.gwo[layer, s])

        def prepare_coords():
            hi, lo = pair(r.co[...])
            tmp = r.G
            tmp[...] = jnp.zeros(tmp.shape, f32)
            one = jnp.ones((1, points), f32)
            tmp[0, 0:3], tmp[0, 3:4] = hi, one
            tmp[1, 0:3], tmp[1, 3:4] = hi, one
            tmp[2, 0:3] = lo
            r.CA[...] = jnp.concatenate([tmp[n] for n in range(4)], axis=0).astype(bf16)

        def gates(n):
            def body(s):
                hidden, _ = gelu_both(tn(r.GW[n], r.CA[:, s]))
                logits = nn(r.GWK[n], k3(*split(hidden)))[0:8]
                real = lax.broadcasted_iota(jnp.int32, logits.shape, 0) < EXPERTS
                logits = jnp.where(real, logits, -1e30)
                power = jnp.exp(logits - jnp.max(logits, axis=0, keepdims=True))
                power = jnp.where(real, power, 0.0)
                share = power / jnp.sum(power, axis=0, keepdims=True)
                r.G[n, :, s] = share
                hi, lo = pair(share)
                r.GB[n, :, s] = jnp.concatenate([hi, hi, lo, jnp.zeros_like(hi)], axis=0).astype(bf16)

            over_tiles(body)

        def gates_back(n):
            r.GGA[n] = jnp.zeros((8, D), f32)
            r.GGB[n] = jnp.zeros((8, D), f32)

            def body(s):
                hidden, slope = gelu_both(tn(r.GW[n], r.CA[:, s]))
                hi, lo = pair(r.DL[n, :, s])
                stacked = jnp.concatenate([hi, hi, lo, jnp.zeros_like(hi)], axis=0).astype(bf16)
                h_hi, h_lo = split(hidden)
                first = nt(stacked, h_hi)
                r.GGA[n] += first[0:8] + first[16:24] + nt(stacked, h_lo)[0:8]
                d_hi, d_lo = split(tn(r.GWR[n], stacked) * slope)
                coords = r.CA[:, s]
                first = nt(coords, d_hi)
                r.GGB[n] += first[0:8] + first[16:24] + nt(coords, d_lo)[0:8]

            over_tiles(body)

        def func_parts(layer, f, s):
            unit, scale = normalise(r.ff[f, s, :].T)
            hi, lo = split(unit * col(layer, 1) + bias_col(layer, 1))
            kv = tn(r.WF[layer], k3(hi, lo))
            position = (
                lax.axis_index("fn") * f_rows
                + s.start
                + lax.broadcasted_iota(jnp.int32, (1, s.size), 1)
            )
            mask = jnp.where(position < r.counts[f], 1.0, 0.0).astype(f32)
            return unit, scale, hi, lo, head_softmax(kv[:D]) * mask, kv[D:]

        ones = lambda width: jnp.ones((16, width), bf16)

        def summary_part(k_hi, k_lo, v_hi, v_lo):
            width = k_hi.shape[1]
            v_ones = jnp.concatenate([v_hi, ones(width)], axis=0)
            wide = nt(v_ones, jnp.concatenate([k_hi, k_lo], axis=0))
            part = wide[:, :D] + wide[:, D:]
            return jnp.concatenate([part[:D] + nt(v_lo, k_hi), part[D:]], axis=0)

        def func_forward(layer):
            def per_function(f):
                r.ACC[0:144] = jnp.zeros((144, D), f32)

                def body(j):
                    _, _, _, _, keys, values = func_parts(layer, f, rows_of(j, f_tile))
                    r.ACC[0:144] += summary_part(*split(keys), *split(values))

                over(f_tiles, body)
                packed = pack_summary(r.ACC[0:D], r.ACC[D : D + 1], square())
                r.PK[rows_of(f, 24), :] = packed

            over(NF, per_function)
            return r.PK[...]

        def use_cross(layer, block):
            spread, rows = [], []
            for f in range(NF):
                wide, total = unpack_summary(block[24 * f : 24 * f + 24], square())
                spread.append(wide)
                rows.append(total * mask8())
            full = jnp.concatenate(spread + rows + [jnp.zeros((8, D), f32)], axis=0)
            hi, lo = split(full)
            r.CR[layer] = jnp.concatenate([hi, lo, hi], axis=1)

        def use_self(layer, block):
            wide, total = unpack_summary(block, square())
            full = jnp.concatenate([wide, total * mask8(), jnp.zeros((8, D), f32)], axis=0)
            hi, lo = split(full)
            r.SE[layer] = jnp.concatenate([hi, lo, hi], axis=1)

        def use_back(block):
            wide, total = unpack_summary(block, square())
            hi, lo = split(jnp.concatenate([wide, total, jnp.zeros((15, D), f32)], axis=0))
            r.DK[...] = jnp.concatenate([hi, lo, hi], axis=0)

        def keys_values_back(k_hi, k_lo, v_hi, v_lo):
            one = ones(k_hi.shape[1])
            zero = jnp.zeros_like(one)
            d_keys = tn(r.DK[...], jnp.concatenate([v_hi, one, v_hi, one, v_lo, zero], axis=0))
            both = nn(r.DK[0:272], k_hi)
            d_values = both[0:D] + both[144:272] + nn(r.DK[0:D], k_lo)
            return d_keys, d_values

        def func_backward(layer, into_keys, into_values, share):
            clear_norm_grads(1)
            into_keys[...] = jnp.zeros((D, D), f32)
            into_values[...] = jnp.zeros((D, D), f32)

            def per_function(f):
                use_back(r.PK[rows_of(f, 24), :])

                def body(j):
                    s = rows_of(j, f_tile)
                    unit, scale, a_hi, a_lo, keys, values = func_parts(layer, f, s)
                    d_keys, d_values = keys_values_back(*split(keys), *split(values))
                    d_z = jnp.concatenate([head_softmax_back(keys, d_keys), d_values], axis=0)
                    z_hi, z_lo = split(d_z)
                    wide = nt(jnp.concatenate([a_hi, a_lo], axis=0), z_hi)
                    full = wide[:D] + wide[D:] + nt(a_hi, z_lo)
                    into_keys[...] += full[:, :D] * share
                    into_values[...] += full[:, D:] * share
                    d_normed = nn_rows(r.WF, (layer,), z_hi, z_lo)
                    add_norm_grads(1, d_normed, unit)
                    d_rows = norm_back(d_normed, col(layer, 1), unit, scale).T
                    if layer == LAYERS - 1:
                        r.f_grad[f, s, :] = d_rows
                    else:
                        r.f_grad[f, s, :] += d_rows

                over(f_tiles, body)

            for f in range(NF):
                per_function(f)
            put_norm_grads(layer, 1)

        def present_shares(width):
            total = r.present[0] + r.present[1] + r.present[2]
            total = jnp.full((1, width), total, jnp.int32).astype(f32)
            return [
                jnp.full((1, width), r.present[f], jnp.int32).astype(f32) / total for f in range(NF)
            ]

        def cross_apply(layer, q_hi, q_lo):
            applied = nn(r.CR[layer], k3(q_hi, q_lo))
            outs, inverse = [], []
            for f in range(NF):
                spread = head_spread(1.0 / applied[3 * D + 8 * f : 3 * D + 8 * f + 8])
                inverse.append(spread)
                outs.append(applied[D * f : D * (f + 1)] * spread)
            shares = present_shares(q_hi.shape[1])
            mixed = outs[0] * shares[0] + outs[1] * shares[1] + outs[2] * shares[2]
            return outs, inverse, shares, mixed

        def self_apply(layer, q_hi, q_lo):
            applied = nn(r.SE[layer], k3(q_hi, q_lo))
            spread = head_spread(1.0 / applied[D : D + 8])
            return applied[:D] * spread, spread

        def cross_forward(layer, x, s):
            unit, _ = normalise(x)
            normed = unit * col(layer, 0) + bias_col(layer, 0)
            q_hi, q_lo = split(head_softmax(tn(r.WC[layer], k3(*split(normed)))))
            r.QCH[layer, :, s] = q_hi
            r.QCL[layer, :, s] = q_lo
            _, _, _, mixed = cross_apply(layer, q_hi, q_lo)
            return x + tn(r.WAO[layer, 0], k3(*split(mixed)))

        def experts_forward(layer, which, x, s):
            n = 2 * layer + which
            j = 2 + 2 * which
            unit, _ = normalise(x)
            hi, lo = split(unit * col(layer, j) + bias_col(layer, j))
            stacked = jnp.concatenate([hi, hi, lo, ones(hi.shape[1])], axis=0)
            share = r.G[n, :, s]
            for c in range(HID // CHUNK):
                rows = slice(c * CHUNK, (c + 1) * CHUNK)
                e = c * CHUNK // FH
                value, slope = gelu_both(tn(r.WI[n, :, rows], stacked))
                h_hi, h_lo = split(value * share[e : e + 1])
                r.GHH[which, rows, s] = h_hi
                r.GHL[which, rows, s] = h_lo
                r.GD[which, rows, s] = slope * share[e : e + 1]
            both = tn(r.WO[n], r.GHH[which, :, s])
            more = tn(r.WO[n, :, 0:D], r.GHL[which, :, s])
            return x + tn(r.BO[n], r.GB[n, :, s]) + (both[:D] + both[D:] + more)

        def stream(layer, n):
            return 4 * layer + n - 1

        def first_stream(layer, s):
            return r.XS[stream(layer, 0), :, s] if layer else r.q_grad[s, :].T

        def phase_a(layer):
            r.ACC[0:144] = jnp.zeros((144, D), f32)

            xs = r.XS

            def cross(s):
                xs[stream(layer, 1), :, s] = cross_forward(layer, first_stream(layer, s), s)

            over_tiles(cross)

            def experts(s):
                x1 = xs[stream(layer, 1), :, s]
                xs[stream(layer, 2), :, s] = experts_forward(layer, 0, x1, s)

            over_tiles(experts)
            if layer == 0:
                start(kept(0, False))

            def sums(s):
                x2 = xs[stream(layer, 2), :, s]
                unit, _ = normalise(x2)
                normed = unit * col(layer, 3) + bias_col(layer, 3)
                hi, lo = split(normed)
                r.A4[2, 0:D, s], r.A4[2, D : 2 * D, s] = lo, hi
                kv = tn(r.WS[layer, :, D:], k3(hi, lo))
                k_hi, k_lo = split(head_softmax(kv[:D]))
                v_hi, v_lo = split(kv[D:])
                r.QSH[layer, D:, s] = jnp.concatenate([k_hi, v_hi], axis=0)
                r.QSL[layer, D:, s] = jnp.concatenate([k_lo, v_lo], axis=0)
                r.ACC[0:144] += summary_part(k_hi, k_lo, v_hi, v_lo)

            over_tiles(sums)
            return pack_summary(r.ACC[0:D], r.ACC[D : D + 1], square())

        def self_queries(layer):
            def body(s):
                lo, hi = r.A4[2, 0:D, s], r.A4[2, D : 2 * D, s]
                soft = head_softmax(tn(r.WS[layer, :, 0:D], k3(hi, lo)))
                r.QSH[layer, 0:D, s], r.QSL[layer, 0:D, s] = split(soft)

            over_tiles(body)

        def self_forward(layer, s):
            mixed, _ = self_apply(layer, r.QSH[layer, 0:D, s], r.QSL[layer, 0:D, s])
            x2 = r.XS[stream(layer, 2), :, s]
            return x2 + tn(r.WAO[layer, 1], k3(*split(mixed)))

        def keep_cot(m, cot, s):
            c_hi, c_lo = split(cot)
            r.CC[m, 0:D, s] = c_hi
            r.CC[m, D : 2 * D, s] = c_lo

        def experts_backward(layer, which, x, cot, s):
            n = 2 * layer + which
            j = 2 + 2 * which
            c_hi, c_lo = r.CC[2 * which + 1, 0:D, s], r.CC[2 * which + 1, D : 2 * D, s]
            stacked = jnp.concatenate([c_hi, c_hi], axis=0)
            share = r.G[n, :, s]
            scores = share * nn(r.BK[n], k3(c_hi, c_lo))[0:8]
            place = lax.broadcasted_iota(jnp.int32, scores.shape, 0)

            part = None
            for c in range(HID // CHUNK):
                rows = slice(c * CHUNK, (c + 1) * CHUNK)
                back = nn(r.WO[n, rows, :], stacked) + nn(r.WO[n, rows, 0:D], c_lo)
                hidden = join(r.GHH[which, rows, s], r.GHL[which, rows, s])
                terms = (back * hidden).reshape(CHUNK // 8, 8, back.shape[1])
                terms = jnp.sum(terms, axis=0)
                part = terms if part is None else part + terms
                if (c + 1) * CHUNK % FH == 0:
                    total = jnp.sum(part, axis=0, keepdims=True)
                    scores = scores + jnp.where(place == c * CHUNK // FH, total, 0.0)
                    part = None
                z_hi, z_lo = split(back * r.GD[which, rows, s])
                r.GHH[2, rows, s] = z_hi
                r.GHL[2, rows, s] = z_lo
            both = nn(r.WI[n, 0 : 2 * D, :], r.GHH[2, :, s])
            d_normed = both[:D] + both[D:] + nn(r.WI[n, 0:D, :], r.GHL[2, :, s])
            r.DL[n, :, s] = scores - share * jnp.sum(scores, axis=0, keepdims=True)
            unit, scale = normalise(x)
            keep_normed(layer, j, unit, s, which * 2 + 1)
            add_norm_grads(j, d_normed, unit)
            return cot + norm_back(d_normed, col(layer, j), unit, scale)

        def keep_normed(layer, j, unit, s, n):
            hi, lo = split(unit * col(layer, j) + bias_col(layer, j))
            r.A4[n, 0:D, s] = lo
            r.A4[n, D : 2 * D, s] = hi

        def self_back_first(layer, d_x3, s):
            q_hi, q_lo = r.QSH[layer, 0:D, s], r.QSL[layer, 0:D, s]
            mixed, inverse = self_apply(layer, q_hi, q_lo)
            r.OH[1, :, s], r.OL[1, :, s] = split(mixed)
            c_hi, c_lo = split(d_x3)
            r.CC[2, 0:D, s] = c_hi
            r.CC[2, D : 2 * D, s] = c_lo
            d_num = nn_rows(r.WAO, (layer, 1), c_hi, c_lo) * inverse
            d_den = -head_rows(d_num * mixed)
            n_hi, n_lo = split(jnp.concatenate([d_num, d_den, jnp.zeros_like(d_den)], axis=0))
            r.ACC[0:144] += nt_pair(n_hi, n_lo, jnp.concatenate([q_hi, q_lo], axis=0), q_hi)
            r.DZH[D : D + 144, s], r.DZL[D : D + 144, s] = n_hi, n_lo

        def self_queries_back(layer):
            def body(s):
                n_hi, n_lo = r.DZH[D : D + 144, s], r.DZL[D : D + 144, s]
                both = tn(r.SE[layer, :, 0 : 2 * D], n_hi)
                d_q = both[:D] + both[D:] + tn(r.SE[layer, :, 0:D], n_lo)
                soft = join(r.QSH[layer, 0:D, s], r.QSL[layer, 0:D, s])
                r.DZH[0:D, s], r.DZL[0:D, s] = split(head_softmax_back(soft, d_q))

            over_tiles(body)

        def phase_c(layer, tile_body):
            r.ACC[0:144] = jnp.zeros((144, D), f32)
            clear_norm_grads(4)

            def experts(s):
                r.CUR[:, s] = tile_body(s)

            over_tiles(experts)
            over_tiles(lambda s: self_back_first(layer, r.CUR[:, s], s))
            acc = r.ACC
            total = jnp.sum(acc[D : D + 8] * mask8(), axis=0, keepdims=True)
            return pack_summary(acc[0:D], total, square())

        def phase_d(layer, put, after_self, after_experts):
            r.ACC[...] = jnp.zeros(r.ACC.shape, f32)
            clear_norm_grads(3, 2, 0)
            n = 2 * layer

            def self_side(s):
                k_hi, k_lo = r.QSH[layer, D : 2 * D, s], r.QSL[layer, D : 2 * D, s]
                v_hi, v_lo = r.QSH[layer, 2 * D :, s], r.QSL[layer, 2 * D :, s]
                d_keys, d_values = keys_values_back(k_hi, k_lo, v_hi, v_lo)
                d_z = jnp.concatenate([head_softmax_back(join(k_hi, k_lo), d_keys), d_values], axis=0)
                z_hi, z_lo = split(d_z)
                r.DZH[D : 3 * D, s] = z_hi
                r.DZL[D : 3 * D, s] = z_lo
                d_normed = nn_rows(r.WS, (layer,), r.DZH[0 : 3 * D, s], r.DZL[0 : 3 * D, s])
                unit, scale = normalise(r.XS[stream(layer, 2), :, s])
                keep_normed(layer, 3, unit, s, 2)
                add_norm_grads(3, d_normed, unit)
                d_x2 = r.CUR[:, s] + norm_back(d_normed, col(layer, 3), unit, scale)
                r.CUR[:, s] = d_x2
                keep_cot(1, d_x2, s)

            over_tiles(self_side)
            spend(2.5)
            after_self()

            def experts(s):
                x1 = r.XS[stream(layer, 1), :, s]
                r.CUR[:, s] = experts_backward(layer, 0, x1, r.CUR[:, s], s)

            over_tiles(experts)
            spend(4)
            after_experts()

            def cross(s):
                d_x1 = r.CUR[:, s]
                q_hi, q_lo = r.QCH[layer, :, s], r.QCL[layer, :, s]
                outs, inverse, shares, mixed = cross_apply(layer, q_hi, q_lo)
                r.OH[0, :, s], r.OL[0, :, s] = split(mixed)
                c_hi, c_lo = split(d_x1)
                r.CC[0, 0:D, s] = c_hi
                r.CC[0, D : 2 * D, s] = c_lo
                d_o = nn_rows(r.WAO, (layer, 0), c_hi, c_lo)
                d_nums = [d_o * shares[f] * inverse[f] for f in range(NF)]
                d_dens = [-head_rows(d_nums[f] * outs[f]) for f in range(NF)]
                n_hi, n_lo = split(
                    jnp.concatenate(d_nums + d_dens + [jnp.zeros_like(d_dens[0])], axis=0)
                )
                r.ACC[...] += nt_pair(n_hi, n_lo, jnp.concatenate([q_hi, q_lo], axis=0), q_hi)
                both = tn(r.CR[layer, :, 0 : 2 * D], n_hi)
                d_q = both[:D] + both[D:] + tn(r.CR[layer, :, 0:D], n_lo)
                z_hi, z_lo = split(head_softmax_back(join(q_hi, q_lo), d_q))
                r.DZH[3 * D :, s] = z_hi
                r.DZL[3 * D :, s] = z_lo
                d_normed = nn_rows(r.WC, (layer,), z_hi, z_lo)
                unit, scale = normalise(first_stream(layer, s))
                keep_normed(layer, 0, unit, s, 0)
                add_norm_grads(0, d_normed, unit)
                put(s, d_x1 + norm_back(d_normed, col(layer, 0), unit, scale))

            over_tiles(cross)
            acc, blocks = r.ACC, []
            for f in range(NF):
                rows = acc[3 * D + 8 * f : 3 * D + 8 * f + 8] * mask8()
                total = jnp.sum(rows, axis=0, keepdims=True)
                blocks.append(pack_summary(acc[f * D : (f + 1) * D], total, square()))
            return jnp.concatenate(blocks, axis=0)

        def grad_in(layer, which):
            into = staging(("in", layer, which))
            m = 2 * which + 1

            def body(e):
                rows = rows_of(e, FH)
                wide = nt(r.A4[m], r.GHH[2, rows, :])
                more = nt(r.A4[m, D:, :], r.GHL[2, rows, :])
                into[rows_of(e, D), :] = wide[0:D] + wide[D : 2 * D] + more[0:D]
                bias = wide[2 * D : 2 * D + 1] + more[D : D + 1]
                small(layer)[pl.ds(8 + EXPERTS * which + e, 1), :] = bias

            over(EXPERTS, body)
            spend(2)

        def grad_out(layer, which):
            into = staging(("out", layer, which))
            m = 2 * which + 1

            def body(e):
                rows = rows_of(e, FH)
                h_hi, h_lo = r.GHH[which, rows, :], r.GHL[which, rows, :]
                down = pl.ds(pl.multiple_of(lax.rem(e, 2) * FH, FH), FH)
                across = pl.ds(pl.multiple_of(lax.div(e, 2) * D, D), D)
                into[down, across] = nt_pair(h_hi, h_lo, r.CC[m], r.CC[m, 0:D])

            over(EXPERTS, body)
            spend(1.6)

        def grad_gates(layer, which):
            n = 2 * layer + which
            wide = nt(r.GB[n], r.CC[2 * which + 1])
            bias = wide[0:4, :D] + wide[0:4, D:] + wide[16:20, :D]
            at = 16 + EXPERTS * which
            small(layer)[at : at + 4, 0:D] = bias
            gates_back(n)
            spend(1.6)
            small(layer)[at : at + 4, D:] = r.GGA[n, 0:4]
            at = 24 + 3 * which
            small(layer)[at : at + 3, 0:D] = r.GGB[n, 0:3]
            small(layer)[24 + which : 25 + which, D:] = r.GGB[n, 3:4]

        def grad_out_proj(c):
            m = 2 * c
            return nt_pair(r.OH[c], r.OL[c], r.CC[m], r.CC[m, 0:D])

        def grad_proj(c):
            rows = slice(0, 3 * D) if c else slice(3 * D, 4 * D)
            wide = nt(r.A4[2 * c, 0 : 2 * D, :], r.DZH[rows, :])
            return wide[:D] + wide[D:] + nt(r.A4[2 * c, D : 2 * D, :], r.DZL[rows, :])

        def grad_self(into, at):
            full = grad_proj(1)
            into[at : at + D, :] = full[:, 0 : 2 * D]
            into[at + D : at + 2 * D, 0:D] = full[:, 2 * D :]
            into[at + D : at + 2 * D, D:] = grad_out_proj(1)

        def grad_cross(into, at):
            into[at : at + D, 0:D] = grad_proj(0)
            into[at : at + D, D:] = grad_out_proj(0)

        running, clock = [], [0.0]

        def advance(entry):
            one = entry[0]
            one.step()
            if one.steps:
                entry[1] = clock[0] + one.waits[len(one.waits) - len(one.steps)]
            else:
                running.remove(entry)

        def spend(us):
            clock[0] += us
            for entry in list(running):
                if entry[1] <= clock[0]:
                    advance(entry)

        def begin(name):
            piece[name].begin()
            running.append([piece[name], clock[0] + piece[name].waits[0]])

        def drain(those=None):
            while True:
                left = [each for each in running if those is None or each[0] is those]
                if not left:
                    return
                entry = min(left, key=lambda each: each[1])
                clock[0] = max(clock[0], entry[1])
                advance(entry)

        def send(name, n, value):
            ex[name].start(n, value)

        def arrived(name, n):
            return ex[name].finish(n)

        def settled(name, n):
            return ex[name].finish_all(n)

        prepare_norms()
        prepare_func(0)
        block = func_forward(0)
        pl.semaphore_wait(barrier, greeted)
        send("P0", 0, block)
        prepare_attention(0)
        prepare_coords()
        for m in (1, 3):
            r.A4[m, 2 * D :, :] = jnp.ones((16, points), bf16)
        for n in range(4):
            prepare_gates(n // 2, n % 2)
        prepare_experts(0, 0)
        gates(0)
        wait(points_in())
        use_cross(0, arrived("P0", 0))

        block = phase_a(0)
        send("S0", 0, block)
        prepare_func(1)
        send("P1", 0, func_forward(1))
        self_queries(0)
        gates(1)
        send("S0", 1, arrived("S0", 0))
        prepare_attention(1)
        for n in range(1, 4):
            prepare_experts(n // 2, n % 2)
        gates(2)
        use_self(0, settled("S0", 1))

        def first_self(s):
            r.XS[stream(0, 3), :, s] = self_forward(0, s)

        over_tiles(first_self)

        def first_out(s):
            x3 = r.XS[stream(0, 3), :, s]
            r.XS[stream(1, 0), :, s] = experts_forward(0, 1, x3, s)

        over_tiles(first_out)
        start(kept(1, False))
        wait(kept(0, False))
        use_cross(1, arrived("P1", 0))
        block = phase_a(1)
        send("S1", 0, block)
        self_queries(1)
        gates(3)
        send("S1", 1, arrived("S1", 0))
        for name in ("points", "functions"):
            staging(name)[...] = jnp.zeros(staging(name).shape, f32)
        over_tiles(lambda s: keep_cot(3, r.q_out[s, :].T, s))
        wait(kept(1, False))
        use_self(1, settled("S1", 1))

        def last_self(s):
            r.CUR[:, s] = self_forward(1, s)

        over_tiles(last_self)

        def turn(s):
            x3 = r.CUR[:, s]
            x4 = experts_forward(1, 1, x3, s)
            r.q_out[s, :] = x4.T
            return experts_backward(1, 1, x3, join(r.CC[3, 0:D, s], r.CC[3, D : 2 * D, s]), s)

        def put_current(s, v):
            r.CUR[:, s] = v
            keep_cot(3, v, s)

        def put_result(s, v):
            r.q_grad[s, :] = v.T

        block = phase_c(1, turn)
        send("dS1", 0, block)
        grad_out(1, 1)
        begin(("out", 1, 1))
        grad_in(1, 1)
        begin(("in", 1, 1))
        start(kept(1, True))
        put_norm_grads(1, 4)
        send("dS1", 1, arrived("dS1", 0))
        spend(1)
        self_queries_back(1)
        grad_gates(1, 1)
        use_back(settled("dS1", 1))
        spend(2)

        def after_self(layer):
            name = ("out", layer, 0)
            if not layer:
                drain(piece["out", 1, 0])
            grad_out(layer, 0)
            grad_self(staging(name), HALF)
            spend(0.8)
            begin(name)

        def after_experts(layer):
            if layer:
                start(kept(0, True))
            else:
                drain(piece["in", 1, 0])
            grad_in(layer, 0)
            begin(("in", layer, 0))

        block = phase_d(1, put_current, lambda: after_self(1), lambda: after_experts(1))
        send("dC1", 0, block)
        spend(5)
        put_norm_grads(1, 3, 2, 0)
        wait(kept(1, True))
        grad_out(0, 1)
        begin(("out", 0, 1))
        grad_gates(1, 0)

        def second_experts(s):
            return experts_backward(0, 1, r.XS[stream(0, 3), :, s], r.CUR[:, s], s)

        send("dC1", 1, arrived("dC1", 0))
        block = phase_c(0, second_experts)
        send("dS0", 0, block)
        spend(6)
        put_norm_grads(0, 4)
        drain(piece["in", 1, 1])
        into = staging(("in", 0, 1))
        grad_cross(into, HALF)
        spend(0.6)
        grad_in(0, 1)
        r.PK[...] = settled("dC1", 1)
        send("dS0", 1, arrived("dS0", 0))
        keys, values = [into.at[pl.ds(HALF + D, D), pl.ds(n * D, D)] for n in range(2)]
        func_backward(1, keys, values, 1.0 / n_pts)
        begin(("in", 0, 1))
        spend(6)
        self_queries_back(0)
        use_back(settled("dS0", 1))
        wait(kept(0, True))
        block = phase_d(0, put_result, lambda: after_self(0), lambda: after_experts(0))
        send("dC0", 0, block)
        spend(5)
        put_norm_grads(0, 3, 2, 0)
        grad_cross(staging("points"), 0)
        grad_gates(0, 0)
        send("dC0", 1, arrived("dC0", 0))
        grad_gates(0, 1)
        begin("points")
        r.PK[...] = settled("dC0", 1)
        spend(3)
        keys, values = [staging("functions").at[pl.ds(n * D, D)] for n in range(2)]
        func_backward(0, keys, values, 1.0)
        begin("functions")
        spend(6)
        drain()

    return kernel, shapes


RESULTS = ["q_out", "q_grad", "f_grad"] + WEIGHTS
SMALL = ["ng", "nb", "ebi", "ebo", "gwi", "gbi", "gwo"]


def hand_out(*refs):
    sources = SimpleNamespace(**dict(zip(OUT_NAMES, refs)))
    refs = refs[len(OUT_NAMES) :]
    results = SimpleNamespace(**dict(zip(RESULTS, refs)))
    total, f_total, q_out, q_grad, f_grad, sems = refs[len(RESULTS) :]
    staged = [
        pltpu.make_async_copy(src, dst, sems.at[n])
        for n, (src, dst) in enumerate(
            [
                (sources.f_total, f_total),
                (sources.q_out, q_out),
                (sources.q_grad, q_grad),
                (sources.f_grad, f_grad),
            ]
            + [
                (sources.total.at[pl.ds(FIRST_ROW[name], count)], total.at[pl.ds(FIRST_ROW[name], count)])
                for name, (_, count) in PIECES.items()
            ]
        )
    ]
    for copy in staged:
        copy.start()

    def rows(name, start, count, lanes=slice(None)):
        lanes = pl.ds(lanes * D, D) if isinstance(lanes, int) else lanes
        return total.at[pl.ds(FIRST_ROW[name] + start, count), lanes]

    pairs = [(q_out, results.q_out), (q_grad, results.q_grad), (f_grad, results.f_grad)]
    for layer in range(LAYERS):
        for which in range(2):
            pairs.append((rows(("in", layer, which), 0, HALF), results.ewi.at[layer, which]))
            for n in range(2):
                into = results.ewo.at[layer, which, pl.ds(n * HALF, HALF)]
                pairs.append((rows(("out", layer, which), 0, HALF, n), into))
        self_rows, cross_rows = ("out", layer, 0), ("in", 0, 1)
        for n in range(3):
            pairs.append((rows(self_rows, HALF + n // 2 * D, D, n % 2), results.ap.at[layer, 1, n]))
        pairs.append((rows(self_rows, HALF + D, D, 1), results.ao.at[layer, 1]))
        if layer:
            for n, place in enumerate((0, 2, 3)):
                src = rows(cross_rows, HALF + place // 2 * D, D, place % 2)
                pairs.append((src, results.ap.at[layer, 0, n]))
            pairs.append((rows(cross_rows, HALF, D, 1), results.ao.at[layer, 0]))
        else:
            pairs.append((rows("points", 0, D, 0), results.ap.at[layer, 0, 0]))
            for n in range(2):
                pairs.append((f_total.at[pl.ds(n * D, D)], results.ap.at[layer, 0, 1 + n]))
            pairs.append((rows("points", 0, D, 1), results.ao.at[layer, 0]))
    for copy in staged:
        copy.wait()
    copies = [
        pltpu.make_async_copy(src, dst, sems.at[len(staged) + n]) for n, (src, dst) in enumerate(pairs)
    ]
    for copy in copies:
        copy.start()
    for layer in range(LAYERS):
        mine = rows("points", D + 32 * layer, 32)
        at = pl.ds(layer, 1)
        for j in range(5):
            if j == 1 and layer == 0:
                results.ng[j, at] = f_total[2 * D : 2 * D + 1]
                results.nb[j, at] = f_total[2 * D + 1 : 2 * D + 2]
            else:
                results.ng[j, at] = mine[j : j + 1, 0:D]
                results.nb[j, at] = mine[j : j + 1, D:]
        for which in range(2):
            at = EXPERTS * which
            results.ebi[layer, which] = mine[8 + at : 8 + at + EXPERTS, :]
            results.ebo[layer, which] = mine[16 + at : 16 + at + EXPERTS, 0:D]
            results.gwo[layer, which] = mine[16 + at : 16 + at + EXPERTS, D:]
            for k in range(3):
                row = 24 + 3 * which + k
                results.gwi[layer, k, which : which + 1] = mine[row : row + 1, 0:D]
            results.gbi[layer, which : which + 1] = mine[24 + which : 25 + which, D:]
    for copy in copies:
        copy.wait()


def solution(mesh):
    n_pts, n_fn = mesh.shape["pts"], mesh.shape["fn"]

    def per_device(*args):
        named = dict(zip(IN_NAMES, args))
        points, f_rows = named["x"].shape[0], named["ff"].shape[1]
        kernel, scratch = make_kernel(n_pts, n_fn, points, f_rows)
        named["ewi"] = named["ewi"].reshape(LAYERS, 2, EXPERTS * D, FH)
        named["ewo"] = named["ewo"].reshape(LAYERS, 2, HID, D)
        named["ng"], named["nb"] = [named[n].transpose(1, 0, 2) for n in ("ng", "nb")]
        named["gwi"] = named["gwi"].transpose(0, 2, 1, 3)
        vmem = pl.BlockSpec(memory_space=pltpu.VMEM)
        smem = pl.BlockSpec(memory_space=pltpu.SMEM)
        anywhere = pl.BlockSpec(memory_space=pl.ANY)
        places = {"counts": smem, "present": smem}
        for name in ["x", "cot", "ewi", "ewo", "total", "f_total"] + KEPT_NAMES:
            places[name] = anywhere
        like = lambda name: jax.ShapeDtypeStruct(named[name].shape, f32)
        out_shape = [like(n) for n in ("x", "x", "ff")]
        out_shape.append(jax.ShapeDtypeStruct((TOTAL_ROWS, 256), f32))
        out_shape.append(jax.ShapeDtypeStruct((function_rows(n_pts), D), f32))
        kept = (2, HID, points)
        out_shape += [jax.ShapeDtypeStruct(kept, kind) for kind in (bf16, bf16, f32)]
        outs = pl.pallas_call(
            kernel,
            out_shape=out_shape,
            in_specs=[places.get(n, vmem) for n in IN_NAMES],
            out_specs=[places.get(n, vmem) for n in OUT_NAMES + KEPT_NAMES],
            scratch_shapes=scratch,
            compiler_params=pltpu.CompilerParams(
                collective_id=0, has_side_effects=True, vmem_limit_bytes=int(63.5 * 2**20)
            ),
        )(*[named[n] for n in IN_NAMES])
        results = pl.pallas_call(
            hand_out,
            out_shape=out_shape[:3] + [like(n) for n in WEIGHTS],
            in_specs=[anywhere] * len(OUT_NAMES),
            out_specs=[vmem if n in SMALL else anywhere for n in RESULTS],
            scratch_shapes=[
                pltpu.VMEM(out_shape[n].shape, f32) for n in (3, 4, 0, 1, 2)
            ]
            + [pltpu.SemaphoreType.DMA((64,))],
            compiler_params=pltpu.CompilerParams(vmem_limit_bytes=60 * 2**20),
        )(*outs[: len(OUT_NAMES)])
        results = list(results)
        results[5], results[6] = results[5].transpose(1, 0, 2), results[6].transpose(1, 0, 2)
        results[11] = results[11].transpose(0, 2, 1, 3)
        results[7] = results[7].reshape(LAYERS, 2, EXPERTS, D, FH)
        results[9] = results[9].reshape(LAYERS, 2, EXPERTS, FH, D)
        return tuple(results)

    points = P(("pts", "fn"), None)
    return jax.shard_map(
        per_device,
        mesh=mesh,
        in_specs=(points, P(None, ("pts", "fn")), P(None, "fn", None)) + (P(),) * 13 + (points,),
        out_specs=(points, points, P(None, "fn", None)) + (P(),) * 11,
        check_vma=False,
    )
```

```python
import math
from types import SimpleNamespace

import jax
import jax.numpy as jnp
from jax import lax
from jax.experimental import pallas as pl
from jax.experimental.pallas import tpu as pltpu
from jax.sharding import PartitionSpec as P

D = 128
HEADS = 8
HEAD_SIZE = 16
FH = 256
EXPERTS = 4
HID = EXPERTS * FH
NF = 3
LAYERS = 2
GROUP = 8

f32, bf16 = jnp.float32, jnp.bfloat16
CHUNK = 128
MESH = pl.DeviceIdType.MESH


def split(v):
    hi = v.astype(bf16)
    return hi, (v - hi.astype(f32)).astype(bf16)


def join(hi, lo):
    return hi.astype(f32) + lo.astype(f32)


def dot(a, b, ca, cb):
    return lax.dot_general(a, b, (((ca,), (cb,)), ((), ())), preferred_element_type=f32)


def nn(a, b):
    return dot(a, b, 1, 0)


def tn(a, b):
    return dot(a, b, 0, 0)


def nt(a, b):
    return dot(a, b, 1, 1)


def k3(hi, lo):
    return jnp.concatenate([hi, hi, lo], axis=0)


def nn_rows(w_ref, at, hi, lo):
    both = nn(w_ref[at + (slice(0, 256),)], hi)
    return both[:128] + both[128:] + nn(w_ref[at + (slice(0, 128),)], lo)


def nt_pair(a_hi, a_lo, b_both, b_hi):
    wide = nt(a_hi, b_both)
    n = b_hi.shape[0]
    return wide[:, :n] + wide[:, n:] + nt(a_lo, b_hi)


def normalise(v):
    average = jnp.mean(v, axis=0, keepdims=True)
    centred = v - average
    variance = jnp.mean(centred * centred, axis=0, keepdims=True)
    scale = lax.rsqrt(variance + 1e-05)
    return centred * scale, scale


def norm_back(d_normed, gain_col, unit, scale):
    d_unit = d_normed * gain_col
    first = jnp.mean(d_unit, axis=0, keepdims=True)
    second = jnp.mean(d_unit * unit, axis=0, keepdims=True)
    return scale * (d_unit - first - unit * second)


def by_head(v):
    return v.reshape(HEADS, HEAD_SIZE, v.shape[1])


def head_softmax(v):
    shaped = by_head(v)
    top = jnp.max(shaped, axis=1, keepdims=True)
    power = jnp.exp(shaped - top)
    total = jnp.sum(power, axis=1, keepdims=True)
    return (power * (1.0 / total)).reshape(v.shape)


def head_softmax_back(soft, d_soft):
    total = jnp.sum(by_head(soft * d_soft), axis=1, keepdims=True)
    return (by_head(soft) * (by_head(d_soft) - total)).reshape(soft.shape)


def head_rows(v):
    total = jnp.sum(by_head(v), axis=1, keepdims=True)
    return jnp.concatenate([total[h] for h in range(HEADS)], axis=0)


def head_spread(rows):
    return jnp.concatenate(
        [jnp.broadcast_to(rows[h : h + 1], (HEAD_SIZE, rows.shape[1])) for h in range(HEADS)], axis=0
    )


C1 = 0.7978845608028654
C2 = C1 * 0.044715


def gelu_both(v):
    square = v * v
    gate = 0.5 + 0.5 * jnp.tanh(v * (C1 + C2 * square))
    value = v * gate
    slope = gate + value * (1.0 - gate) * (2.0 * C1 + 6.0 * C2 * square)
    return value, slope


def fold_lanes(v):
    total = v[:, :128]
    for start in range(128, v.shape[1], 128):
        total = total + v[:, start : start + 128]
    return total


def row_sum(folded):
    return jnp.sum(folded.T, axis=0, keepdims=True)


def head_masks():
    rows = lax.broadcasted_iota(jnp.int32, (D, D), 0) // HEAD_SIZE
    cols = lax.broadcasted_iota(jnp.int32, (D, D), 1) // HEAD_SIZE
    square = jnp.where(rows == cols, 1.0, 0.0).astype(f32)
    heads = lax.broadcasted_iota(jnp.int32, (HEADS, D), 0)
    cols8 = lax.broadcasted_iota(jnp.int32, (HEADS, D), 1) // HEAD_SIZE
    return square, jnp.where(heads == cols8, 1.0, 0.0).astype(f32)


def pack_summary(square_part, total_row, square):
    compact = jnp.sum((square_part * square).reshape(HEADS, HEAD_SIZE, D), axis=0)
    return jnp.concatenate([compact, total_row, jnp.zeros((7, D), f32)], axis=0)


def unpack_summary(block, square):
    spread = jnp.concatenate([block[:HEAD_SIZE]] * HEADS, axis=0) * square
    return spread, block[HEAD_SIZE : HEAD_SIZE + 1]


class Exchange:
    def __init__(self, stages, slots, sends, receives):
        self.stages, self.slots, self.sends, self.receives = stages, slots, sends, receives

    @staticmethod
    def place(stage):
        axis, stride, size = stage
        index = lax.axis_index(axis)
        digit = lax.rem(lax.div(index, stride), size)
        return axis, index - digit * stride, digit

    @staticmethod
    def member(stage, offset):
        axis, stride, size = stage
        axis, base, digit = Exchange.place(stage)
        other = lax.rem(digit + offset, size)
        return other, {axis: base + other * stride}

    def copy(self, n, offset, arriving=False):
        stage = self.stages[n]
        _, _, digit = self.place(stage)
        other, device = self.member(stage, offset)
        place = other if arriving else digit
        return pltpu.make_async_remote_copy(
            src_ref=self.slots[n].at[place],
            dst_ref=self.slots[n].at[place],
            send_sem=self.sends[n].at[offset],
            recv_sem=self.receives[n].at[place],
            device_id=device,
            device_id_type=MESH,
        )

    def start(self, n, value):
        _, _, digit = self.place(self.stages[n])
        self.slots[n][digit] = value
        for offset in range(1, self.stages[n][2]):
            self.copy(n, offset).start()

    def finish(self, n):
        size = self.stages[n][2]
        for offset in range(1, size):
            self.copy(n, offset, True).wait_recv()
        total = self.slots[n][0]
        for place in range(1, size):
            total = total + self.slots[n][place]
        for offset in range(1, size):
            self.copy(n, offset).wait_send()
        return total

    def finish_all(self, n=0):
        while True:
            total = self.finish(n)
            n += 1
            if n == len(self.stages):
                return total
            self.start(n, total)


class Reduction:
    def __init__(self, buffers, total, rows, first, n_pts, n_fn):
        self.r = SimpleNamespace(**buffers)
        self.total, self.first = total, first
        self.plane, self.n_fn = n_pts // 2, n_fn
        self.half = rows // 2
        self.part = self.half // self.plane
        self.deep = self.part % (8 * n_fn) == 0
        self.last = self.part // n_fn if self.deep else self.part
        index, self.z = lax.axis_index("pts"), lax.axis_index("fn")
        self.core, self.q = lax.rem(index, 2), lax.div(index, 2)
        self.steps = [self.add_pair, self.add_plane, self.add_fn, self.spread_plane, self.spread_pair, self.end]
        pair, plane, fn = 1.1 + rows / 1000, 2.5 + rows / 230, 3.2 + rows / 460
        self.waits = [pair, plane, fn, fn if self.deep else 0.3, plane + 0.3, pair + 0.3]

    @staticmethod
    def scratch(rows, n_pts, n_fn):
        plane = n_pts // 2
        part = max(rows // (2 * plane), 1)
        last = part // n_fn if part % (8 * n_fn) == 0 else part
        dma = pltpu.SemaphoreType.DMA
        return dict(
            stage=pltpu.VMEM((rows, 256), f32),
            pair=pltpu.VMEM((rows // 2, 256), f32),
            planes=pltpu.VMEM((plane, part, 256), f32),
            fns=pltpu.VMEM((n_fn, last, 256), f32),
            pair_sems=dma((2,)),
            plane_sends=dma((plane,)),
            plane_receives=dma((plane,)),
            fn_sends=dma((n_fn,)),
            fn_receives=dma((n_fn,)),
            out_pair_sems=dma((2,)),
            out_plane_sends=dma((plane,)),
            out_plane_receives=dma((plane,)),
            out_fn_sends=dma((n_fn,)),
            out_fn_receives=dma((n_fn,)),
            local_sem=dma((1,)),
        )

    @staticmethod
    def remote(src, dst, send, receive, device):
        return pltpu.make_async_remote_copy(
            src_ref=src, dst_ref=dst, send_sem=send, recv_sem=receive, device_id=device, device_id_type=MESH
        )

    def rows(self, start, count):
        return pl.ds(pl.multiple_of(start, 8), count)

    def own_part(self):
        return self.core * self.half + self.q * self.part

    def own_last(self):
        return self.own_part() + (self.z * self.last if self.deep else 0)

    def in_total(self, start, count):
        return self.total.at[self.rows(self.first + start, count)]

    def pair_copy(self):
        away = self.r.stage.at[self.rows((1 - self.core) * self.half, self.half)]
        sems = self.r.pair_sems
        device = {"pts": 2 * self.q + 1 - self.core}
        return self.remote(away, self.r.pair.at[pl.ds(0, self.half)], sems.at[0], sems.at[1], device)

    def plane_copy(self, offset, arriving=False):
        other = lax.rem(self.q + offset, self.plane)
        src = self.r.stage.at[self.rows(self.core * self.half + other * self.part, self.part)]
        slot = other if arriving else self.q
        return self.remote(
            src,
            self.r.planes.at[slot, pl.ds(0, self.part)],
            self.r.plane_sends.at[offset],
            self.r.plane_receives.at[slot],
            {"pts": 2 * other + self.core},
        )

    def fn_copy(self, offset, arriving=False):
        other = lax.rem(self.z + offset, self.n_fn)
        start = self.own_part() + (other * self.last if self.deep else 0)
        slot = other if arriving else self.z
        return self.remote(
            self.r.stage.at[self.rows(start, self.last)],
            self.r.fns.at[slot, pl.ds(0, self.last)],
            self.r.fn_sends.at[offset],
            self.r.fn_receives.at[slot],
            {"fn": other},
        )

    def local_copy(self):
        src = self.r.stage.at[self.rows(self.own_last(), self.last)]
        return pltpu.make_async_copy(src, self.in_total(self.own_last(), self.last), self.r.local_sem.at[0])

    def out_fn_copy(self, offset, arriving=False):
        other = lax.rem(self.z + offset, self.n_fn)
        place = other if arriving else self.z
        src = self.r.stage.at[self.rows(self.own_last(), self.last)]
        return self.remote(
            src,
            self.in_total(self.own_part() + place * self.last, self.last),
            self.r.out_fn_sends.at[offset],
            self.r.out_fn_receives.at[place],
            {"fn": other},
        )

    def out_plane_copy(self, offset, arriving=False):
        other = lax.rem(self.q + offset, self.plane)
        place = other if arriving else self.q
        region = self.in_total(self.core * self.half + place * self.part, self.part)
        return self.remote(
            region,
            region,
            self.r.out_plane_sends.at[offset],
            self.r.out_plane_receives.at[place],
            {"pts": 2 * other + self.core},
        )

    def out_pair_copy(self, arriving=False):
        place = 1 - self.core if arriving else self.core
        region = self.in_total(place * self.half, self.half)
        sems = self.r.out_pair_sems
        return self.remote(region, region, sems.at[0], sems.at[1], {"pts": 2 * self.q + 1 - self.core})

    def begin(self):
        self.pair_copy().start()

    def step(self):
        self.steps.pop(0)()

    def add_pair(self):
        self.pair_copy().wait()
        mine = self.rows(self.core * self.half, self.half)
        self.r.stage[mine, :] += self.r.pair[0 : self.half, :]
        for offset in range(1, self.plane):
            self.plane_copy(offset).start()

    def add_plane(self):
        mine = self.rows(self.own_part(), self.part)
        sums = self.r.stage[mine, :]
        for offset in range(1, self.plane):
            self.plane_copy(offset, True).wait_recv()
            sums = sums + self.r.planes[lax.rem(self.q + offset, self.plane), 0 : self.part, :]
        self.r.stage[mine, :] = sums
        for offset in range(1, self.plane):
            self.plane_copy(offset).wait_send()
        for offset in range(1, self.n_fn):
            self.fn_copy(offset).start()

    def add_fn(self):
        mine = self.rows(self.own_last(), self.last)
        self.r.fns[self.z, 0 : self.last, :] = self.r.stage[mine, :]
        for offset in range(1, self.n_fn):
            self.fn_copy(offset, True).wait_recv()
        for offset in range(1, self.n_fn):
            self.fn_copy(offset).wait_send()
        sums = self.r.fns[0, 0 : self.last, :]
        for place in range(1, self.n_fn):
            sums = sums + self.r.fns[place, 0 : self.last, :]
        self.r.stage[mine, :] = sums
        self.local_copy().start()
        if self.deep:
            for offset in range(1, self.n_fn):
                self.out_fn_copy(offset).start()

    def spread_plane(self):
        self.local_copy().wait()
        if self.deep:
            for offset in range(1, self.n_fn):
                self.out_fn_copy(offset, True).wait_recv()
            for offset in range(1, self.n_fn):
                self.out_fn_copy(offset).wait_send()
        for offset in range(1, self.plane):
            self.out_plane_copy(offset).start()

    def spread_pair(self):
        for offset in range(1, self.plane):
            self.out_plane_copy(offset, True).wait_recv()
        for offset in range(1, self.plane):
            self.out_plane_copy(offset).wait_send()
        self.out_pair_copy().start()

    def end(self):
        self.out_pair_copy().wait_send()
        self.out_pair_copy(True).wait_recv()


class SharedReduction:
    def __init__(self, buffers, total, n_pts, n_fn):
        self.r = SimpleNamespace(**buffers)
        self.total, self.n_pts, self.n_fn = total, n_pts, n_fn
        self.part = self.r.stage.shape[0] // n_pts
        self.p, self.z = lax.axis_index("pts"), lax.axis_index("fn")
        self.steps = [self.add, self.end]
        self.waits = [5.0, 5.0]

    @staticmethod
    def scratch(rows, n_pts, n_fn):
        dma = pltpu.SemaphoreType.DMA
        return dict(
            stage=pltpu.VMEM((rows, D), f32),
            slots=pltpu.VMEM((n_fn, rows // n_pts, D), f32),
            fn_sends=dma((n_fn,)),
            fn_receives=dma((n_fn,)),
            sends=dma((n_pts,)),
            receives=dma((n_pts,)),
            local_sem=dma((1,)),
        )

    def mine(self, place):
        return pl.ds(pl.multiple_of(place * self.part, 8), self.part)

    def fn_copy(self, offset, arriving=False):
        other = lax.rem(self.z + offset, self.n_fn)
        slot = other if arriving else self.z
        src, dst = self.r.stage.at[self.mine(self.p)], self.r.slots.at[slot]
        return Reduction.remote(
            src, dst, self.r.fn_sends.at[offset], self.r.fn_receives.at[slot], {"fn": other}
        )

    def out_copy(self, offset, arriving=False):
        other = lax.rem(self.p + offset, self.n_pts)
        place = other if arriving else self.p
        src, dst = self.r.stage.at[self.mine(self.p)], self.total.at[self.mine(place)]
        return Reduction.remote(
            src, dst, self.r.sends.at[offset], self.r.receives.at[place], {"pts": other}
        )

    def local_copy(self):
        src, dst = self.r.stage.at[self.mine(self.p)], self.total.at[self.mine(self.p)]
        return pltpu.make_async_copy(src, dst, self.r.local_sem.at[0])

    def begin(self):
        for offset in range(1, self.n_fn):
            self.fn_copy(offset).start()
        self.r.slots[self.z] = self.r.stage[self.mine(self.p), :]

    def step(self):
        self.steps.pop(0)()

    def add(self):
        for offset in range(1, self.n_fn):
            self.fn_copy(offset, True).wait_recv()
        for offset in range(1, self.n_fn):
            self.fn_copy(offset).wait_send()
        sums = self.r.slots[0]
        for place in range(1, self.n_fn):
            sums = sums + self.r.slots[place]
        self.r.stage[self.mine(self.p), :] = sums
        self.local_copy().start()
        for offset in range(1, self.n_pts):
            self.out_copy(offset).start()

    def end(self):
        self.local_copy().wait()
        for offset in range(1, self.n_pts):
            self.out_copy(offset, True).wait_recv()
        for offset in range(1, self.n_pts):
            self.out_copy(offset).wait_send()


HALF = EXPERTS * D
PIECES = {
    ("out", 1, 1): ("out0", 512),
    ("in", 1, 1): ("in0", 512),
    ("out", 1, 0): ("out1", 768),
    ("in", 1, 0): ("in1", 512),
    ("out", 0, 1): ("out2", 512),
    ("in", 0, 1): ("in0", 768),
    ("out", 0, 0): ("out1", 768),
    ("in", 0, 0): ("in1", 512),
    "points": ("points", 256),
}
FIRST_ROW = {name: sum(rows for _, rows in list(PIECES.values())[:n]) for n, name in enumerate(PIECES)}
TOTAL_ROWS = sum(rows for _, rows in PIECES.values())


def function_rows(n_pts):
    return -(-(2 * D + 8) // (8 * n_pts)) * 8 * n_pts


WEIGHTS = ["ap", "ao", "ng", "nb", "ewi", "ebi", "ewo", "ebo", "gwi", "gbi", "gwo"]
IN_NAMES = ["x", "co", "ff", "counts", "present"] + WEIGHTS + ["cot"]
OUT_NAMES = ["q_out", "q_grad", "f_grad", "total", "f_total"]
KEPT_NAMES = ["kept_hi", "kept_lo", "kept_slope"]


def make_kernel(n_pts, n_fn, points, f_rows):
    tile = next(width for width in (512, 256, 128) if points % width == 0)
    f_tile = next(width for width in (512, 256, 128) if f_rows % width == 0)
    f_tiles = f_rows // f_tile
    inner = min(n_pts, GROUP)
    pts_stages = [("pts", 1, inner)]
    if n_pts > inner:
        pts_stages.append(("pts", inner, n_pts // inner))
    fn_stages = [("fn", 1, n_fn)]
    every = pts_stages + fn_stages
    syncs = {
        "P0": (fn_stages, 72),
        "P1": (fn_stages, 72),
        "S0": (every, 24),
        "S1": (every, 24),
        "dS1": (every, 24),
        "dC1": (every, 72),
        "dS0": (every, 24),
        "dC0": (every, 72),
    }
    scratch = dict(
        XS=pltpu.VMEM((6, D, points), f32),
        CUR=pltpu.VMEM((D, points), f32),
        COL=pltpu.VMEM((D, D), f32),
        TMP=pltpu.VMEM((32, D), f32),
        TMPK=pltpu.VMEM((16, 3 * D), f32),
        WC=pltpu.VMEM((LAYERS, 3 * D, D), bf16),
        WS=pltpu.VMEM((LAYERS, 3 * D, 3 * D), bf16),
        WF=pltpu.VMEM((LAYERS, 3 * D, 2 * D), bf16),
        WAO=pltpu.VMEM((LAYERS, 2, 3 * D, D), bf16),
        WI=pltpu.VMEM((4, 3 * D + 16, HID), bf16),
        WO=pltpu.VMEM((4, HID, 2 * D), bf16),
        BO=pltpu.VMEM((4, 32, D), bf16),
        BK=pltpu.VMEM((4, 16, 3 * D), bf16),
        GW=pltpu.VMEM((4, 32, D), bf16),
        GWK=pltpu.VMEM((4, 16, 3 * D), bf16),
        GWR=pltpu.VMEM((4, 32, D), bf16),
        CA=pltpu.VMEM((32, points), bf16),
        G=pltpu.VMEM((4, 8, points), f32),
        GB=pltpu.VMEM((4, 32, points), bf16),
        DL=pltpu.VMEM((4, 8, points), f32),
        GHH=pltpu.VMEM((3, HID, points), bf16),
        GHL=pltpu.VMEM((3, HID, points), bf16),
        GD=pltpu.VMEM((2, HID, points), f32),
        QCH=pltpu.VMEM((LAYERS, D, points), bf16),
        QCL=pltpu.VMEM((LAYERS, D, points), bf16),
        QSH=pltpu.VMEM((LAYERS, 3 * D, points), bf16),
        QSL=pltpu.VMEM((LAYERS, 3 * D, points), bf16),
        CR=pltpu.VMEM((LAYERS, 416, 3 * D), bf16),
        SE=pltpu.VMEM((LAYERS, 144, 3 * D), bf16),
        DK=pltpu.VMEM((432, D), bf16),
        PK=pltpu.VMEM((72, D), f32),
        ACC=pltpu.VMEM((416, D), f32),
        A4=pltpu.VMEM((4, 2 * D + 16, points), bf16),
        CC=pltpu.VMEM((4, 2 * D, points), bf16),
        OH=pltpu.VMEM((2, D, points), bf16),
        OL=pltpu.VMEM((2, D, points), bf16),
        DZH=pltpu.VMEM((4 * D, points), bf16),
        DZL=pltpu.VMEM((4 * D, points), bf16),
        LG=pltpu.VMEM((8, D, D), f32),
        GGA=pltpu.VMEM((4, 8, D), f32),
        GGB=pltpu.VMEM((4, 8, D), f32),
        dma_in=pltpu.SemaphoreType.DMA((10,)),
        dma_keep=pltpu.SemaphoreType.DMA((2, 2, 3)),
    )
    dma = pltpu.SemaphoreType.DMA
    for name, (stages, rows) in syncs.items():
        scratch[name] = [
            [pltpu.VMEM((stage[2], rows, D), f32), dma((stage[2],)), dma((stage[2],))] for stage in stages
        ]
    for buffers in dict.fromkeys(buffers for buffers, _ in PIECES.values()):
        rows = max(count for name, count in PIECES.values() if name == buffers)
        scratch[buffers] = Reduction.scratch(rows, n_pts, n_fn)
    scratch["functions"] = SharedReduction.scratch(function_rows(n_pts), n_pts, n_fn)
    shapes, tree = jax.tree.flatten(scratch)
    names = IN_NAMES + OUT_NAMES + KEPT_NAMES

    def kernel(*refs):
        r = SimpleNamespace(
            **dict(zip(names, refs)), **jax.tree.unflatten(tree, refs[len(names) :])
        )
        ex = {name: Exchange(stages, *zip(*vars(r)[name])) for name, (stages, _) in syncs.items()}
        piece = {
            name: Reduction(vars(r)[buffers], r.total, rows, FIRST_ROW[name], n_pts, n_fn)
            for name, (buffers, rows) in PIECES.items()
        }

        piece["functions"] = SharedReduction(r.functions, r.f_total, n_pts, n_fn)

        def staging(name):
            return piece[name].r.stage

        def small(layer):
            return staging("points").at[pl.ds(D + 32 * layer, 32)]

        barrier = pltpu.get_barrier_semaphore()
        greeted = 0
        for stage in every:
            for offset in range(1, stage[2]):
                _, device = Exchange.member(stage, offset)
                pl.semaphore_signal(barrier, inc=1, device_id=device, device_id_type=MESH)
                greeted += 1

        def weight_in(layer):
            into = r.GD.at[layer]
            every_copy = []
            for s in range(2):
                n = 4 * layer + 2 * s
                every_copy.append(
                    pltpu.make_async_copy(
                        r.ewi.at[layer, s],
                        into.at[pl.ds(s * EXPERTS * D, EXPERTS * D), pl.ds(0, FH)],
                        r.dma_in.at[n],
                    )
                )
                every_copy.append(
                    pltpu.make_async_copy(
                        r.ewo.at[layer, s],
                        into.at[:, pl.ds(FH + D * s, D)],
                        r.dma_in.at[n + 1],
                    )
                )
            return every_copy

        def points_in():
            return (
                pltpu.make_async_copy(r.x, r.q_grad, r.dma_in.at[8]),
                pltpu.make_async_copy(r.cot, r.q_out, r.dma_in.at[9]),
            )

        def kept(n, back):
            pairs = ((r.GHH, r.kept_hi), (r.GHL, r.kept_lo), (r.GD, r.kept_slope))
            copies = []
            for k, (near, far) in enumerate(pairs):
                ends = (near.at[n], far.at[n])
                src, dst = reversed(ends) if back else ends
                copies.append(pltpu.make_async_copy(src, dst, r.dma_keep.at[n, int(back), k]))
            return copies

        def start(copies):
            for copy in copies:
                copy.start()

        def wait(copies):
            for copy in copies:
                copy.wait()

        for copy in weight_in(0) + list(points_in()) + weight_in(1):
            copy.start()

        square, mask8 = head_masks()
        square = lambda: head_masks()[0]
        mask8 = lambda: head_masks()[1]

        def over_tiles(body, width=tile):
            def step(j, carry):
                body(pl.ds(pl.multiple_of(j * width, width), width))
                return carry

            lax.fori_loop(0, points // width, step, 0)

        def over(count, body):
            def step(j, carry):
                body(j)
                return carry

            lax.fori_loop(0, count, step, 0)

        def rows_of(e, width):
            return pl.ds(pl.multiple_of(e * width, width), width)

        def col(layer, j):
            return r.COL[:, layer * 5 + j : layer * 5 + j + 1]

        def bias_col(layer, j):
            return r.COL[:, 16 + layer * 5 + j : 17 + layer * 5 + j]

        norm_slot = {4: 0, 3: 0, 2: 1, 0: 2, 1: 3}

        def add_norm_grads(j, d_normed, unit):
            n = 2 * norm_slot[j]
            r.LG[n] += fold_lanes(d_normed * unit)
            r.LG[n + 1] += fold_lanes(d_normed)

        def clear_norm_grads(*which):
            for j in which:
                n = 2 * norm_slot[j]
                r.LG[n : n + 2] = jnp.zeros((2, D, D), f32)

        def put_norm_grads(layer, *which):
            for j in which:
                n = 2 * norm_slot[j]
                gain, bias = row_sum(r.LG[n]), row_sum(r.LG[n + 1])
                if j == 1 and layer == 0:
                    staging("functions")[2 * D : 2 * D + 1, :] = gain
                    staging("functions")[2 * D + 1 : 2 * D + 2, :] = bias
                    continue
                share = 1.0 / n_pts if j == 1 else 1.0
                small(layer)[j : j + 1, 0:D] = gain * share
                small(layer)[j : j + 1, D:] = bias * share

        def row_stack(ref, at, w):
            hi, lo = split(w)
            ref[at + (slice(0, D),)] = hi
            ref[at + (slice(D, 2 * D),)] = lo
            ref[at + (slice(2 * D, 3 * D),)] = hi

        def prepare_norms():
            r.COL[...] = jnp.zeros((D, D), f32)
            for layer in range(LAYERS):
                for j in range(5):
                    n = layer * 5 + j
                    r.COL[n : n + 1, :] = r.ng[j, layer : layer + 1]
                    r.COL[16 + n : 17 + n, :] = r.nb[j, layer : layer + 1]
            r.COL[...] = r.COL[...].T

        def prepare_func(layer):
            both = jnp.concatenate([r.ap[layer, 0, 1], r.ap[layer, 0, 2]], axis=1)
            row_stack(r.WF, (layer,), both)

        def prepare_attention(layer):
            row_stack(r.WC, (layer,), r.ap[layer, 0, 0])
            three = jnp.concatenate([r.ap[layer, 1, n] for n in range(3)], axis=1)
            row_stack(r.WS, (layer,), three)
            for c in range(2):
                row_stack(r.WAO, (layer, c), r.ao[layer, c])

        def small_rows(ref, n, hi, lo, count):
            tmp = r.TMP
            tmp[...] = jnp.zeros(tmp.shape, f32)
            tmp[0:count] = hi
            tmp[8 : 8 + count] = lo
            tmp[16 : 16 + count] = hi
            ref[n] = tmp[...].astype(bf16)

        def small_cols(ref, n, w):
            hi, lo = split(w)
            tmp = r.TMPK
            tmp[...] = jnp.zeros(tmp.shape, f32)
            tmp[0:4] = jnp.concatenate([hi.astype(f32), lo.astype(f32), hi.astype(f32)], axis=1)
            ref[n] = tmp[...].astype(bf16)

        def pair(v):
            hi, lo = split(v)
            return hi.astype(f32), lo.astype(f32)

        def prepare_experts(layer, s):
            n = 2 * layer + s
            staged = r.GD

            def body(e):
                w = staged[layer, rows_of(s * EXPERTS + e, D), 0:FH]
                hi, lo = split(w)
                cols = rows_of(e, FH)
                r.WI[n, 0:D, cols] = hi
                r.WI[n, D : 2 * D, cols] = lo
                r.WI[n, 2 * D : 3 * D, cols] = hi
                b_hi, b_lo = pair(r.ebi[layer, s, pl.ds(e, 1), :])
                r.WI[n, 3 * D : 3 * D + 16, cols] = jnp.concatenate(
                    [b_hi, b_lo, jnp.zeros((14, FH), f32)], axis=0
                ).astype(bf16)
                w = staged[layer, cols, FH + D * s : FH + D * (s + 1)]
                hi, lo = split(w)
                r.WO[n, cols, :] = jnp.concatenate([hi, lo], axis=1)

            over(EXPERTS, body)
            b_hi, b_lo = pair(r.ebo[layer, s])
            small_rows(r.BO, n, b_hi, b_lo, EXPERTS)
            small_cols(r.BK, n, r.ebo[layer, s])

        def prepare_gates(layer, s):
            n = 2 * layer + s
            for k in range(3):
                r.TMP[k : k + 1] = r.gwi[layer, k, s : s + 1]
            r.TMP[3:4] = r.gbi[layer, s : s + 1]
            hi, lo = pair(r.TMP[0:4])
            small_rows(r.GW, n, hi, lo, 4)
            hi, lo = pair(r.gwo[layer, s])
            small_rows(r.GWR, n, hi, lo, EXPERTS)
            small_cols(r.GWK, n, r.gwo[layer, s])

        def prepare_coords():
            hi, lo = pair(r.co[...])
            tmp = r.G
            tmp[...] = jnp.zeros(tmp.shape, f32)
            one = jnp.ones((1, points), f32)
            tmp[0, 0:3], tmp[0, 3:4] = hi, one
            tmp[1, 0:3], tmp[1, 3:4] = hi, one
            tmp[2, 0:3] = lo
            r.CA[...] = jnp.concatenate([tmp[n] for n in range(4)], axis=0).astype(bf16)

        def gates(n):
            def body(s):
                hidden, _ = gelu_both(tn(r.GW[n], r.CA[:, s]))
                logits = nn(r.GWK[n], k3(*split(hidden)))[0:8]
                real = lax.broadcasted_iota(jnp.int32, logits.shape, 0) < EXPERTS
                logits = jnp.where(real, logits, -1e30)
                power = jnp.exp(logits - jnp.max(logits, axis=0, keepdims=True))
                power = jnp.where(real, power, 0.0)
                share = power / jnp.sum(power, axis=0, keepdims=True)
                r.G[n, :, s] = share
                hi, lo = pair(share)
                r.GB[n, :, s] = jnp.concatenate([hi, hi, lo, jnp.zeros_like(hi)], axis=0).astype(bf16)

            over_tiles(body)

        def gates_back(n):
            r.GGA[n] = jnp.zeros((8, D), f32)
            r.GGB[n] = jnp.zeros((8, D), f32)

            def body(s):
                hidden, slope = gelu_both(tn(r.GW[n], r.CA[:, s]))
                hi, lo = pair(r.DL[n, :, s])
                stacked = jnp.concatenate([hi, hi, lo, jnp.zeros_like(hi)], axis=0).astype(bf16)
                h_hi, h_lo = split(hidden)
                first = nt(stacked, h_hi)
                r.GGA[n] += first[0:8] + first[16:24] + nt(stacked, h_lo)[0:8]
                d_hi, d_lo = split(tn(r.GWR[n], stacked) * slope)
                coords = r.CA[:, s]
                first = nt(coords, d_hi)
                r.GGB[n] += first[0:8] + first[16:24] + nt(coords, d_lo)[0:8]

            over_tiles(body)

        def func_parts(layer, f, s):
            unit, scale = normalise(r.ff[f, s, :].T)
            hi, lo = split(unit * col(layer, 1) + bias_col(layer, 1))
            kv = tn(r.WF[layer], k3(hi, lo))
            position = (
                lax.axis_index("fn") * f_rows
                + s.start
                + lax.broadcasted_iota(jnp.int32, (1, s.size), 1)
            )
            mask = jnp.where(position < r.counts[f], 1.0, 0.0).astype(f32)
            return unit, scale, hi, lo, head_softmax(kv[:D]) * mask, kv[D:]

        ones = lambda width: jnp.ones((16, width), bf16)

        def summary_part(k_hi, k_lo, v_hi, v_lo):
            width = k_hi.shape[1]
            v_ones = jnp.concatenate([v_hi, ones(width)], axis=0)
            wide = nt(v_ones, jnp.concatenate([k_hi, k_lo], axis=0))
            part = wide[:, :D] + wide[:, D:]
            return jnp.concatenate([part[:D] + nt(v_lo, k_hi), part[D:]], axis=0)

        def func_forward(layer):
            def per_function(f):
                r.ACC[0:144] = jnp.zeros((144, D), f32)

                def body(j):
                    _, _, _, _, keys, values = func_parts(layer, f, rows_of(j, f_tile))
                    r.ACC[0:144] += summary_part(*split(keys), *split(values))

                over(f_tiles, body)
                packed = pack_summary(r.ACC[0:D], r.ACC[D : D + 1], square())
                r.PK[rows_of(f, 24), :] = packed

            over(NF, per_function)
            return r.PK[...]

        def use_cross(layer, block):
            spread, rows = [], []
            for f in range(NF):
                wide, total = unpack_summary(block[24 * f : 24 * f + 24], square())
                spread.append(wide)
                rows.append(total * mask8())
            full = jnp.concatenate(spread + rows + [jnp.zeros((8, D), f32)], axis=0)
            hi, lo = split(full)
            r.CR[layer] = jnp.concatenate([hi, lo, hi], axis=1)

        def use_self(layer, block):
            wide, total = unpack_summary(block, square())
            full = jnp.concatenate([wide, total * mask8(), jnp.zeros((8, D), f32)], axis=0)
            hi, lo = split(full)
            r.SE[layer] = jnp.concatenate([hi, lo, hi], axis=1)

        def use_back(block):
            wide, total = unpack_summary(block, square())
            hi, lo = split(jnp.concatenate([wide, total, jnp.zeros((15, D), f32)], axis=0))
            r.DK[...] = jnp.concatenate([hi, lo, hi], axis=0)

        def keys_values_back(k_hi, k_lo, v_hi, v_lo):
            one = ones(k_hi.shape[1])
            zero = jnp.zeros_like(one)
            d_keys = tn(r.DK[...], jnp.concatenate([v_hi, one, v_hi, one, v_lo, zero], axis=0))
            both = nn(r.DK[0:272], k_hi)
            d_values = both[0:D] + both[144:272] + nn(r.DK[0:D], k_lo)
            return d_keys, d_values

        def func_backward(layer, into_keys, into_values, share):
            clear_norm_grads(1)
            into_keys[...] = jnp.zeros((D, D), f32)
            into_values[...] = jnp.zeros((D, D), f32)

            def per_function(f):
                use_back(r.PK[rows_of(f, 24), :])

                def body(j):
                    s = rows_of(j, f_tile)
                    unit, scale, a_hi, a_lo, keys, values = func_parts(layer, f, s)
                    d_keys, d_values = keys_values_back(*split(keys), *split(values))
                    d_z = jnp.concatenate([head_softmax_back(keys, d_keys), d_values], axis=0)
                    z_hi, z_lo = split(d_z)
                    wide = nt(jnp.concatenate([a_hi, a_lo], axis=0), z_hi)
                    full = wide[:D] + wide[D:] + nt(a_hi, z_lo)
                    into_keys[...] += full[:, :D] * share
                    into_values[...] += full[:, D:] * share
                    d_normed = nn_rows(r.WF, (layer,), z_hi, z_lo)
                    add_norm_grads(1, d_normed, unit)
                    d_rows = norm_back(d_normed, col(layer, 1), unit, scale).T
                    if layer == LAYERS - 1:
                        r.f_grad[f, s, :] = d_rows
                    else:
                        r.f_grad[f, s, :] += d_rows

                over(f_tiles, body)

            over(NF, per_function)
            put_norm_grads(layer, 1)

        def present_shares(width):
            total = r.present[0] + r.present[1] + r.present[2]
            total = jnp.full((1, width), total, jnp.int32).astype(f32)
            return [
                jnp.full((1, width), r.present[f], jnp.int32).astype(f32) / total for f in range(NF)
            ]

        def cross_apply(layer, q_hi, q_lo):
            applied = nn(r.CR[layer], k3(q_hi, q_lo))
            outs, inverse = [], []
            for f in range(NF):
                spread = head_spread(1.0 / applied[3 * D + 8 * f : 3 * D + 8 * f + 8])
                inverse.append(spread)
                outs.append(applied[D * f : D * (f + 1)] * spread)
            shares = present_shares(q_hi.shape[1])
            mixed = outs[0] * shares[0] + outs[1] * shares[1] + outs[2] * shares[2]
            return outs, inverse, shares, mixed

        def self_apply(layer, q_hi, q_lo):
            applied = nn(r.SE[layer], k3(q_hi, q_lo))
            spread = head_spread(1.0 / applied[D : D + 8])
            return applied[:D] * spread, spread

        def cross_forward(layer, x, s):
            unit, _ = normalise(x)
            normed = unit * col(layer, 0) + bias_col(layer, 0)
            q_hi, q_lo = split(head_softmax(tn(r.WC[layer], k3(*split(normed)))))
            r.QCH[layer, :, s] = q_hi
            r.QCL[layer, :, s] = q_lo
            _, _, _, mixed = cross_apply(layer, q_hi, q_lo)
            return x + tn(r.WAO[layer, 0], k3(*split(mixed)))

        def experts_forward(layer, which, x, s):
            n = 2 * layer + which
            j = 2 + 2 * which
            unit, _ = normalise(x)
            hi, lo = split(unit * col(layer, j) + bias_col(layer, j))
            stacked = jnp.concatenate([hi, hi, lo, ones(hi.shape[1])], axis=0)
            share = r.G[n, :, s]
            for c in range(HID // CHUNK):
                rows = slice(c * CHUNK, (c + 1) * CHUNK)
                e = c * CHUNK // FH
                value, slope = gelu_both(tn(r.WI[n, :, rows], stacked))
                h_hi, h_lo = split(value * share[e : e + 1])
                r.GHH[which, rows, s] = h_hi
                r.GHL[which, rows, s] = h_lo
                r.GD[which, rows, s] = slope * share[e : e + 1]
            both = tn(r.WO[n], r.GHH[which, :, s])
            more = tn(r.WO[n, :, 0:D], r.GHL[which, :, s])
            return x + tn(r.BO[n], r.GB[n, :, s]) + (both[:D] + both[D:] + more)

        def stream(layer, n):
            return 4 * layer + n - 1

        def first_stream(layer, s):
            return r.XS[stream(layer, 0), :, s] if layer else r.q_grad[s, :].T

        def phase_a(layer):
            r.ACC[0:144] = jnp.zeros((144, D), f32)

            xs = r.XS

            def cross(s):
                xs[stream(layer, 1), :, s] = cross_forward(layer, first_stream(layer, s), s)

            over_tiles(cross)

            def experts(s):
                x1 = xs[stream(layer, 1), :, s]
                xs[stream(layer, 2), :, s] = experts_forward(layer, 0, x1, s)

            over_tiles(experts)
            if layer == 0:
                start(kept(0, False))

            def sums(s):
                x2 = xs[stream(layer, 2), :, s]
                unit, _ = normalise(x2)
                normed = unit * col(layer, 3) + bias_col(layer, 3)
                qkv = tn(r.WS[layer], k3(*split(normed)))
                q_hi, q_lo = split(head_softmax(qkv[:D]))
                k_hi, k_lo = split(head_softmax(qkv[D : 2 * D]))
                v_hi, v_lo = split(qkv[2 * D :])
                r.QSH[layer, :, s] = jnp.concatenate([q_hi, k_hi, v_hi], axis=0)
                r.QSL[layer, :, s] = jnp.concatenate([q_lo, k_lo, v_lo], axis=0)
                r.ACC[0:144] += summary_part(k_hi, k_lo, v_hi, v_lo)

            over_tiles(sums)
            return pack_summary(r.ACC[0:D], r.ACC[D : D + 1], square())

        def self_forward(layer, s):
            mixed, _ = self_apply(layer, r.QSH[layer, 0:D, s], r.QSL[layer, 0:D, s])
            x2 = r.XS[stream(layer, 2), :, s]
            return x2 + tn(r.WAO[layer, 1], k3(*split(mixed)))

        def keep_cot(m, cot, s):
            c_hi, c_lo = split(cot)
            r.CC[m, 0:D, s] = c_hi
            r.CC[m, D : 2 * D, s] = c_lo

        def experts_backward(layer, which, x, cot, s):
            n = 2 * layer + which
            j = 2 + 2 * which
            c_hi, c_lo = r.CC[2 * which + 1, 0:D, s], r.CC[2 * which + 1, D : 2 * D, s]
            stacked = jnp.concatenate([c_hi, c_hi], axis=0)
            share = r.G[n, :, s]
            scores = share * nn(r.BK[n], k3(c_hi, c_lo))[0:8]
            place = lax.broadcasted_iota(jnp.int32, scores.shape, 0)

            part = None
            for c in range(HID // CHUNK):
                rows = slice(c * CHUNK, (c + 1) * CHUNK)
                back = nn(r.WO[n, rows, :], stacked) + nn(r.WO[n, rows, 0:D], c_lo)
                hidden = join(r.GHH[which, rows, s], r.GHL[which, rows, s])
                terms = (back * hidden).reshape(CHUNK // 8, 8, back.shape[1])
                terms = jnp.sum(terms, axis=0)
                part = terms if part is None else part + terms
                if (c + 1) * CHUNK % FH == 0:
                    total = jnp.sum(part, axis=0, keepdims=True)
                    scores = scores + jnp.where(place == c * CHUNK // FH, total, 0.0)
                    part = None
                z_hi, z_lo = split(back * r.GD[which, rows, s])
                r.GHH[2, rows, s] = z_hi
                r.GHL[2, rows, s] = z_lo
            both = nn(r.WI[n, 0 : 2 * D, :], r.GHH[2, :, s])
            d_normed = both[:D] + both[D:] + nn(r.WI[n, 0:D, :], r.GHL[2, :, s])
            r.DL[n, :, s] = scores - share * jnp.sum(scores, axis=0, keepdims=True)
            unit, scale = normalise(x)
            keep_normed(layer, j, unit, s, which * 2 + 1)
            add_norm_grads(j, d_normed, unit)
            return cot + norm_back(d_normed, col(layer, j), unit, scale)

        def keep_normed(layer, j, unit, s, n):
            hi, lo = split(unit * col(layer, j) + bias_col(layer, j))
            r.A4[n, 0:D, s] = lo
            r.A4[n, D : 2 * D, s] = hi

        def self_back_first(layer, d_x3, s):
            q_hi, q_lo = r.QSH[layer, 0:D, s], r.QSL[layer, 0:D, s]
            mixed, inverse = self_apply(layer, q_hi, q_lo)
            r.OH[1, :, s], r.OL[1, :, s] = split(mixed)
            c_hi, c_lo = split(d_x3)
            r.CC[2, 0:D, s] = c_hi
            r.CC[2, D : 2 * D, s] = c_lo
            d_num = nn_rows(r.WAO, (layer, 1), c_hi, c_lo) * inverse
            d_den = -head_rows(d_num * mixed)
            n_hi, n_lo = split(jnp.concatenate([d_num, d_den, jnp.zeros_like(d_den)], axis=0))
            r.ACC[0:144] += nt_pair(n_hi, n_lo, jnp.concatenate([q_hi, q_lo], axis=0), q_hi)
            both = tn(r.SE[layer, :, 0 : 2 * D], n_hi)
            d_q = both[:D] + both[D:] + tn(r.SE[layer, :, 0:D], n_lo)
            z_hi, z_lo = split(head_softmax_back(join(q_hi, q_lo), d_q))
            r.DZH[0:D, s] = z_hi
            r.DZL[0:D, s] = z_lo

        def phase_c(layer, tile_body):
            r.ACC[0:144] = jnp.zeros((144, D), f32)
            clear_norm_grads(4)

            def experts(s):
                r.CUR[:, s] = tile_body(s)

            over_tiles(experts)
            over_tiles(lambda s: self_back_first(layer, r.CUR[:, s], s))
            acc = r.ACC
            total = jnp.sum(acc[D : D + 8] * mask8(), axis=0, keepdims=True)
            return pack_summary(acc[0:D], total, square())

        def phase_d(layer, put, after_self, after_experts):
            r.ACC[...] = jnp.zeros(r.ACC.shape, f32)
            clear_norm_grads(3, 2, 0)
            n = 2 * layer

            def self_side(s):
                k_hi, k_lo = r.QSH[layer, D : 2 * D, s], r.QSL[layer, D : 2 * D, s]
                v_hi, v_lo = r.QSH[layer, 2 * D :, s], r.QSL[layer, 2 * D :, s]
                d_keys, d_values = keys_values_back(k_hi, k_lo, v_hi, v_lo)
                d_z = jnp.concatenate([head_softmax_back(join(k_hi, k_lo), d_keys), d_values], axis=0)
                z_hi, z_lo = split(d_z)
                r.DZH[D : 3 * D, s] = z_hi
                r.DZL[D : 3 * D, s] = z_lo
                d_normed = nn_rows(r.WS, (layer,), r.DZH[0 : 3 * D, s], r.DZL[0 : 3 * D, s])
                unit, scale = normalise(r.XS[stream(layer, 2), :, s])
                keep_normed(layer, 3, unit, s, 2)
                add_norm_grads(3, d_normed, unit)
                d_x2 = r.CUR[:, s] + norm_back(d_normed, col(layer, 3), unit, scale)
                r.CUR[:, s] = d_x2
                keep_cot(1, d_x2, s)

            over_tiles(self_side)
            spend(2.5)
            after_self()

            def experts(s):
                x1 = r.XS[stream(layer, 1), :, s]
                r.CUR[:, s] = experts_backward(layer, 0, x1, r.CUR[:, s], s)

            over_tiles(experts)
            spend(4)
            after_experts()

            def cross(s):
                d_x1 = r.CUR[:, s]
                q_hi, q_lo = r.QCH[layer, :, s], r.QCL[layer, :, s]
                outs, inverse, shares, mixed = cross_apply(layer, q_hi, q_lo)
                r.OH[0, :, s], r.OL[0, :, s] = split(mixed)
                c_hi, c_lo = split(d_x1)
                r.CC[0, 0:D, s] = c_hi
                r.CC[0, D : 2 * D, s] = c_lo
                d_o = nn_rows(r.WAO, (layer, 0), c_hi, c_lo)
                d_nums = [d_o * shares[f] * inverse[f] for f in range(NF)]
                d_dens = [-head_rows(d_nums[f] * outs[f]) for f in range(NF)]
                n_hi, n_lo = split(
                    jnp.concatenate(d_nums + d_dens + [jnp.zeros_like(d_dens[0])], axis=0)
                )
                r.ACC[...] += nt_pair(n_hi, n_lo, jnp.concatenate([q_hi, q_lo], axis=0), q_hi)
                both = tn(r.CR[layer, :, 0 : 2 * D], n_hi)
                d_q = both[:D] + both[D:] + tn(r.CR[layer, :, 0:D], n_lo)
                z_hi, z_lo = split(head_softmax_back(join(q_hi, q_lo), d_q))
                r.DZH[3 * D :, s] = z_hi
                r.DZL[3 * D :, s] = z_lo
                d_normed = nn_rows(r.WC, (layer,), z_hi, z_lo)
                unit, scale = normalise(first_stream(layer, s))
                keep_normed(layer, 0, unit, s, 0)
                add_norm_grads(0, d_normed, unit)
                put(s, d_x1 + norm_back(d_normed, col(layer, 0), unit, scale))

            over_tiles(cross)
            acc, blocks = r.ACC, []
            for f in range(NF):
                rows = acc[3 * D + 8 * f : 3 * D + 8 * f + 8] * mask8()
                total = jnp.sum(rows, axis=0, keepdims=True)
                blocks.append(pack_summary(acc[f * D : (f + 1) * D], total, square()))
            return jnp.concatenate(blocks, axis=0)

        def grad_in(layer, which):
            into = staging(("in", layer, which))
            m = 2 * which + 1

            def body(e):
                rows = rows_of(e, FH)
                wide = nt(r.A4[m], r.GHH[2, rows, :])
                more = nt(r.A4[m, D:, :], r.GHL[2, rows, :])
                into[rows_of(e, D), :] = wide[0:D] + wide[D : 2 * D] + more[0:D]
                bias = wide[2 * D : 2 * D + 1] + more[D : D + 1]
                small(layer)[pl.ds(8 + EXPERTS * which + e, 1), :] = bias

            over(EXPERTS, body)
            spend(2)

        def grad_out(layer, which):
            into = staging(("out", layer, which))
            m = 2 * which + 1

            def body(e):
                rows = rows_of(e, FH)
                h_hi, h_lo = r.GHH[which, rows, :], r.GHL[which, rows, :]
                down = pl.ds(pl.multiple_of(lax.rem(e, 2) * FH, FH), FH)
                across = pl.ds(pl.multiple_of(lax.div(e, 2) * D, D), D)
                into[down, across] = nt_pair(h_hi, h_lo, r.CC[m], r.CC[m, 0:D])

            over(EXPERTS, body)
            spend(1.6)

        def grad_gates(layer, which):
            n = 2 * layer + which
            wide = nt(r.GB[n], r.CC[2 * which + 1])
            bias = wide[0:4, :D] + wide[0:4, D:] + wide[16:20, :D]
            at = 16 + EXPERTS * which
            small(layer)[at : at + 4, 0:D] = bias
            gates_back(n)
            spend(1.6)
            small(layer)[at : at + 4, D:] = r.GGA[n, 0:4]
            at = 24 + 3 * which
            small(layer)[at : at + 3, 0:D] = r.GGB[n, 0:3]
            small(layer)[24 + which : 25 + which, D:] = r.GGB[n, 3:4]

        def grad_out_proj(c):
            m = 2 * c
            return nt_pair(r.OH[c], r.OL[c], r.CC[m], r.CC[m, 0:D])

        def grad_proj(c):
            rows = slice(0, 3 * D) if c else slice(3 * D, 4 * D)
            wide = nt(r.A4[2 * c, 0 : 2 * D, :], r.DZH[rows, :])
            return wide[:D] + wide[D:] + nt(r.A4[2 * c, D : 2 * D, :], r.DZL[rows, :])

        def grad_self(into, at):
            full = grad_proj(1)
            into[at : at + D, :] = full[:, 0 : 2 * D]
            into[at + D : at + 2 * D, 0:D] = full[:, 2 * D :]
            into[at + D : at + 2 * D, D:] = grad_out_proj(1)

        def grad_cross(into, at):
            into[at : at + D, 0:D] = grad_proj(0)
            into[at : at + D, D:] = grad_out_proj(0)

        running, clock = [], [0.0]

        def spend(us):
            clock[0] += us
            tick()

        def begin(name):
            piece[name].begin()
            running.append([piece[name], clock[0] + piece[name].waits[0]])

        def advance(entry):
            one = entry[0]
            one.step()
            if one.steps:
                entry[1] = clock[0] + one.waits[len(one.waits) - len(one.steps)]
            else:
                running.remove(entry)

        def tick():
            for entry in list(running):
                if entry[1] <= clock[0]:
                    advance(entry)

        def drain(name=None):
            while True:
                left = [entry for entry in running if name is None or entry[0] is piece[name]]
                if not left:
                    return
                entry = min(left, key=lambda each: each[1])
                clock[0] = max(clock[0], entry[1])
                advance(entry)

        prepare_norms()
        prepare_func(0)
        block = func_forward(0)
        pl.semaphore_wait(barrier, greeted)
        ex["P0"].start(0, block)
        prepare_func(1)
        for layer in range(LAYERS):
            prepare_attention(layer)
        prepare_coords()
        for m in (1, 3):
            r.A4[m, 2 * D :, :] = jnp.ones((16, points), bf16)
        for layer in range(LAYERS):
            for s in range(2):
                prepare_gates(layer, s)
        for copy in weight_in(0) + list(points_in()):
            copy.wait()
        for s in range(2):
            prepare_experts(0, s)
        gates(0)
        gates(1)
        ex["P1"].start(0, func_forward(1))
        use_cross(0, ex["P0"].finish(0))

        block = phase_a(0)
        ex["S0"].start(0, block)
        for copy in weight_in(1):
            copy.wait()
        for s in range(2):
            prepare_experts(1, s)
        gates(2)
        gates(3)
        use_cross(1, ex["P1"].finish(0))
        use_self(0, ex["S0"].finish_all())

        def first_self(s):
            r.XS[stream(0, 3), :, s] = self_forward(0, s)

        over_tiles(first_self)

        def first_out(s):
            x3 = r.XS[stream(0, 3), :, s]
            r.XS[stream(1, 0), :, s] = experts_forward(0, 1, x3, s)

        over_tiles(first_out)
        start(kept(1, False))
        wait(kept(0, False))
        block = phase_a(1)
        ex["S1"].start(0, block)
        use_self(1, ex["S1"].finish_all())

        wait(kept(1, False))

        def last_self(s):
            r.CUR[:, s] = self_forward(1, s)

        over_tiles(last_self)

        def turn(s):
            x3 = r.CUR[:, s]
            x4 = experts_forward(1, 1, x3, s)
            cot = r.q_out[s, :].T
            r.q_out[s, :] = x4.T
            keep_cot(3, cot, s)
            return experts_backward(1, 1, x3, cot, s)

        def put_current(s, v):
            r.CUR[:, s] = v
            keep_cot(3, v, s)

        def put_result(s, v):
            r.q_grad[s, :] = v.T

        for name in ("points", "functions"):
            staging(name)[...] = jnp.zeros(staging(name).shape, f32)
        block = phase_c(1, turn)
        ex["dS1"].start(0, block)
        put_norm_grads(1, 4)
        grad_out(1, 1)
        begin(("out", 1, 1))
        grad_in(1, 1)
        begin(("in", 1, 1))
        start(kept(1, True))
        ex["dS1"].start(1, ex["dS1"].finish(0))
        spend(1)
        grad_gates(1, 1)
        use_back(ex["dS1"].finish_all(1))
        spend(2)

        def after_self(layer):
            name = ("out", layer, 0)
            if not layer:
                drain(("out", 1, 0))
            grad_out(layer, 0)
            grad_self(staging(name), HALF)
            spend(0.8)
            begin(name)

        def after_experts(layer):
            if layer:
                start(kept(0, True))
            else:
                drain(("in", 1, 0))
            grad_in(layer, 0)
            begin(("in", layer, 0))

        block = phase_d(1, put_current, lambda: after_self(1), lambda: after_experts(1))
        ex["dC1"].start(0, block)
        spend(5)
        put_norm_grads(1, 3, 2, 0)
        wait(kept(1, True))
        grad_out(0, 1)
        begin(("out", 0, 1))
        grad_gates(1, 0)

        def second_experts(s):
            return experts_backward(0, 1, r.XS[stream(0, 3), :, s], r.CUR[:, s], s)

        ex["dC1"].start(1, ex["dC1"].finish(0))
        block = phase_c(0, second_experts)
        ex["dS0"].start(0, block)
        spend(6)
        put_norm_grads(0, 4)
        drain(("in", 1, 1))
        into = staging(("in", 0, 1))
        grad_cross(into, HALF)
        grad_in(0, 1)
        r.PK[...] = ex["dC1"].finish_all(1)
        ex["dS0"].start(1, ex["dS0"].finish(0))
        spend(1)
        keys, values = [into.at[pl.ds(HALF + D, D), pl.ds(n * D, D)] for n in range(2)]
        func_backward(1, keys, values, 1.0 / n_pts)
        begin(("in", 0, 1))
        spend(6)
        grad_gates(0, 1)
        use_back(ex["dS0"].finish_all(1))
        wait(kept(0, True))
        block = phase_d(0, put_result, lambda: after_self(0), lambda: after_experts(0))
        ex["dC0"].start(0, block)
        spend(5)
        put_norm_grads(0, 3, 2, 0)
        grad_cross(staging("points"), 0)
        grad_gates(0, 0)
        begin("points")
        ex["dC0"].start(1, ex["dC0"].finish(0))
        spend(2)
        r.PK[...] = ex["dC0"].finish_all(1)
        spend(3)
        keys, values = [staging("functions").at[pl.ds(n * D, D)] for n in range(2)]
        func_backward(0, keys, values, 1.0)
        begin("functions")
        spend(6)
        drain()

    return kernel, shapes


RESULTS = ["q_out", "q_grad", "f_grad"] + WEIGHTS
SMALL = ["ng", "nb", "ebi", "ebo", "gwi", "gbi", "gwo"]


def hand_out(*refs):
    sources = SimpleNamespace(**dict(zip(OUT_NAMES, refs)))
    refs = refs[len(OUT_NAMES) :]
    results = SimpleNamespace(**dict(zip(RESULTS, refs)))
    total, f_total, q_out, q_grad, f_grad, sems = refs[len(RESULTS) :]
    staged = [
        pltpu.make_async_copy(src, dst, sems.at[n])
        for n, (src, dst) in enumerate(
            [
                (sources.f_total, f_total),
                (sources.q_out, q_out),
                (sources.q_grad, q_grad),
                (sources.f_grad, f_grad),
            ]
            + [
                (sources.total.at[pl.ds(FIRST_ROW[name], count)], total.at[pl.ds(FIRST_ROW[name], count)])
                for name, (_, count) in PIECES.items()
            ]
        )
    ]
    for copy in staged:
        copy.start()

    def rows(name, start, count, lanes=slice(None)):
        lanes = pl.ds(lanes * D, D) if isinstance(lanes, int) else lanes
        return total.at[pl.ds(FIRST_ROW[name] + start, count), lanes]

    pairs = [(q_out, results.q_out), (q_grad, results.q_grad), (f_grad, results.f_grad)]
    for layer in range(LAYERS):
        for which in range(2):
            pairs.append((rows(("in", layer, which), 0, HALF), results.ewi.at[layer, which]))
            for n in range(2):
                into = results.ewo.at[layer, which, pl.ds(n * HALF, HALF)]
                pairs.append((rows(("out", layer, which), 0, HALF, n), into))
        self_rows, cross_rows = ("out", layer, 0), ("in", 0, 1)
        for n in range(3):
            pairs.append((rows(self_rows, HALF + n // 2 * D, D, n % 2), results.ap.at[layer, 1, n]))
        pairs.append((rows(self_rows, HALF + D, D, 1), results.ao.at[layer, 1]))
        if layer:
            for n, place in enumerate((0, 2, 3)):
                src = rows(cross_rows, HALF + place // 2 * D, D, place % 2)
                pairs.append((src, results.ap.at[layer, 0, n]))
            pairs.append((rows(cross_rows, HALF, D, 1), results.ao.at[layer, 0]))
        else:
            pairs.append((rows("points", 0, D, 0), results.ap.at[layer, 0, 0]))
            for n in range(2):
                pairs.append((f_total.at[pl.ds(n * D, D)], results.ap.at[layer, 0, 1 + n]))
            pairs.append((rows("points", 0, D, 1), results.ao.at[layer, 0]))
    for copy in staged:
        copy.wait()
    copies = [
        pltpu.make_async_copy(src, dst, sems.at[len(staged) + n]) for n, (src, dst) in enumerate(pairs)
    ]
    for copy in copies:
        copy.start()
    for layer in range(LAYERS):
        mine = rows("points", D + 32 * layer, 32)
        at = pl.ds(layer, 1)
        for j in range(5):
            if j == 1 and layer == 0:
                results.ng[j, at] = f_total[2 * D : 2 * D + 1]
                results.nb[j, at] = f_total[2 * D + 1 : 2 * D + 2]
            else:
                results.ng[j, at] = mine[j : j + 1, 0:D]
                results.nb[j, at] = mine[j : j + 1, D:]
        for which in range(2):
            at = EXPERTS * which
            results.ebi[layer, which] = mine[8 + at : 8 + at + EXPERTS, :]
            results.ebo[layer, which] = mine[16 + at : 16 + at + EXPERTS, 0:D]
            results.gwo[layer, which] = mine[16 + at : 16 + at + EXPERTS, D:]
            for k in range(3):
                row = 24 + 3 * which + k
                results.gwi[layer, k, which : which + 1] = mine[row : row + 1, 0:D]
            results.gbi[layer, which : which + 1] = mine[24 + which : 25 + which, D:]
    for copy in copies:
        copy.wait()


def solution(mesh):
    n_pts, n_fn = mesh.shape["pts"], mesh.shape["fn"]

    def per_device(*args):
        named = dict(zip(IN_NAMES, args))
        points, f_rows = named["x"].shape[0], named["ff"].shape[1]
        kernel, scratch = make_kernel(n_pts, n_fn, points, f_rows)
        named["ewi"] = named["ewi"].reshape(LAYERS, 2, EXPERTS * D, FH)
        named["ewo"] = named["ewo"].reshape(LAYERS, 2, HID, D)
        named["ng"], named["nb"] = [named[n].transpose(1, 0, 2) for n in ("ng", "nb")]
        named["gwi"] = named["gwi"].transpose(0, 2, 1, 3)
        vmem = pl.BlockSpec(memory_space=pltpu.VMEM)
        smem = pl.BlockSpec(memory_space=pltpu.SMEM)
        anywhere = pl.BlockSpec(memory_space=pl.ANY)
        places = {"counts": smem, "present": smem}
        for name in ["x", "cot", "ewi", "ewo", "total", "f_total"] + KEPT_NAMES:
            places[name] = anywhere
        like = lambda name: jax.ShapeDtypeStruct(named[name].shape, f32)
        out_shape = [like(n) for n in ("x", "x", "ff")]
        out_shape.append(jax.ShapeDtypeStruct((TOTAL_ROWS, 256), f32))
        out_shape.append(jax.ShapeDtypeStruct((function_rows(n_pts), D), f32))
        kept = (2, HID, points)
        out_shape += [jax.ShapeDtypeStruct(kept, kind) for kind in (bf16, bf16, f32)]
        outs = pl.pallas_call(
            kernel,
            out_shape=out_shape,
            in_specs=[places.get(n, vmem) for n in IN_NAMES],
            out_specs=[places.get(n, vmem) for n in OUT_NAMES + KEPT_NAMES],
            scratch_shapes=scratch,
            compiler_params=pltpu.CompilerParams(
                collective_id=0, has_side_effects=True, vmem_limit_bytes=int(63.5 * 2**20)
            ),
        )(*[named[n] for n in IN_NAMES])
        results = pl.pallas_call(
            hand_out,
            out_shape=out_shape[:3] + [like(n) for n in WEIGHTS],
            in_specs=[anywhere] * len(OUT_NAMES),
            out_specs=[vmem if n in SMALL else anywhere for n in RESULTS],
            scratch_shapes=[
                pltpu.VMEM(out_shape[n].shape, f32) for n in (3, 4, 0, 1, 2)
            ]
            + [pltpu.SemaphoreType.DMA((64,))],
            compiler_params=pltpu.CompilerParams(vmem_limit_bytes=60 * 2**20),
        )(*outs[: len(OUT_NAMES)])
        results = list(results)
        results[5], results[6] = results[5].transpose(1, 0, 2), results[6].transpose(1, 0, 2)
        results[11] = results[11].transpose(0, 2, 1, 3)
        results[7] = results[7].reshape(LAYERS, 2, EXPERTS, D, FH)
        results[9] = results[9].reshape(LAYERS, 2, EXPERTS, FH, D)
        return tuple(results)

    points = P(("pts", "fn"), None)
    return jax.shard_map(
        per_device,
        mesh=mesh,
        in_specs=(points, P(None, ("pts", "fn")), P(None, "fn", None)) + (P(),) * 13 + (points,),
        out_specs=(points, points, P(None, "fn", None)) + (P(),) * 11,
        check_vma=False,
    )
```
